128 devices in a mesh: dp: 16 (over z, x), tensor: 8 (over y, core).
Axes of the slice: x: 4, y: 4, z: 4, core: 2. Of those that a mesh axis runs over, the one named last changes fastest.
Arguments:
- activations: bfloat16 [4096, 3072], P('dp', 'tensor'), may hold values from -6 to 6
- act_grad: bfloat16 [4096, 12288], P('dp', 'tensor'), may hold values from -6 to 6
- up_weight: bfloat16 [3072, 12288], P('dp', 'tensor'), may hold values from -0.15625 to 0.15625
- width_steps: int32 [4096], P('dp'), may hold values from 1 to 8
Outputs:
- input_grad: bfloat16 [4096, 3072], P('dp', 'tensor')
- weight_grad: bfloat16 [3072, 12288], P('dp', 'tensor')
The draws below stay inside these ranges and needn't reach their ends.
Inputs may be any that keep to these rules, and one draw needn't show every extreme that they name: Token r uses the hidden units below 1536 * width_steps[r].
All inputs are finite; a program needn't handle non-finite values.
Results may differ from the reference program's by a relative error of at most 0.022.
Values may be sent and summed in bfloat16 or wider, within the bound.
A program may use at most 128 MiB of HBM per device.

```python
import math
import jax
import jax.numpy as jnp
from jax import lax

D = 3072
FF = 12288
TOK_DEV = 256
TOKENS = 4096
N_DP = 16


def place_ends(drawn, rng, least, largest):
    dims = drawn.shape
    place = [jax.random.randint(jax.random.fold_in(rng, axis), (), 0, dims[axis]) for axis in range(len(dims))]
    drawn = drawn.at[tuple(place)].set(least)
    longest = dims.index(max(dims))
    place[longest] = (place[longest] + 1) % dims[longest]
    return drawn.at[tuple(place)].set(largest)


def with_spikes(drawn, key, source, target, parts, factor):
    owner, partner = [(jnp.arange(drawn.shape[position]) // (drawn.shape[position] // parts)).reshape([-1 if axis == position else 1 for axis in range(drawn.ndim)]) for position in (source, target)]
    chosen = jax.random.permutation(key, parts)[partner]
    strong = (owner == chosen) | (owner == (partner + parts // 2) % parts)
    return jnp.where(strong, factor * drawn, drawn)


def shard_levels(own_key, dims, cuts, least, largest):
    factor_of, own = 1.0, jax.random.fold_in(own_key, 6)
    for axis_at, parts in cuts:
        heights = jnp.exp(jax.random.uniform(jax.random.fold_in(own, axis_at), (parts,), jnp.float32, least / len(cuts), largest / len(cuts)))
        factor_of = factor_of * jnp.repeat(heights, dims[axis_at] // parts).reshape([-1 if axis == axis_at else 1 for axis in range(len(dims))])
    return factor_of


def scatter_about(own_key, dims, width, bound, cuts=(), kind=jnp.bfloat16):
    drawn = width * jax.random.normal(own_key, dims, jnp.float32)
    if cuts:
        drawn = drawn * shard_levels(own_key, dims, cuts, -0.22, 0.18)
    return jnp.clip(drawn, -bound, bound).astype(kind)


def heavy_noise(stream_key, dims, width, reach, cuts, heavy, kind=jnp.bfloat16):
    result = width * jax.random.normal(stream_key, dims, jnp.float32)
    if cuts:
        result = result * shard_levels(stream_key, dims, cuts, -0.22, 0.18)
    return jnp.clip(with_spikes(result, jax.random.fold_in(stream_key, 3), *heavy), -reach, reach).astype(kind)


def setup_inputs(seed: int = 0) -> dict:
    streams_of = jax.random.split(jax.random.key(seed), 5)
    return {
        "activations": heavy_noise(streams_of[0], (TOKENS, D), 1.0, 6.0, ((0, 16), (1, 8)), (0, 1, 16, 2.0)),
        "act_grad": scatter_about(streams_of[1], (TOKENS, FF), 1.0, 6.0, ((0, 16), (1, 8))),
        "up_weight": heavy_noise(streams_of[2], (D, FF), D ** -0.5, 0.15625, ((0, 16), (1, 8)), (1, 0, 16, 2.0)),
        "width_steps": place_ends(jax.random.randint(streams_of[3], (TOKENS,), 1, 9), jax.random.fold_in(streams_of[3], 1), 1, 8).astype(jnp.int32),
    }


def reference(activations, act_grad, up_weight, width_steps):
    block_cols = FF // 8
    column_block = jnp.arange(FF, dtype=jnp.int32) // block_cols
    grad_scale = 1.0 / math.sqrt(TOKENS)
    x_groups = activations.reshape(N_DP, TOK_DEV, D)
    g_groups = act_grad.reshape(N_DP, TOK_DEV, FF)
    w_groups = width_steps.reshape(N_DP, TOK_DEV)

    def one_group(total, pieces):
        x_part, g_part, widths = pieces
        preact = jnp.dot(x_part, up_weight, preferred_element_type=jnp.float32)
        in_use = column_block[None, :] < widths[:, None]
        slope = jnp.where(in_use, 2.0 * jnp.maximum(preact, 0.0), 0.0)
        hidden_grad = (g_part.astype(jnp.float32) * slope).astype(jnp.bfloat16)
        input_grad = jnp.dot(hidden_grad, up_weight.T, preferred_element_type=jnp.float32).astype(jnp.bfloat16)
        partial_value = lax.dot_general(x_part, hidden_grad, (((0,), (0,)), ((), ())), preferred_element_type=jnp.float32)
        partial_value = (partial_value * grad_scale).astype(jnp.bfloat16)
        return (total + partial_value.astype(jnp.float32), input_grad)
    total, input_grad = lax.scan(one_group, jnp.zeros((D, FF), jnp.float32), (x_groups, g_groups, w_groups))
    return (input_grad.reshape(TOKENS, D), total.astype(jnp.bfloat16))
```

```python
import jax
import jax.numpy as jnp
from jax import lax
from jax.experimental import pallas as pl
from jax.experimental.pallas import tpu as pltpu
from jax.sharding import PartitionSpec as P

MESH = pl.DeviceIdType.MESH
F32 = jnp.float32
BF16 = jnp.bfloat16
TOK = 256
ROWS = 192
COLS = 384
HID = 1536
SCALE = 1.0 / 64.0
N_SEM = 160


def gray(j):
    return (0, 1, 3, 2)[j]


def kernel(
    x_ref, g_ref, w_ref, wid_ref, dx_ref, dw_ref,
    xb, wb, gb, gin, hid, sd, sr, vp, vm, ap, am, xr, dw, zvp, zvm, zap, zam, tot,
    ssem, rsem, lsem,
):
    dp, tensor = lax.axis_index("dp"), lax.axis_index("tensor")
    z, x = lax.div(dp, 4), lax.rem(dp, 4)
    y, c = lax.div(tensor, 2), lax.rem(tensor, 2)

    def ring(v, step):
        return lax.rem(v + step, 4)

    def device(dz=0, dx=0, dy=0, dc=0):
        return (
            ring(z, dz) * 4 + ring(x, dx),
            ring(y, dy) * 2 + lax.rem(c + dc, 2),
        )

    sites = {}

    def send(name, src, dst, **to):
        slot = len(sites)
        copy = pltpu.make_async_remote_copy(
            src_ref=src,
            dst_ref=dst,
            send_sem=ssem.at[slot],
            recv_sem=rsem.at[slot],
            device_id=device(**to),
            device_id_type=MESH,
        )
        copy.start()
        sites[name] = copy

    def arrived(name):
        sites[name].wait_recv()

    def token_rows(step):
        return pl.ds(pl.multiple_of(ring(x, step) * TOK, TOK), TOK)

    def token_half(step, half):
        return pl.ds(pl.multiple_of(ring(x, step) * TOK + half * 128, 128), 128)

    def weight_rows(dz, dx):
        return pl.ds(pl.multiple_of((ring(z, dz) * 4 + ring(x, dx)) * ROWS, ROWS), ROWS)

    def weight_half(dz, dx, half):
        start = (ring(z, dz) * 4 + ring(x, dx)) * ROWS + half * 96
        return pl.ds(pl.multiple_of(start, 96), 96)

    def cols_of(step):
        return pl.ds(pl.multiple_of(ring(x, step) * COLS, COLS), COLS)

    def feature(dy):
        return ring(y, dy) * 2 + c

    own_g = pltpu.make_async_copy(g_ref, gin, lsem.at[0])
    own_x = pltpu.make_async_copy(x_ref, xb.at[feature(0), token_rows(0)], lsem.at[1])
    own_w = pltpu.make_async_copy(w_ref.at[:, cols_of(0)], wb.at[weight_rows(0, 0)], lsem.at[2])
    own_g.start()
    own_x.start()
    own_w.start()

    partners = (
        dict(dx=1), dict(dx=3), dict(dx=2), dict(dy=1), dict(dy=3), dict(dz=1), dict(dz=3), dict(dc=1),
    )
    barrier = pltpu.get_barrier_semaphore()
    for to in partners:
        pl.semaphore_signal(barrier, inc=1, device_id=device(**to), device_id_type=MESH)
    with jax.named_scope("barrier"):
        pl.semaphore_wait(barrier, len(partners))

    def x_ref_or(j):
        return x_ref if j == 0 else xb.at[feature(0), token_rows(gray(j))]

    def y_send(j):
        dst = xb.at[feature(0), token_rows(gray(j))]
        send(f"yp{j}", x_ref_or(j), dst, dy=1)
        send(f"ym{j}", x_ref_or(j), dst, dy=3)
        send(f"s0{j}", x_ref_or(j), dst, dc=1)

    def y_forward(j):
        arrived(f"yp{j}")
        ref = xb.at[feature(3), token_half(gray(j), 0)]
        send(f"yfp{j}", ref, ref, dy=1)
        arrived(f"ym{j}")
        ref = xb.at[feature(1), token_half(gray(j), 1)]
        send(f"yfm{j}", ref, ref, dy=3)
        ref = xb.at[feature(3), token_rows(gray(j))]
        send(f"s1{j}", ref, ref, dc=1)
        ref = xb.at[feature(1), token_rows(gray(j))]
        send(f"s2{j}", ref, ref, dc=1)

    def y_last(j):
        arrived(f"yfp{j}")
        arrived(f"yfm{j}")
        ref = xb.at[feature(2), token_rows(gray(j))]
        send(f"s3{j}", ref, ref, dc=1)

    def tokens_ready(j):
        for part in range(4):
            arrived(f"s{part}{j}")

    def z_send(j):
        dst = wb.at[weight_rows(0, gray(j))]
        src = w_ref.at[:, cols_of(0)] if j == 0 else dst
        send(f"zp{j}", src, dst, dz=1)
        send(f"zm{j}", src, dst, dz=3)

    def z_forward(j):
        arrived(f"zp{j}")
        ref = wb.at[weight_half(3, gray(j), 0)]
        send(f"zfp{j}", ref, ref, dz=1)
        arrived(f"zm{j}")
        ref = wb.at[weight_half(1, gray(j), 1)]
        send(f"zfm{j}", ref, ref, dz=3)

    def z_last(j):
        arrived(f"zfp{j}")
        arrived(f"zfm{j}")

    def x_send(step):
        send(f"x{step}", x_ref, xb.at[feature(0), token_rows(0)], dx=step)

    def w_send(step):
        send(f"w{step}", w_ref.at[:, cols_of(step)], wb.at[weight_rows(0, 0)], dx=step)

    def g_send(step):
        send(f"g{step}", gin.at[:, cols_of(step)], gb.at[token_rows(0)], dx=step)

    x_send(1)
    x_send(3)
    y_send(0)
    z_send(0)
    w_send(1)
    w_send(3)
    w_send(2)
    x_send(2)

    own_g.wait()
    with jax.named_scope("mask"):
        for half in range(2):
            rows = pl.ds(half * 128, 128)
            width = jnp.broadcast_to(wid_ref[half : half + 1, :], (128, 128)).T
            keep = jnp.where(width > tensor, 1.0, 0.0).astype(BF16)
            for part in range(HID // 128):
                lanes = pl.ds(part * 128, 128)
                gin[rows, lanes] = gin[rows, lanes] * keep
    put_g = pltpu.make_async_copy(gin.at[:, cols_of(0)], gb.at[token_rows(0)], lsem.at[0])
    put_g.start()
    own_x.wait()
    own_w.wait()

    with jax.named_scope("z_forward0"):
        z_forward(0)
    with jax.named_scope("x_arrive13"):
        arrived("x3")
        y_send(1)
        arrived("x1")
        y_send(2)
    with jax.named_scope("y_forward0"):
        y_forward(0)
    with jax.named_scope("w_arrive13"):
        arrived("w3")
        z_send(1)
        arrived("w1")
        z_send(2)
    g_send(1)
    g_send(3)
    with jax.named_scope("z_last0"):
        z_last(0)
    with jax.named_scope("y_last0"):
        y_last(0)
    with jax.named_scope("w_arrive2"):
        arrived("w2")
        z_send(3)
    with jax.named_scope("x_arrive2"):
        arrived("x2")
        y_send(3)
    g_send(2)
    with jax.named_scope("z_forward1"):
        z_forward(1)
        z_forward(2)
    with jax.named_scope("y_forward1"):
        y_forward(1)
        y_forward(2)
    with jax.named_scope("z_last1"):
        z_last(1)
        z_last(2)
    with jax.named_scope("z_forward3"):
        z_forward(3)
    with jax.named_scope("y_last1"):
        y_last(1)
        y_last(2)
    with jax.named_scope("z_last3"):
        z_last(3)

    def hidden(j):
        tokens_ready(j)
        if j == 0:
            put_g.wait()
        else:
            arrived(f"g{(None, 3, 1, 2)[j]}")
        rows = token_rows(gray(j))
        whole = jnp.concatenate([xb[k, rows, :] for k in range(8)], axis=1)
        preact = jnp.dot(whole, wb[...], preferred_element_type=F32)
        slope = 2.0 * jnp.maximum(preact, 0.0)
        hid[rows, :] = (gb[rows, :].astype(F32) * slope).astype(BF16)

    def input_parts(j):
        h = hid[token_rows(gray(j)), :]
        for d in (2, 1, 3, 0):
            rows = pl.ds(pl.multiple_of(ring(y, d) * 768, 768), 768)
            part = lax.dot_general(
                h, wb[rows, :], (((1,), (1,)), ((), ())), preferred_element_type=F32
            ).astype(BF16)
            sd[j, d, 0] = part[:, :COLS]
            sd[j, d, 1] = part[:, COLS:]
            send(f"p{d}{j}", sd.at[j, d, 1 - c], sr.at[j, d], dc=1)

    def add_pair(j, d):
        arrived(f"p{d}{j}")
        total = sd[j, d, c].astype(F32) + sr[j, d].astype(F32)
        sd[j, d, c] = total.astype(BF16)

    top, low = pl.ds(0, 128), pl.ds(128, 128)

    def input_sends(j):
        add_pair(j, 2)
        send(f"vp{j}", sd.at[j, 2, c, top], vp.at[j], dy=1)
        send(f"vm{j}", sd.at[j, 2, c, low], vm.at[j], dy=3)
        add_pair(j, 1)
        send(f"apl{j}", sd.at[j, 1, c, low], ap.at[j, low], dy=1)
        add_pair(j, 3)
        send(f"amt{j}", sd.at[j, 3, c, top], am.at[j, top], dy=3)

    def input_via(j):
        arrived(f"vp{j}")
        sd[j, 1, c, top] = (sd[j, 1, c, top].astype(F32) + vp[j].astype(F32)).astype(BF16)
        send(f"apt{j}", sd.at[j, 1, c, top], ap.at[j, top], dy=1)
        arrived(f"vm{j}")
        sd[j, 3, c, low] = (sd[j, 3, c, low].astype(F32) + vm[j].astype(F32)).astype(BF16)
        send(f"aml{j}", sd.at[j, 3, c, low], am.at[j, low], dy=3)

    def input_total(j):
        for name in ("p0", "apl", "amt", "apt", "aml"):
            arrived(f"{name}{j}")
        return (
            sd[j, 0, c].astype(F32)
            + sr[j, 0].astype(F32)
            + ap[j].astype(F32)
            + am[j].astype(F32)
        )

    def input_last(j):
        sd[j, 0, c] = input_total(j).astype(BF16)
        step = gray(j)
        send(f"xr{step}", sd.at[j, 0, c], xr.at[step - 1], dx=step)

    def weight_parts(d):
        for half in range(2):
            part = lax.dot_general(
                xb[ring(z, d) * 2 + half],
                hid[...],
                (((0,), (0,)), ((), ())),
                preferred_element_type=F32,
            ).astype(BF16)
            for piece in range(2):
                place = lax.rem(half * 2 + piece - x + 7, 4)
                rows = pl.ds(pl.multiple_of(place * 96, 96), 96)
                first = piece * ROWS
                dw[d, 0, rows, :] = part[first : first + 96]
                dw[d, 1, rows, :] = part[first + 96 : first + ROWS]

    def weight_via():
        arrived("zvp")
        arrived("zvm")
        for q in range(4):
            rows = pl.ds(q * 96, 96)
            dw[1, 0, rows] = (dw[1, 0, rows].astype(F32) + zvp[rows].astype(F32)).astype(BF16)
            send(f"zapc{q}", dw.at[1, 0, rows], zap.at[0, rows], dz=1)
            dw[3, 1, rows] = (dw[3, 1, rows].astype(F32) + zvm[rows].astype(F32)).astype(BF16)
            send(f"zamc{q}", dw.at[3, 1, rows], zam.at[1, rows], dz=3)

    def weight_last(q):
        if q == 0:
            arrived("zapd")
            arrived("zamd")
        arrived(f"zapc{q}")
        arrived(f"zamc{q}")
        rows = pl.ds(q * 96, 96)
        for half in range(2):
            total = (
                dw[0, half, rows].astype(F32)
                + zap[half, rows].astype(F32)
                + zam[half, rows].astype(F32)
            )
            tot[q, pl.ds(half * 96, 96)] = (total * SCALE).astype(BF16)
        if q < 3:
            send(f"t{q}", tot.at[q], dw_ref.at[:, cols_of(0)], dx=q + 1)

    with jax.named_scope("hidden0"):
        hidden(0)
    with jax.named_scope("hidden1"):
        hidden(1)
    with jax.named_scope("input_parts1"):
        input_parts(1)
        input_sends(1)
    with jax.named_scope("hidden2"):
        hidden(2)
    with jax.named_scope("input_via1"):
        input_via(1)
    with jax.named_scope("input_parts2"):
        input_parts(2)
        input_sends(2)
    with jax.named_scope("y_forward3"):
        y_forward(3)
        y_last(3)
    with jax.named_scope("hidden3"):
        hidden(3)
    with jax.named_scope("weight_parts2"):
        weight_parts(2)
        send("zvp", dw.at[2, 0], zvp, dz=1)
        send("zvm", dw.at[2, 1], zvm, dz=3)
    with jax.named_scope("input_via2"):
        input_via(2)
    with jax.named_scope("input_parts3"):
        input_parts(3)
        input_sends(3)
    with jax.named_scope("weight_parts13"):
        weight_parts(1)
        send("zapd", dw.at[1, 1], zap.at[1], dz=1)
        weight_parts(3)
        send("zamd", dw.at[3, 0], zam.at[0], dz=3)
    with jax.named_scope("input_last1"):
        input_last(1)
    with jax.named_scope("input_via3"):
        input_via(3)
    with jax.named_scope("input_parts0"):
        input_parts(0)
        input_sends(0)
    with jax.named_scope("weight_via"):
        weight_via()
    with jax.named_scope("weight_parts0"):
        weight_parts(0)
    with jax.named_scope("input_last2"):
        input_last(2)
    with jax.named_scope("input_via0"):
        input_via(0)
    with jax.named_scope("weight_last0"):
        weight_last(0)
    with jax.named_scope("input_last3"):
        input_last(3)
    with jax.named_scope("weight_last1"):
        weight_last(1)
        weight_last(2)
        weight_last(3)
        put_w = pltpu.make_async_copy(tot.at[3], dw_ref.at[:, cols_of(0)], lsem.at[1])
        put_w.start()
    with jax.named_scope("input_final"):
        total = input_total(0)
        for step in (1, 3, 2):
            arrived(f"xr{step}")
            total = total + xr[step - 1].astype(F32)
        dx_ref[...] = total.astype(BF16)
    with jax.named_scope("ends"):
        for q in range(3):
            arrived(f"t{q}")
        put_w.wait()
        for copy in sites.values():
            copy.wait_send()


def shards(activations, act_grad, up_weight, width_steps):
    any_space = pl.BlockSpec(memory_space=pl.ANY)
    vmem = pl.BlockSpec(memory_space=pltpu.VMEM)

    def buffer(*shape):
        return pltpu.VMEM(shape, BF16)

    return pl.pallas_call(
        kernel,
        out_shape=(
            jax.ShapeDtypeStruct((TOK, COLS), BF16),
            jax.ShapeDtypeStruct((ROWS, HID), BF16),
        ),
        in_specs=[any_space, any_space, any_space, vmem],
        out_specs=(vmem, any_space),
        scratch_shapes=[
            buffer(8, 4 * TOK, COLS),
            buffer(16 * ROWS, COLS),
            buffer(4 * TOK, COLS),
            buffer(TOK, HID),
            buffer(4 * TOK, COLS),
            buffer(4, 4, 2, TOK, COLS),
            buffer(4, 4, TOK, COLS),
            buffer(4, 128, COLS),
            buffer(4, 128, COLS),
            buffer(4, TOK, COLS),
            buffer(4, TOK, COLS),
            buffer(3, TOK, COLS),
            buffer(4, 2, 384, COLS),
            buffer(384, COLS),
            buffer(384, COLS),
            buffer(2, 384, COLS),
            buffer(2, 384, COLS),
            buffer(4, ROWS, COLS),
            pltpu.SemaphoreType.DMA((N_SEM,)),
            pltpu.SemaphoreType.DMA((N_SEM,)),
            pltpu.SemaphoreType.DMA((3,)),
        ],
        compiler_params=pltpu.CompilerParams(
            collective_id=0, has_side_effects=True, vmem_limit_bytes=50 * 2**20
        ),
        cost_estimate=pl.CostEstimate(
            flops=3 * 2 * 1024 * 3072 * 384, bytes_accessed=4 * 2**20, transcendentals=0
        ),
        name="elastic_up_backward",
    )(activations, act_grad, up_weight, width_steps.reshape(2, 128))


def solution(mesh):
    placed = (P("dp", "tensor"), P("dp", "tensor"), P("dp", "tensor"), P("dp"))
    return jax.shard_map(
        shards,
        mesh=mesh,
        in_specs=placed,
        out_specs=(P("dp", "tensor"), P("dp", "tensor")),
        check_vma=False,
    )
```

```python
import jax
import jax.numpy as jnp
from jax import lax
from jax.experimental import pallas as pl
from jax.experimental.pallas import tpu as pltpu
from jax.sharding import PartitionSpec as P

MESH = pl.DeviceIdType.MESH
F32 = jnp.float32
BF16 = jnp.bfloat16
TOK = 256
HALF = 128
ROWS = 192
COLS = 384
HID = 1536
SCALE = 1.0 / 64.0
N_SEM = 168

STEP = (0, 1, 3, 2)
FROM = (0, 3, 1, 2)
PLACE = (2, 0, 1, 3)

ORDER = (
    "mask", "g13", "g2", "zfp0", "zfm0", "yfp0", "yfm0", "wa2", "wa1", "zdm0", "zdp0", "xa2", "xa1", "zl0",
    "zfp2", "zfm2", "xb2", "xb1", "zdp2", "zdm2", "yfp2", "zfp1", "zfm1", "wa3", "yfp1", "zdp1", "zdm1",
    "zl2", "xa3", "yfm2", "zl1", "xb3", "yfm1", "zfp3", "zfm3", "zdp3", "zdm3", "zl3", "wr2", "P0", "yfp3",
    "yfm3", "PA", "IA1", "IA3", "P3", "D21", "IA0", "IB2", "IA2", "E21", "D20", "D10", "D31", "R1", "E20",
    "IB3", "E10", "E31", "IB1", "D11", "R2", "D30", "IB0", "E11", "D01", "E30", "ZVm", "S0", "ZVp", "D00",
    "E01", "R3", "E00", "Vm", "Vp", "ZL0", "ZL1", "ZL2", "R0", "ZL3", "RF",
)

def kernel(
    x_ref, g_ref, w_ref, wid_ref, dx_ref, dw_ref,
    xb, wb, gb, gin, wid, hid, sd, qb, vp, vm, ap, am, rb, xr, own,
    dwp, dwr, dws, zvp, zvm, zap, zam, tot, ssem, rsem, lsem,
):
    dp, tensor = lax.axis_index("dp"), lax.axis_index("tensor")
    z, x = lax.div(dp, 4), lax.rem(dp, 4)
    y, c = lax.div(tensor, 2), lax.rem(tensor, 2)
    other = 1 - c

    def ring(v, step):
        return lax.rem(v + step, 4)

    def device(dz=0, dx=0, dy=0, dc=0):
        return (
            ring(z, dz) * 4 + ring(x, dx),
            ring(y, dy) * 2 + (other if dc else c),
        )

    sites = {}

    def send(name, src, dst, **to):
        slot = len(sites)
        copy = pltpu.make_async_remote_copy(
            src_ref=src,
            dst_ref=dst,
            send_sem=ssem.at[slot],
            recv_sem=rsem.at[slot],
            device_id=device(**to),
            device_id_type=MESH,
        )
        copy.start()
        sites[name] = copy

    def arrived(*names):
        for name in names:
            sites[name].wait_recv()

    def place(j):
        return pl.ds(PLACE[j] * HALF, HALF)

    def chunk(dy, core):
        return ring(y, dy) * 2 + core

    def half_of(core):
        return pl.ds(pl.multiple_of(core * HALF, HALF), HALF)

    def weight_rows(dz, dx):
        return pl.ds(pl.multiple_of((ring(z, dz) * 4 + ring(x, dx)) * ROWS, ROWS), ROWS)

    def weight_half(dz, dx, half):
        start = (ring(z, dz) * 4 + ring(x, dx)) * ROWS + half * 96
        return pl.ds(pl.multiple_of(start, 96), 96)

    def sub_block(step):
        return pl.ds(pl.multiple_of(ring(x, step) * COLS, COLS), COLS)

    own_cols = pl.ds(pl.multiple_of(c * COLS, COLS), COLS)

    own_w = pltpu.make_async_copy(
        w_ref.at[:, sub_block(0)], wb.at[weight_rows(0, 0), own_cols], lsem.at[2]
    )
    own_x = pltpu.make_async_copy(
        x_ref.at[half_of(c)], xb.at[chunk(0, c), place(0)], lsem.at[1]
    )
    own_g = pltpu.make_async_copy(g_ref, gin, lsem.at[0])
    own_wid = pltpu.make_async_copy(wid_ref, wid, lsem.at[3])
    own_wid.start()
    own_g.start()
    own_x.start()
    own_w.start()
    put_g = pltpu.make_async_copy(
        gin.at[half_of(c), sub_block(0)], gb.at[place(0), own_cols], lsem.at[0]
    )
    put_w = pltpu.make_async_copy(tot.at[3], dw_ref.at[:, sub_block(0)], lsem.at[1])

    partners = (
        dict(dx=1), dict(dx=3), dict(dx=2), dict(dy=1), dict(dy=3), dict(dz=1), dict(dz=3), dict(dc=1),
        dict(dx=1, dc=1), dict(dx=3, dc=1), dict(dx=2, dc=1), dict(dy=1, dc=1), dict(dy=3, dc=1),
    )
    barrier = pltpu.get_barrier_semaphore()
    for to in partners:
        pl.semaphore_signal(barrier, inc=1, device_id=device(**to), device_id_type=MESH)
    pl.semaphore_wait(barrier, len(partners))

    tasks = {}

    def task(name, *args):
        def enter(step):
            tasks[name] = lambda: step(*args)
            return step

        return enter

    def x_send(step, kind):
        core, dc = (c, 0) if kind == "s" else (other, 1)
        j = FROM[STEP.index(step)]
        dst = xb.at[chunk(0, c), place(STEP.index(j))]
        send(f"x{step}{kind}", x_ref.at[half_of(core)], dst, dx=step, dc=dc)

    def y_send(j, name, kind):
        dy = 1 if name == "yp" else 3
        if j == 0:
            core, dc = (c, 0) if kind == "s" else (other, 1)
            send(f"{name}0{kind}", x_ref.at[half_of(core)], xb.at[chunk(0, c), place(0)], dy=dy, dc=dc)
        else:
            ref = xb.at[chunk(0, c if kind == "s" else other), place(j)]
            send(f"{name}{j}{kind}", ref, ref, dy=dy)

    def x_arrive(j, kind):
        arrived(f"x{FROM[j]}{kind}")
        y_send(j, "yp", kind)
        y_send(j, "ym", kind)

    def y_forward_up(j):
        arrived(f"yp{j}s")
        ref = xb.at[chunk(3, c), place(j)]
        send(f"yfp{j}", ref, ref, dy=1)

    def y_forward_down(j):
        arrived(f"ym{j}o")
        ref = xb.at[chunk(1, other), place(j)]
        send(f"yfm{j}", ref, ref, dy=3)

    def w_send(step):
        dst = wb.at[weight_rows(0, 0), own_cols]
        send(f"w{step}", w_ref.at[:, sub_block(step)], dst, dx=step)

    def z_send(j, name, half):
        dst = wb.at[weight_half(0, STEP[j], half), own_cols]
        src = w_ref.at[pl.ds(half * 96, 96), sub_block(0)] if j == 0 else dst
        send(f"{name}{j}{'ab'[half]}", src, dst, dz=1 if name == "zp" else 3)

    def w_arrive(j):
        arrived(f"w{FROM[j]}")
        z_send(j, "zp", 0)
        z_send(j, "zm", 1)
        z_send(j, "zp", 1)
        z_send(j, "zm", 0)
        w_pair(f"ws{j}", 0, j)

    def w_pair(name, dz, j):
        dst = wb.at[weight_rows(dz, STEP[j]), own_cols]
        src = w_ref.at[:, sub_block(0)] if name == "ws0" else dst
        send(name, src, dst, dc=1)

    def z_forward_up(j):
        arrived(f"zp{j}a")
        ref = wb.at[weight_half(3, STEP[j], 0), own_cols]
        send(f"zfp{j}", ref, ref, dz=1)

    def z_forward_down(j):
        arrived(f"zm{j}b")
        ref = wb.at[weight_half(1, STEP[j], 1), own_cols]
        send(f"zfm{j}", ref, ref, dz=3)

    def z_whole_up(j):
        arrived(f"zp{j}b")
        w_pair(f"d1{j}", 3, j)

    def z_whole_down(j):
        arrived(f"zm{j}a")
        w_pair(f"d3{j}", 1, j)

    def z_across(j):
        arrived(f"zfp{j}", f"zfm{j}")
        w_pair(f"d2{j}", 2, j)

    @task("wr2")
    def weights_ready():
        own_w.wait()
        for j in range(4):
            arrived(f"ws{j}", f"d1{j}", f"d3{j}", f"d2{j}")

    def g_send(step, kind):
        core, dc = (c, 0) if kind == "s" else (other, 1)
        j = FROM[STEP.index(step)]
        dst = gb.at[place(STEP.index(j)), own_cols]
        send(f"g{step}{kind}", gin.at[half_of(core), sub_block(step)], dst, dx=step, dc=dc)

    @task("mask")
    def mask():
        own_wid.wait()
        own_g.wait()
        for half in range(2):
            rows = pl.ds(half * 128, 128)
            width = jnp.broadcast_to(wid[half : half + 1, :], (128, 128)).T
            keep = jnp.where(width > tensor, 1.0, 0.0).astype(BF16)
            for part in range(HID // 128):
                lanes = pl.ds(part * 128, 128)
                gin[rows, lanes] = gin[rows, lanes] * keep
        put_g.start()
        send("gs", gin.at[half_of(other), sub_block(0)], gb.at[place(0), own_cols], dc=1)

    @task("g13")
    def g_near():
        g_send(1, "s")
        g_send(3, "s")
        g_send(1, "o")
        g_send(3, "o")

    @task("g2")
    def g_across():
        g_send(2, "s")
        g_send(2, "o")

    for j in range(4):
        if j:
            task(f"xa{j}", j, "s")(x_arrive)
            task(f"xb{j}", j, "o")(x_arrive)
            task(f"wa{j}", j)(w_arrive)
        task(f"yfp{j}", j)(y_forward_up)
        task(f"yfm{j}", j)(y_forward_down)
        task(f"zfp{j}", j)(z_forward_up)
        task(f"zfm{j}", j)(z_forward_down)
        task(f"zdp{j}", j)(z_whole_up)
        task(f"zdm{j}", j)(z_whole_down)
        task(f"zl{j}", j)(z_across)

    def hidden(*places):
        for j in places:
            arrived(f"yp{j}o", f"ym{j}s", f"yfp{j}", f"yfm{j}")
            if j == 0:
                own_x.wait()
                put_g.wait()
                arrived("xs", "gs")
            else:
                arrived(f"g{FROM[j]}s", f"g{FROM[j]}o")
        rows = pl.ds(PLACE[places[0]] * HALF, HALF * len(places))
        whole = jnp.concatenate([xb[k, rows, :] for k in range(8)], axis=1)
        preact = jnp.dot(whole, wb[...], preferred_element_type=F32)
        slope = 2.0 * jnp.maximum(preact, 0.0)
        hid[rows, :] = (gb[rows, :].astype(F32) * slope).astype(BF16)

    task("PA", 1, 2)(hidden)
    task("P0", 0)(hidden)
    task("P3", 3)(hidden)

    first, second = pl.ds(0, 128), pl.ds(128, 128)
    upper, lower = pl.ds(0, 64), pl.ds(64, 64)

    def input_part(b, d):
        rows = pl.ds(pl.multiple_of(ring(y, d) * 768, 768), 768)
        sd[b, d] = lax.dot_general(
            hid[pl.ds(b * 256, 256), :], wb[rows, :], (((1,), (1,)), ((), ())), preferred_element_type=F32
        ).astype(BF16)
        if d == 2 and b == 0:
            send("q1", sd.at[0, 2, first], qb.at[0], dx=1)
            send("q3", sd.at[0, 2, second], qb.at[2], dx=3)
        elif d == 2:
            send("q2", sd.at[1, 2, second], qb.at[1], dx=2)
        elif d == 1 and b == 0:
            send("a11", sd.at[0, 1, first], ap.at[0], dy=1)
            send("a12", sd.at[0, 1, second], ap.at[1], dy=1)
        elif d == 3 and b == 0:
            send("a31", sd.at[0, 3, first], am.at[0], dy=3)
            send("a32", sd.at[0, 3, second], am.at[1], dy=3)
        elif d == 1:
            send("a13", sd.at[1, 1, second], ap.at[3], dy=1)
            send("a10l", sd.at[1, 1, lower], ap.at[2, lower], dy=1)
        elif d == 3:
            send("a33", sd.at[1, 3, second], am.at[3], dy=3)
            send("a30t", sd.at[1, 3, upper], am.at[2, upper], dy=3)

    for b in range(2):
        for d in range(4):
            task(f"I{'AB'[b]}{d}", b, d)(input_part)

    @task("S0")
    def across_total():
        arrived("q1", "q3", "q2")
        total = sd[1, 2, first].astype(F32)
        for slot in range(3):
            total = total + qb[slot].astype(F32)
        sd[1, 2, first] = total.astype(BF16)
        send("vp", sd.at[1, 2, upper], vp, dy=1)
        send("vm", sd.at[1, 2, lower], vm, dy=3)

    @task("Vp")
    def via_up():
        arrived("vp")
        sd[1, 1, upper] = (sd[1, 1, upper].astype(F32) + vp[...].astype(F32)).astype(BF16)
        send("a10t", sd.at[1, 1, upper], ap.at[2, upper], dy=1)

    @task("Vm")
    def via_down():
        arrived("vm")
        sd[1, 3, lower] = (sd[1, 3, lower].astype(F32) + vm[...].astype(F32)).astype(BF16)
        send("a30l", sd.at[1, 3, lower], am.at[2, lower], dy=3)

    def input_total(j):
        if j == 0:
            arrived("a10l", "a10t", "a30t", "a30l")
        else:
            arrived(f"a1{j}", f"a3{j}")
        at, rows = PLACE[j], (first, second)[PLACE[j] % 2]
        total = sd[at // 2, 0, rows].astype(F32) + ap[at].astype(F32) + am[at].astype(F32)
        total = total.astype(BF16)
        rb[at, 0] = total[:, :COLS]
        rb[at, 1] = total[:, COLS:]
        if j == 0:
            own[c] = rb[at, c]
            send("xro", rb.at[at, other], own.at[c], dc=1)
        else:
            step = STEP[j]
            send(f"xr{step}s", rb.at[at, c], xr.at[step - 1, c], dx=step)
            send(f"xr{step}o", rb.at[at, other], xr.at[step - 1, c], dx=step, dc=1)

    for j in range(4):
        task(f"R{j}", j)(input_total)

    @task("RF")
    def input_final():
        arrived("xr1s", "xr1o", "xr3s", "xr3o", "xr2s", "xr2o", "xro")
        for half in range(2):
            total = own[half].astype(F32)
            for slot in range(3):
                total = total + xr[slot, half].astype(F32)
            dx_ref[pl.ds(half * HALF, HALF), :] = total.astype(BF16)

    def weight_part(d, h):
        part = lax.dot_general(
            xb[ring(z, d) * 2 + h], hid[...], (((0,), (0,)), ((), ())), preferred_element_type=F32
        ).astype(BF16)
        dwp[d, h, 0] = part[:, :COLS]
        dwp[d, h, 1] = part[:, COLS:]
        send(f"e{d}{h}", dwp.at[d, h, other], dwr.at[d, h], dc=1)

    def weight_pair(d, h):
        arrived(f"e{d}{h}")
        total = (dwp[d, h, c].astype(F32) + dwr[d, h].astype(F32)).astype(BF16)
        for p in range(2):
            at = lax.rem(h * 2 + p - x + 7, 4)
            rows = pl.ds(pl.multiple_of(at * 96, 96), 96)
            dws[d, 0, rows] = total[p * ROWS : p * ROWS + 96]
            dws[d, 1, rows] = total[p * ROWS + 96 : p * ROWS + ROWS]
            if d == 2:
                send(f"zvp{h}{p}", dws.at[2, 0, rows], zvp.at[rows], dz=1)
                send(f"zvm{h}{p}", dws.at[2, 1, rows], zvm.at[rows], dz=3)
            elif d == 1:
                send(f"zdp{h}{p}", dws.at[1, 1, rows], zap.at[1, rows], dz=1)
            elif d == 3:
                send(f"zdm{h}{p}", dws.at[3, 0, rows], zam.at[0, rows], dz=3)

    for d in range(4):
        for h in range(2):
            task(f"D{d}{h}", d, h)(weight_part)
            task(f"E{d}{h}", d, h)(weight_pair)

    def sub_rows(q):
        return pl.ds(q * 96, 96)

    @task("ZVp")
    def weight_via_up():
        arrived("zvp00", "zvp01", "zvp10", "zvp11")
        for q in range(4):
            rows = sub_rows(q)
            dws[1, 0, rows] = (dws[1, 0, rows].astype(F32) + zvp[rows].astype(F32)).astype(BF16)
            send(f"zcp{q}", dws.at[1, 0, rows], zap.at[0, rows], dz=1)

    @task("ZVm")
    def weight_via_down():
        arrived("zvm00", "zvm01", "zvm10", "zvm11")
        for q in range(4):
            rows = sub_rows(q)
            dws[3, 1, rows] = (dws[3, 1, rows].astype(F32) + zvm[rows].astype(F32)).astype(BF16)
            send(f"zcm{q}", dws.at[3, 1, rows], zam.at[1, rows], dz=3)

    def weight_last(q):
        if q == 0:
            for tail in ("00", "01", "10", "11"):
                arrived("zdp" + tail, "zdm" + tail)
        arrived(f"zcp{q}", f"zcm{q}")
        rows = sub_rows(q)
        for half in range(2):
            total = (
                dws[0, half, rows].astype(F32) + zap[half, rows].astype(F32) + zam[half, rows].astype(F32)
            )
            tot[q, pl.ds(half * 96, 96)] = (total * SCALE).astype(BF16)
        if q < 3:
            send(f"t{q}", tot.at[q], dw_ref.at[:, sub_block(0)], dx=q + 1)
        else:
            put_w.start()

    for q in range(4):
        task(f"ZL{q}", q)(weight_last)

    w_send(1)
    w_send(3)
    x_send(1, "s")
    x_send(3, "s")
    y_send(0, "yp", "s")
    y_send(0, "ym", "o")
    z_send(0, "zp", 0)
    z_send(0, "zm", 1)
    x_send(1, "o")
    x_send(3, "o")
    y_send(0, "yp", "o")
    y_send(0, "ym", "s")
    z_send(0, "zp", 1)
    z_send(0, "zm", 0)
    w_pair("ws0", 0, 0)
    send("xs", x_ref.at[half_of(other)], xb.at[chunk(0, c), place(0)], dc=1)
    w_send(2)
    x_send(2, "s")
    x_send(2, "o")
    for name in ORDER:
        tasks[name]()
    arrived("t0", "t1", "t2")
    put_w.wait()
    for copy in sites.values():
        copy.wait_send()


def shards(activations, act_grad, up_weight, width_steps):
    any_space = pl.BlockSpec(memory_space=pl.ANY)
    vmem = pl.BlockSpec(memory_space=pltpu.VMEM)

    def buffer(*shape):
        return pltpu.VMEM(shape, BF16)

    return pl.pallas_call(
        kernel,
        out_shape=(
            jax.ShapeDtypeStruct((TOK, COLS), BF16),
            jax.ShapeDtypeStruct((ROWS, HID), BF16),
        ),
        in_specs=[any_space, any_space, any_space, any_space],
        out_specs=(vmem, any_space),
        scratch_shapes=[
            buffer(8, 4 * HALF, COLS),
            buffer(16 * ROWS, 2 * COLS),
            buffer(4 * HALF, 2 * COLS),
            buffer(TOK, HID),
            pltpu.VMEM((2, 128), jnp.int32),
            buffer(4 * HALF, 2 * COLS),
            buffer(2, 4, 2 * HALF, 2 * COLS),
            buffer(3, HALF, 2 * COLS),
            buffer(64, 2 * COLS),
            buffer(64, 2 * COLS),
            buffer(4, HALF, 2 * COLS),
            buffer(4, HALF, 2 * COLS),
            buffer(4, 2, HALF, COLS),
            buffer(3, 2, HALF, COLS),
            buffer(2, HALF, COLS),
            buffer(4, 2, 2, 384, COLS),
            buffer(4, 2, 384, COLS),
            buffer(4, 2, 384, COLS),
            buffer(384, COLS),
            buffer(384, COLS),
            buffer(2, 384, COLS),
            buffer(2, 384, COLS),
            buffer(4, ROWS, COLS),
            pltpu.SemaphoreType.DMA((N_SEM,)),
            pltpu.SemaphoreType.DMA((N_SEM,)),
            pltpu.SemaphoreType.DMA((4,)),
        ],
        compiler_params=pltpu.CompilerParams(
            collective_id=0, has_side_effects=True, vmem_limit_bytes=60 * 2**20
        ),
        cost_estimate=pl.CostEstimate(
            flops=3 * 2 * 512 * 3072 * 768, bytes_accessed=4 * 2**20, transcendentals=0
        ),
        name="elastic_up_backward",
    )(activations, act_grad, up_weight, width_steps.reshape(2, 128))


def solution(mesh):
    placed = (P("dp", "tensor"), P("dp", "tensor"), P("dp", "tensor"), P("dp"))
    return jax.shard_map(
        shards,
        mesh=mesh,
        in_specs=placed,
        out_specs=(P("dp", "tensor"), P("dp", "tensor")),
        check_vma=False,
    )
```

```python
import jax
import jax.numpy as jnp
from jax import lax
from jax.experimental import pallas as pl
from jax.experimental.pallas import tpu as pltpu
from jax.sharding import PartitionSpec as P

MESH = pl.DeviceIdType.MESH
F32 = jnp.float32
BF16 = jnp.bfloat16
TOK = 256
HALF = 128
ROWS = 192
COLS = 384
HID = 1536
SCALE = 1.0 / 64.0
N_SEM = 176

STEP = (0, 1, 3, 2)
FROM = (0, 3, 1, 2)
PLACE = (2, 0, 1, 3)
SLOT = (0, 1, 3, 2)
SUB = (2, 1, 3, 0)

ORDER = (
    "xa2", "yfp0", "xb1", "zfm0", "zfp0", "wa2", "yfm0", "zdm0", "w2s", "wa1", "xa1", "xa3", "mask", "zfp2",
    "yfp2", "xb3", "zfm2", "xy3", "xy1", "zdp0", "wa3", "g13", "zdm2", "zl0", "yfm1", "zfp1", "zfm1", "xb2",
    "zdm1", "zdp2", "zfm3", "zfp3", "zdp1", "yfp3", "g2", "yfm3", "zl2", "zdp3", "zdm3", "zl1", "wr1", "Pa0",
    "zl3", "PaA", "wr2", "PbA", "IA1", "IA3", "Pa3", "Pb0", "Pb3", "D20", "IA2", "D31", "IB2", "D10", "IA0",
    "E20", "D21", "D11", "E31", "D30", "E21", "D00", "IB1", "E10", "IB3", "E11", "sent", "E30", "R1", "Zc0",
    "E00", "Zd0", "R2", "D01", "V3p", "E01", "V3m", "S0", "Zd1", "Zd2", "Zc1", "ZL0", "IB0", "Zc2", "R3",
    "Vm", "Zd3", "ZL1", "Vp", "ZL2", "Zc3", "R0", "RF", "ZL3",
)

def kernel(
    x_ref, g_ref, w_ref, wid_ref, dx_ref, dw_ref,
    xb, wb, gb, gin, wid, acc, hid, sd, qb, vp, vm, vp3, vm3, ap, am, rb, xr, own, out,
    dwp, dwr, dws, zvp, zvm, zap, zam, tot, ssem, rsem, lsem,
):
    dp, tensor = lax.axis_index("dp"), lax.axis_index("tensor")
    z, x = lax.div(dp, 4), lax.rem(dp, 4)
    y, c = lax.div(tensor, 2), lax.rem(tensor, 2)
    other = 1 - c

    def ring(v, step):
        return lax.rem(v + step, 4)

    def device(dz=0, dx=0, dy=0, dc=0):
        return (
            ring(z, dz) * 4 + ring(x, dx),
            ring(y, dy) * 2 + (other if dc else c),
        )

    sites = {}

    def send(name, src, dst, **to):
        slot = len(sites)
        copy = pltpu.make_async_remote_copy(
            src_ref=src,
            dst_ref=dst,
            send_sem=ssem.at[slot],
            recv_sem=rsem.at[slot],
            device_id=device(**to),
            device_id_type=MESH,
        )
        copy.start()
        sites[name] = copy

    taken = set()

    def arrived(*names):
        for name in names:
            if name not in taken:
                taken.add(name)
                sites[name].wait_recv()

    def place(j):
        return pl.ds(PLACE[j] * HALF, HALF)

    def chunk(dy, core):
        return ring(y, dy) * 2 + core

    def half_of(core):
        return pl.ds(pl.multiple_of(core * HALF, HALF), HALF)

    def weight_rows(dz, dx):
        return pl.ds(pl.multiple_of(SLOT[dz] * 768 + ring(x, dx) * ROWS, ROWS), ROWS)

    def weight_half(dz, dx, half):
        start = SLOT[dz] * 768 + ring(x, dx) * ROWS + half * 96
        return pl.ds(pl.multiple_of(start, 96), 96)

    def sub_block(step):
        return pl.ds(pl.multiple_of(ring(x, step) * COLS, COLS), COLS)

    own_cols = pl.ds(pl.multiple_of(c * COLS, COLS), COLS)

    own_w = pltpu.make_async_copy(
        w_ref.at[:, sub_block(0)], wb.at[weight_rows(0, 0), own_cols], lsem.at[2]
    )
    own_x = pltpu.make_async_copy(
        x_ref.at[half_of(c)], xb.at[chunk(0, c), place(0)], lsem.at[1]
    )
    own_g = pltpu.make_async_copy(g_ref, gin, lsem.at[0])
    own_wid = pltpu.make_async_copy(wid_ref, wid, lsem.at[3])
    own_wid.start()
    own_g.start()
    own_x.start()
    own_w.start()
    put_g = pltpu.make_async_copy(
        gin.at[half_of(c), sub_block(0)], gb.at[place(0), own_cols], lsem.at[0]
    )
    put_w = pltpu.make_async_copy(tot.at[3], dw_ref.at[:, sub_block(0)], lsem.at[1])
    put_x = pltpu.make_async_copy(out, dx_ref, lsem.at[2])

    partners = (
        dict(dx=1), dict(dx=3), dict(dx=2), dict(dy=1), dict(dy=3), dict(dz=1), dict(dz=3), dict(dc=1),
        dict(dx=1, dc=1), dict(dx=3, dc=1), dict(dx=2, dc=1), dict(dy=1, dc=1), dict(dy=3, dc=1),
    )
    barrier = pltpu.get_barrier_semaphore()
    for to in partners:
        pl.semaphore_signal(barrier, inc=1, device_id=device(**to), device_id_type=MESH)
    pl.semaphore_wait(barrier, len(partners))

    tasks = {}

    def task(name, *args):
        def enter(step):
            tasks[name] = lambda: step(*args)
            return step

        return enter

    def x_send(step, kind):
        core, dc = (c, 0) if kind == "s" else (other, 1)
        j = FROM[STEP.index(step)]
        dst = xb.at[chunk(0, c), place(STEP.index(j))]
        send(f"x{step}{kind}", x_ref.at[half_of(core)], dst, dx=step, dc=dc)

    def y_send(j, name, kind):
        dy = 1 if name == "yp" else 3
        if j == 0:
            core, dc = (c, 0) if kind == "s" else (other, 1)
            send(f"{name}0{kind}", x_ref.at[half_of(core)], xb.at[chunk(0, c), place(0)], dy=dy, dc=dc)
        else:
            ref = xb.at[chunk(0, c if kind == "s" else other), place(j)]
            send(f"{name}{j}{kind}", ref, ref, dy=dy)

    def x_arrive(j, kind):
        if j < 3:
            arrived(f"x{FROM[j]}{kind}")
        else:
            arrived("xf1" if kind == "s" else "xf3")
        if j == 2 and kind == "s":
            at = chunk(0, c)
            send("xf1", xb.at[at, place(2)], xb.at[at, place(3)], dx=1)
        if j == 1 and kind == "o":
            at = chunk(0, other)
            send("xf3", xb.at[at, place(1)], xb.at[at, place(3)], dx=3)
        for name in ("yp", "ym") if kind == "s" else ("ym", "yp"):
            y_send(j, name, kind)

    @task("xy3")
    def across_back():
        arrived("yfp0")
        at = chunk(2, c)
        send("xy3s", xb.at[at, place(0)], xb.at[at, place(1)], dx=3)

    @task("xy1")
    def across_on():
        arrived("yfm0")
        at = chunk(2, other)
        send("xy1o", xb.at[at, place(0)], xb.at[at, place(2)], dx=1)

    def y_forward_up(j):
        arrived(f"yp{j}s")
        ref = xb.at[chunk(3, c), place(j)]
        send(f"yfp{j}", ref, ref, dy=1)

    def y_forward_down(j):
        arrived(f"ym{j}o")
        ref = xb.at[chunk(1, other), place(j)]
        send(f"yfm{j}", ref, ref, dy=3)

    def w_send(step):
        dst = wb.at[weight_rows(0, 0), own_cols]
        send(f"w{step}", w_ref.at[:, sub_block(step)], dst, dx=step)

    def z_send(j, name, half):
        to = 1 if name == "zp" else 3
        src = wb.at[weight_half(0, STEP[j], half), own_cols]
        if j == 0:
            src = w_ref.at[pl.ds(half * 96, 96), sub_block(0)]
        dst = wb.at[weight_half(4 - to, STEP[j], half), own_cols]
        send(f"{name}{j}{'ab'[half]}", src, dst, dz=to)

    def w_arrive(j):
        arrived(f"w{FROM[j]}")
        z_send(j, "zp", 0)
        z_send(j, "zm", 1)
        z_send(j, "zp", 1)
        z_send(j, "zm", 0)
        w_pair(f"ws{j}", 0, j)

    def w_pair(name, dz, j):
        dst = wb.at[weight_rows(dz, STEP[j]), own_cols]
        src = w_ref.at[:, sub_block(0)] if name == "ws0" else dst
        send(name, src, dst, dc=1)

    def z_forward_up(j):
        arrived(f"zp{j}a")
        src = wb.at[weight_half(3, STEP[j], 0), own_cols]
        send(f"zfp{j}", src, wb.at[weight_half(2, STEP[j], 0), own_cols], dz=1)

    def z_forward_down(j):
        arrived(f"zm{j}b")
        src = wb.at[weight_half(1, STEP[j], 1), own_cols]
        send(f"zfm{j}", src, wb.at[weight_half(2, STEP[j], 1), own_cols], dz=3)

    def z_whole_up(j):
        arrived(f"zp{j}b")
        w_pair(f"d1{j}", 3, j)

    def z_whole_down(j):
        arrived(f"zm{j}a")
        w_pair(f"d3{j}", 1, j)

    def z_across(j):
        arrived(f"zfp{j}", f"zfm{j}")
        w_pair(f"d2{j}", 2, j)

    @task("w2s")
    def w_across():
        w_send(2)

    @task("wr1")
    def weights_near():
        own_w.wait()
        for j in range(4):
            arrived(f"ws{j}", f"d1{j}", f"d3{j}")

    @task("wr2")
    def weights_across():
        for j in range(4):
            arrived(f"d2{j}")

    def g_send(step, kind):
        core, dc = (c, 0) if kind == "s" else (other, 1)
        j = FROM[STEP.index(step)]
        dst = gb.at[place(STEP.index(j)), own_cols]
        send(f"g{step}{kind}", gin.at[half_of(core), sub_block(step)], dst, dx=step, dc=dc)

    @task("mask")
    def mask():
        own_wid.wait()
        own_g.wait()
        for half in range(2):
            rows = pl.ds(half * 128, 128)
            width = jnp.broadcast_to(wid[half : half + 1, :], (128, 128)).T
            keep = jnp.where(width > tensor, 1.0, 0.0).astype(BF16)
            for part in range(HID // 128):
                lanes = pl.ds(part * 128, 128)
                gin[rows, lanes] = gin[rows, lanes] * keep
        put_g.start()
        send("gs", gin.at[half_of(other), sub_block(0)], gb.at[place(0), own_cols], dc=1)

    @task("g13")
    def g_near():
        g_send(1, "s")
        g_send(3, "s")
        g_send(1, "o")
        g_send(3, "o")

    @task("g2")
    def g_across():
        g_send(2, "s")
        g_send(2, "o")

    for j in range(4):
        if j:
            task(f"xa{j}", j, "s")(x_arrive)
            task(f"xb{j}", j, "o")(x_arrive)
            task(f"wa{j}", j)(w_arrive)
        task(f"yfp{j}", j)(y_forward_up)
        task(f"yfm{j}", j)(y_forward_down)
        task(f"zfp{j}", j)(z_forward_up)
        task(f"zfm{j}", j)(z_forward_down)
        task(f"zdp{j}", j)(z_whole_up)
        task(f"zdm{j}", j)(z_whole_down)
        task(f"zl{j}", j)(z_across)

    def features(dz, rows):
        return [xb[ring(z, dz) * 2 + h, rows, :] for h in range(2)]

    def batch(places):
        return pl.ds(PLACE[places[0]] * HALF, HALF * len(places))

    def hidden_near(*places):
        for j in places:
            arrived(f"yp{j}o", f"ym{j}s")
            if j == 1:
                arrived("yp1s", "xy3s")
            else:
                arrived(f"yfp{j}")
            if j == 2:
                arrived("ym2o", "xy1o")
            else:
                arrived(f"yfm{j}")
            if j == 0:
                own_x.wait()
                arrived("xs")
        rows = batch(places)
        part = jnp.concatenate(features(0, rows) + features(1, rows) + features(3, rows), axis=1)
        acc[rows, :] = jnp.dot(part, wb[pl.ds(0, 2304), :], preferred_element_type=F32)

    def hidden_last(*places):
        for j in places:
            if j == 0:
                put_g.wait()
                arrived("gs")
            else:
                arrived(f"g{FROM[j]}s", f"g{FROM[j]}o")
        rows = batch(places)
        part = jnp.concatenate(features(2, rows), axis=1)
        preact = acc[rows, :] + jnp.dot(part, wb[pl.ds(2304, 768), :], preferred_element_type=F32)
        slope = 2.0 * jnp.maximum(preact, 0.0)
        hid[rows, :] = (gb[rows, :].astype(F32) * slope).astype(BF16)

    for name, places in (("A", (1, 2)), ("0", (0,)), ("3", (3,))):
        task("Pa" + name, *places)(hidden_near)
        task("Pb" + name, *places)(hidden_last)

    first, second = pl.ds(0, 128), pl.ds(128, 128)
    upper, lower = pl.ds(0, 64), pl.ds(64, 64)
    upper3, lower3 = pl.ds(128, 64), pl.ds(192, 64)

    def input_part(b, d):
        dz = lax.rem(y + d - z + 4, 4)
        slot = dz + lax.div(dz, 2) - 2 * lax.div(dz, 3)
        rows = pl.ds(pl.multiple_of(slot * 768, 768), 768)
        sd[b, d] = lax.dot_general(
            hid[pl.ds(b * 256, 256), :], wb[rows, :], (((1,), (1,)), ((), ())), preferred_element_type=F32
        ).astype(BF16)
        if d == 2 and b == 0:
            send("q1", sd.at[0, 2, first], qb.at[0], dx=1)
            send("q3", sd.at[0, 2, second], qb.at[1], dx=3)
        elif d == 2:
            send("vp3", sd.at[1, 2, upper3], vp3, dy=1)
            send("vm3", sd.at[1, 2, lower3], vm3, dy=3)
        elif d == 1 and b == 0:
            send("a11", sd.at[0, 1, first], ap.at[0], dy=1)
            send("a12", sd.at[0, 1, second], ap.at[1], dy=1)
        elif d == 3 and b == 0:
            send("a31", sd.at[0, 3, first], am.at[0], dy=3)
            send("a32", sd.at[0, 3, second], am.at[1], dy=3)
        elif d == 1:
            send("a13l", sd.at[1, 1, lower3], ap.at[3, lower], dy=1)
            send("a10l", sd.at[1, 1, lower], ap.at[2, lower], dy=1)
        elif d == 3:
            send("a33t", sd.at[1, 3, upper3], am.at[3, upper], dy=3)
            send("a30t", sd.at[1, 3, upper], am.at[2, upper], dy=3)

    for b in range(2):
        for d in range(4):
            task(f"I{'AB'[b]}{d}", b, d)(input_part)

    @task("S0")
    def across_total():
        arrived("q1", "q3")
        total = sd[1, 2, first].astype(F32)
        for slot in range(2):
            total = total + qb[slot].astype(F32)
        sd[1, 2, first] = total.astype(BF16)
        send("vp", sd.at[1, 2, upper], vp, dy=1)
        send("vm", sd.at[1, 2, lower], vm, dy=3)

    def via_up(name, came, rows, to, at):
        arrived(name)
        sd[1, 1, rows] = (sd[1, 1, rows].astype(F32) + came[...].astype(F32)).astype(BF16)
        send(to, sd.at[1, 1, rows], ap.at[at, upper], dy=1)

    def via_down(name, came, rows, to, at):
        arrived(name)
        sd[1, 3, rows] = (sd[1, 3, rows].astype(F32) + came[...].astype(F32)).astype(BF16)
        send(to, sd.at[1, 3, rows], am.at[at, lower], dy=3)

    task("Vp", "vp", vp, upper, "a10t", 2)(via_up)
    task("Vm", "vm", vm, lower, "a30l", 2)(via_down)
    task("V3p", "vp3", vp3, upper3, "a13t", 3)(via_up)
    task("V3m", "vm3", vm3, lower3, "a33l", 3)(via_down)

    def input_total(j):
        if j in (0, 3):
            arrived(f"a1{j}l", f"a1{j}t", f"a3{j}t", f"a3{j}l")
        else:
            arrived(f"a1{j}", f"a3{j}")
        at, rows = PLACE[j], (first, second)[PLACE[j] % 2]
        total = sd[at // 2, 0, rows].astype(F32) + ap[at].astype(F32) + am[at].astype(F32)
        total = total.astype(BF16)
        rb[at, 0] = total[:, :COLS]
        rb[at, 1] = total[:, COLS:]
        if j == 0:
            own[c] = rb[at, c]
            send("xro", rb.at[at, other], own.at[c], dc=1)
        else:
            step = STEP[j]
            send(f"xr{step}s", rb.at[at, c], xr.at[step - 1, c], dx=step)
            send(f"xr{step}o", rb.at[at, other], xr.at[step - 1, c], dx=step, dc=1)

    for j in range(4):
        task(f"R{j}", j)(input_total)

    @task("RF")
    def input_final():
        arrived("xr1s", "xr1o", "xr3s", "xr3o", "xr2s", "xr2o", "xro")
        for half in range(2):
            total = own[half].astype(F32)
            for slot in range(3):
                total = total + xr[slot, half].astype(F32)
            out[pl.ds(half * HALF, HALF), :] = total.astype(BF16)
        put_x.start()

    def weight_part(d, h):
        part = lax.dot_general(
            xb[ring(z, d) * 2 + h], hid[...], (((0,), (0,)), ((), ())), preferred_element_type=F32
        ).astype(BF16)
        dwp[d, h, 0] = part[:, :COLS]
        dwp[d, h, 1] = part[:, COLS:]
        send(f"e{d}{h}", dwp.at[d, h, other], dwr.at[d, h], dc=1)

    def weight_pair(d, h):
        arrived(f"e{d}{h}")
        total = (dwp[d, h, c].astype(F32) + dwr[d, h].astype(F32)).astype(BF16)
        for p in range(2):
            step = lax.rem(h * 2 + p - x + 4, 4)
            at = lax.rem(lax.rem(3 * step + 3, 5), 4)
            rows = pl.ds(pl.multiple_of(at * 96, 96), 96)
            dws[d, 0, rows] = total[p * ROWS : p * ROWS + 96]
            dws[d, 1, rows] = total[p * ROWS + 96 : p * ROWS + ROWS]
            if d == 2:
                via_copy("zvp", at, rows).start()
                via_copy("zvm", at, rows).start()

    for d in range(4):
        for h in range(2):
            task(f"D{d}{h}", d, h)(weight_part)
            task(f"E{d}{h}", d, h)(weight_pair)

    def sub_rows(q):
        return pl.ds(q * 96, 96)

    via_slots = {}

    def via_copy(name, at, rows):
        up = name == "zvp"
        return pltpu.make_async_remote_copy(
            src_ref=dws.at[2, 0 if up else 1, rows],
            dst_ref=(zvp if up else zvm).at[rows],
            send_sem=ssem.at[via_slots[name] + at],
            recv_sem=rsem.at[via_slots[name] + at],
            device_id=device(dz=1 if up else 3),
            device_id_type=MESH,
        )

    for name in ("zvp", "zvm"):
        via_slots[name] = len(sites)
        for q in range(4):
            sites[f"{name}{q}"] = via_copy(name, q, sub_rows(q))

    def weight_direct(q):
        rows = sub_rows(q)
        send(f"zdp{q}", dws.at[1, 1, rows], zap.at[1, rows], dz=1)
        send(f"zdm{q}", dws.at[3, 0, rows], zam.at[0, rows], dz=3)

    def weight_via(q):
        arrived(f"zvp{q}", f"zvm{q}")
        rows = sub_rows(q)
        dws[1, 0, rows] = (dws[1, 0, rows].astype(F32) + zvp[rows].astype(F32)).astype(BF16)
        send(f"zcp{q}", dws.at[1, 0, rows], zap.at[0, rows], dz=1)
        dws[3, 1, rows] = (dws[3, 1, rows].astype(F32) + zvm[rows].astype(F32)).astype(BF16)
        send(f"zcm{q}", dws.at[3, 1, rows], zam.at[1, rows], dz=3)

    def weight_last(q):
        arrived(f"zdp{q}", f"zdm{q}", f"zcp{q}", f"zcm{q}")
        rows = sub_rows(q)
        for half in range(2):
            total = (
                dws[0, half, rows].astype(F32) + zap[half, rows].astype(F32) + zam[half, rows].astype(F32)
            )
            tot[q, pl.ds(half * 96, 96)] = (total * SCALE).astype(BF16)
        if q < 3:
            send(f"t{q}", tot.at[q], dw_ref.at[:, sub_block(0)], dx=SUB[q])
        else:
            put_w.start()

    for q in range(4):
        task(f"Zd{q}", q)(weight_direct)
        task(f"Zc{q}", q)(weight_via)
        task(f"ZL{q}", q)(weight_last)

    left = set()

    @task("sent")
    def early_sends():
        for name, copy in list(sites.items()):
            if not name.startswith("zv"):
                left.add(name)
                copy.wait_send()

    x_send(1, "s")
    x_send(3, "o")
    w_send(1)
    w_send(3)
    x_send(1, "o")
    x_send(3, "s")
    y_send(0, "yp", "s")
    y_send(0, "ym", "o")
    z_send(0, "zp", 0)
    z_send(0, "zm", 1)
    y_send(0, "yp", "o")
    y_send(0, "ym", "s")
    z_send(0, "zp", 1)
    z_send(0, "zm", 0)
    w_pair("ws0", 0, 0)
    send("xs", x_ref.at[half_of(other)], xb.at[chunk(0, c), place(0)], dc=1)
    for name in ORDER:
        tasks[name]()
    for name, copy in sites.items():
        if name not in left:
            copy.wait_send()
    arrived("t0", "t1", "t2")
    put_w.wait()
    put_x.wait()


def hand_on(a_ref, b_ref, a_out, b_out, sem):
    first = pltpu.make_async_copy(a_ref, a_out, sem.at[0])
    second = pltpu.make_async_copy(b_ref, b_out, sem.at[1])
    second.start()
    first.start()
    first.wait()
    second.wait()


def shards(activations, act_grad, up_weight, width_steps):
    any_space = pl.BlockSpec(memory_space=pl.ANY)

    def buffer(*shape):
        return pltpu.VMEM(shape, BF16)

    results = (
        jax.ShapeDtypeStruct((TOK, COLS), BF16),
        jax.ShapeDtypeStruct((ROWS, HID), BF16),
    )
    input_grad, weight_grad = pl.pallas_call(
        kernel,
        out_shape=results,
        in_specs=[any_space, any_space, any_space, any_space],
        out_specs=(any_space, any_space),
        scratch_shapes=[
            buffer(8, 4 * HALF, COLS),
            buffer(16 * ROWS, 2 * COLS),
            buffer(4 * HALF, 2 * COLS),
            buffer(TOK, HID),
            pltpu.VMEM((2, 128), jnp.int32),
            pltpu.VMEM((4 * HALF, 2 * COLS), F32),
            buffer(4 * HALF, 2 * COLS),
            buffer(2, 4, 2 * HALF, 2 * COLS),
            buffer(2, HALF, 2 * COLS),
            buffer(64, 2 * COLS),
            buffer(64, 2 * COLS),
            buffer(64, 2 * COLS),
            buffer(64, 2 * COLS),
            buffer(4, HALF, 2 * COLS),
            buffer(4, HALF, 2 * COLS),
            buffer(4, 2, HALF, COLS),
            buffer(3, 2, HALF, COLS),
            buffer(2, HALF, COLS),
            buffer(TOK, COLS),
            buffer(4, 2, 2, 384, COLS),
            buffer(4, 2, 384, COLS),
            buffer(4, 2, 384, COLS),
            buffer(384, COLS),
            buffer(384, COLS),
            buffer(2, 384, COLS),
            buffer(2, 384, COLS),
            buffer(4, ROWS, COLS),
            pltpu.SemaphoreType.DMA((N_SEM,)),
            pltpu.SemaphoreType.DMA((N_SEM,)),
            pltpu.SemaphoreType.DMA((4,)),
        ],
        compiler_params=pltpu.CompilerParams(
            collective_id=0, has_side_effects=True, vmem_limit_bytes=60 * 2**20
        ),
        cost_estimate=pl.CostEstimate(
            flops=3 * 2 * 512 * 3072 * 768, bytes_accessed=4 * 2**20, transcendentals=0
        ),
        name="elastic_up_backward",
    )(activations, act_grad, up_weight, width_steps.reshape(2, 128))
    return pl.pallas_call(
        hand_on,
        out_shape=results,
        in_specs=[any_space, any_space],
        out_specs=(any_space, any_space),
        scratch_shapes=[pltpu.SemaphoreType.DMA((2,))],
        compiler_params=pltpu.CompilerParams(vmem_limit_bytes=60 * 2**20),
        name="hand_on",
    )(input_grad, weight_grad)


def solution(mesh):
    placed = (P("dp", "tensor"), P("dp", "tensor"), P("dp", "tensor"), P("dp"))
    return jax.shard_map(
        shards,
        mesh=mesh,
        in_specs=placed,
        out_specs=(P("dp", "tensor"), P("dp", "tensor")),
        check_vma=False,
    )
```

```python
import jax
import jax.numpy as jnp
from jax import lax
from jax.experimental import pallas as pl
from jax.experimental.pallas import tpu as pltpu
from jax.sharding import PartitionSpec as P

MESH = pl.DeviceIdType.MESH
F32 = jnp.float32
BF16 = jnp.bfloat16
TOK = 256
HALF = 128
ROWS = 192
COLS = 384
HID = 1536
SCALE = 1.0 / 64.0
N_SEM = 176

STEP = (0, 1, 3, 2)
FROM = (0, 3, 1, 2)
PLACE = (2, 0, 1, 3)
SLOT = (0, 1, 3, 2)
SUB = (2, 1, 3, 0)

ORDER = (
    "xa2", "yfp0", "xb1", "zfm0", "zfp0", "wa2", "yfm0", "zdm0", "w2s", "wa1", "xa1", "xa3", "mask", "zfp2",
    "yfp2", "xb3", "zfm2", "xy3", "xy1", "zdp0", "wa3", "g13", "zdm2", "zl0", "yfm1", "zfp1", "zfm1", "xb2",
    "zdm1", "zdp2", "zfm3", "zfp3", "zdp1", "yfp3", "g2", "yfm3", "zl2", "zdp3", "zdm3", "zl1", "wr1", "Pa0",
    "zl3", "PaA", "wr2", "PbA", "IA1", "IA3", "Pa3", "Pb0", "Pb3", "D20", "IA2", "D31", "IB2", "D10", "IA0",
    "E20", "D21", "D11", "E31", "D30", "E21", "D00", "IB1", "E10", "IB3", "E11", "sent", "E30", "R1", "Zc0",
    "E00", "Zd0", "R2", "D01", "V3p", "E01", "V3m", "S0", "Zd1", "Zd2", "Zc1", "ZL0", "IB0", "Zc2", "R3",
    "Vm", "Zd3", "ZL1", "Vp", "ZL2", "Zc3", "R0", "RF", "ZL3",
)

def kernel(
    x_ref, g_ref, w_ref, wid_ref, dx_ref, dw_ref,
    xb, wb, gb, gin, wid, acc, hid, sd, qb, vp, vm, vp3, vm3, ap, am, rb, xr, own, out,
    dwp, dwr, dws, zvp, zvm, zap, zam, tot, ssem, rsem, lsem,
):
    dp, tensor = lax.axis_index("dp"), lax.axis_index("tensor")
    z, x = lax.div(dp, 4), lax.rem(dp, 4)
    y, c = lax.div(tensor, 2), lax.rem(tensor, 2)
    other = 1 - c

    def ring(v, step):
        return lax.rem(v + step, 4)

    def device(dz=0, dx=0, dy=0, dc=0):
        return (
            ring(z, dz) * 4 + ring(x, dx),
            ring(y, dy) * 2 + (other if dc else c),
        )

    sites = {}

    def send(name, src, dst, **to):
        slot = len(sites)
        copy = pltpu.make_async_remote_copy(
            src_ref=src,
            dst_ref=dst,
            send_sem=ssem.at[slot],
            recv_sem=rsem.at[slot],
            device_id=device(**to),
            device_id_type=MESH,
        )
        copy.start()
        sites[name] = copy

    taken = set()

    def arrived(*names):
        for name in names:
            if name not in taken:
                taken.add(name)
                sites[name].wait_recv()

    def place(j):
        return pl.ds(PLACE[j] * HALF, HALF)

    def chunk(dy, core):
        return ring(y, dy) * 2 + core

    def half_of(core):
        return pl.ds(pl.multiple_of(core * HALF, HALF), HALF)

    def weight_rows(dz, dx):
        return pl.ds(pl.multiple_of(SLOT[dz] * 768 + ring(x, dx) * ROWS, ROWS), ROWS)

    def weight_half(dz, dx, half):
        start = SLOT[dz] * 768 + ring(x, dx) * ROWS + half * 96
        return pl.ds(pl.multiple_of(start, 96), 96)

    def sub_block(step):
        return pl.ds(pl.multiple_of(ring(x, step) * COLS, COLS), COLS)

    own_cols = pl.ds(pl.multiple_of(c * COLS, COLS), COLS)

    own_w = pltpu.make_async_copy(
        w_ref.at[:, sub_block(0)], wb.at[weight_rows(0, 0), own_cols], lsem.at[2]
    )
    own_x = pltpu.make_async_copy(
        x_ref.at[half_of(c)], xb.at[chunk(0, c), place(0)], lsem.at[1]
    )
    own_g = pltpu.make_async_copy(g_ref, gin, lsem.at[0])
    own_wid = pltpu.make_async_copy(wid_ref, wid, lsem.at[3])
    own_wid.start()
    own_g.start()
    own_x.start()
    own_w.start()
    put_g = pltpu.make_async_copy(
        gin.at[half_of(c), sub_block(0)], gb.at[place(0), own_cols], lsem.at[0]
    )
    put_w = pltpu.make_async_copy(tot.at[3], dw_ref.at[:, sub_block(0)], lsem.at[1])
    put_x = pltpu.make_async_copy(out, dx_ref, lsem.at[2])

    partners = (
        dict(dx=1), dict(dx=3), dict(dx=2), dict(dy=1), dict(dy=3), dict(dz=1), dict(dz=3), dict(dc=1),
        dict(dx=1, dc=1), dict(dx=3, dc=1), dict(dx=2, dc=1), dict(dy=1, dc=1), dict(dy=3, dc=1),
    )
    barrier = pltpu.get_barrier_semaphore()
    for to in partners:
        pl.semaphore_signal(barrier, inc=1, device_id=device(**to), device_id_type=MESH)
    pl.semaphore_wait(barrier, len(partners))

    tasks = {}

    def task(name, *args):
        def enter(step):
            tasks[name] = lambda: step(*args)
            return step

        return enter

    def x_send(step, kind):
        core, dc = (c, 0) if kind == "s" else (other, 1)
        j = FROM[STEP.index(step)]
        dst = xb.at[chunk(0, c), place(STEP.index(j))]
        send(f"x{step}{kind}", x_ref.at[half_of(core)], dst, dx=step, dc=dc)

    def y_send(j, name, kind):
        dy = 1 if name == "yp" else 3
        if j == 0:
            core, dc = (c, 0) if kind == "s" else (other, 1)
            send(f"{name}0{kind}", x_ref.at[half_of(core)], xb.at[chunk(0, c), place(0)], dy=dy, dc=dc)
        else:
            ref = xb.at[chunk(0, c if kind == "s" else other), place(j)]
            send(f"{name}{j}{kind}", ref, ref, dy=dy)

    def x_arrive(j, kind):
        if j < 3:
            arrived(f"x{FROM[j]}{kind}")
        else:
            arrived("xf1" if kind == "s" else "xf3")
        if j == 2 and kind == "s":
            at = chunk(0, c)
            send("xf1", xb.at[at, place(2)], xb.at[at, place(3)], dx=1)
        if j == 1 and kind == "o":
            at = chunk(0, other)
            send("xf3", xb.at[at, place(1)], xb.at[at, place(3)], dx=3)
        for name in ("yp", "ym") if kind == "s" else ("ym", "yp"):
            y_send(j, name, kind)

    @task("xy3")
    def across_back():
        arrived("yfp0")
        at = chunk(2, c)
        send("xy3s", xb.at[at, place(0)], xb.at[at, place(1)], dx=3)

    @task("xy1")
    def across_on():
        arrived("yfm0")
        at = chunk(2, other)
        send("xy1o", xb.at[at, place(0)], xb.at[at, place(2)], dx=1)

    def y_forward_up(j):
        arrived(f"yp{j}s")
        ref = xb.at[chunk(3, c), place(j)]
        send(f"yfp{j}", ref, ref, dy=1)

    def y_forward_down(j):
        arrived(f"ym{j}o")
        ref = xb.at[chunk(1, other), place(j)]
        send(f"yfm{j}", ref, ref, dy=3)

    def w_send(step):
        dst = wb.at[weight_rows(0, 0), own_cols]
        send(f"w{step}", w_ref.at[:, sub_block(step)], dst, dx=step)

    def z_send(j, name, half):
        to = 1 if name == "zp" else 3
        src = wb.at[weight_half(0, STEP[j], half), own_cols]
        if j == 0:
            src = w_ref.at[pl.ds(half * 96, 96), sub_block(0)]
        dst = wb.at[weight_half(4 - to, STEP[j], half), own_cols]
        send(f"{name}{j}{'ab'[half]}", src, dst, dz=to)

    def w_arrive(j):
        arrived(f"w{FROM[j]}")
        z_send(j, "zp", 0)
        z_send(j, "zm", 1)
        z_send(j, "zp", 1)
        z_send(j, "zm", 0)
        w_pair(f"ws{j}", 0, j)

    def w_pair(name, dz, j):
        dst = wb.at[weight_rows(dz, STEP[j]), own_cols]
        src = w_ref.at[:, sub_block(0)] if name == "ws0" else dst
        send(name, src, dst, dc=1)

    def z_forward_up(j):
        arrived(f"zp{j}a")
        src = wb.at[weight_half(3, STEP[j], 0), own_cols]
        send(f"zfp{j}", src, wb.at[weight_half(2, STEP[j], 0), own_cols], dz=1)

    def z_forward_down(j):
        arrived(f"zm{j}b")
        src = wb.at[weight_half(1, STEP[j], 1), own_cols]
        send(f"zfm{j}", src, wb.at[weight_half(2, STEP[j], 1), own_cols], dz=3)

    def z_whole_up(j):
        arrived(f"zp{j}b")
        w_pair(f"d1{j}", 3, j)

    def z_whole_down(j):
        arrived(f"zm{j}a")
        w_pair(f"d3{j}", 1, j)

    def z_across(j):
        arrived(f"zfp{j}", f"zfm{j}")
        w_pair(f"d2{j}", 2, j)

    @task("w2s")
    def w_across():
        w_send(2)

    @task("wr1")
    def weights_near():
        own_w.wait()
        for j in range(4):
            arrived(f"ws{j}", f"d1{j}", f"d3{j}")

    @task("wr2")
    def weights_across():
        for j in range(4):
            arrived(f"d2{j}")

    def g_send(step, kind):
        core, dc = (c, 0) if kind == "s" else (other, 1)
        j = FROM[STEP.index(step)]
        dst = gb.at[place(STEP.index(j)), own_cols]
        send(f"g{step}{kind}", gin.at[half_of(core), sub_block(step)], dst, dx=step, dc=dc)

    @task("mask")
    def mask():
        own_wid.wait()
        own_g.wait()
        for half in range(2):
            rows = pl.ds(half * 128, 128)
            width = jnp.broadcast_to(wid[half : half + 1, :], (128, 128)).T
            keep = jnp.where(width > tensor, 1.0, 0.0).astype(BF16)
            for part in range(HID // 128):
                lanes = pl.ds(part * 128, 128)
                gin[rows, lanes] = gin[rows, lanes] * keep
        put_g.start()
        send("gs", gin.at[half_of(other), sub_block(0)], gb.at[place(0), own_cols], dc=1)

    @task("g13")
    def g_near():
        g_send(1, "s")
        g_send(3, "s")
        g_send(1, "o")
        g_send(3, "o")

    @task("g2")
    def g_across():
        g_send(2, "s")
        g_send(2, "o")

    for j in range(4):
        if j:
            task(f"xa{j}", j, "s")(x_arrive)
            task(f"xb{j}", j, "o")(x_arrive)
            task(f"wa{j}", j)(w_arrive)
        task(f"yfp{j}", j)(y_forward_up)
        task(f"yfm{j}", j)(y_forward_down)
        task(f"zfp{j}", j)(z_forward_up)
        task(f"zfm{j}", j)(z_forward_down)
        task(f"zdp{j}", j)(z_whole_up)
        task(f"zdm{j}", j)(z_whole_down)
        task(f"zl{j}", j)(z_across)

    def features(dz, rows):
        return [xb[ring(z, dz) * 2 + h, rows, :] for h in range(2)]

    def batch(places):
        return pl.ds(PLACE[places[0]] * HALF, HALF * len(places))

    def hidden_near(*places):
        for j in places:
            arrived(f"yp{j}o", f"ym{j}s")
            if j == 1:
                arrived("yp1s", "xy3s")
            else:
                arrived(f"yfp{j}")
            if j == 2:
                arrived("ym2o", "xy1o")
            else:
                arrived(f"yfm{j}")
            if j == 0:
                own_x.wait()
                arrived("xs")
        rows = batch(places)
        part = jnp.concatenate(features(0, rows) + features(1, rows) + features(3, rows), axis=1)
        acc[rows, :] = jnp.dot(part, wb[pl.ds(0, 2304), :], preferred_element_type=F32)

    def hidden_last(*places):
        for j in places:
            if j == 0:
                put_g.wait()
                arrived("gs")
            else:
                arrived(f"g{FROM[j]}s", f"g{FROM[j]}o")
        rows = batch(places)
        part = jnp.concatenate(features(2, rows), axis=1)
        preact = acc[rows, :] + jnp.dot(part, wb[pl.ds(2304, 768), :], preferred_element_type=F32)
        slope = 2.0 * jnp.maximum(preact, 0.0)
        hid[rows, :] = (gb[rows, :].astype(F32) * slope).astype(BF16)

    for name, places in (("A", (1, 2)), ("0", (0,)), ("3", (3,))):
        task("Pa" + name, *places)(hidden_near)
        task("Pb" + name, *places)(hidden_last)

    first, second = pl.ds(0, 128), pl.ds(128, 128)
    upper, lower = pl.ds(0, 64), pl.ds(64, 64)
    upper3, lower3 = pl.ds(128, 64), pl.ds(192, 64)

    def input_part(b, d):
        dz = lax.rem(y + d - z + 4, 4)
        slot = dz + lax.div(dz, 2) - 2 * lax.div(dz, 3)
        rows = pl.ds(pl.multiple_of(slot * 768, 768), 768)
        sd[b, d] = lax.dot_general(
            hid[pl.ds(b * 256, 256), :], wb[rows, :], (((1,), (1,)), ((), ())), preferred_element_type=F32
        ).astype(BF16)
        if d == 2 and b == 0:
            send("q1", sd.at[0, 2, first], qb.at[0], dx=1)
            send("q3", sd.at[0, 2, second], qb.at[1], dx=3)
        elif d == 2:
            send("vp3", sd.at[1, 2, upper3], vp3, dy=1)
            send("vm3", sd.at[1, 2, lower3], vm3, dy=3)
        elif d == 1 and b == 0:
            send("a11", sd.at[0, 1, first], ap.at[0], dy=1)
            send("a12", sd.at[0, 1, second], ap.at[1], dy=1)
        elif d == 3 and b == 0:
            send("a31", sd.at[0, 3, first], am.at[0], dy=3)
            send("a32", sd.at[0, 3, second], am.at[1], dy=3)
        elif d == 1:
            send("a13l", sd.at[1, 1, lower3], ap.at[3, lower], dy=1)
            send("a10l", sd.at[1, 1, lower], ap.at[2, lower], dy=1)
        elif d == 3:
            send("a33t", sd.at[1, 3, upper3], am.at[3, upper], dy=3)
            send("a30t", sd.at[1, 3, upper], am.at[2, upper], dy=3)

    for b in range(2):
        for d in range(4):
            task(f"I{'AB'[b]}{d}", b, d)(input_part)

    @task("S0")
    def across_total():
        arrived("q1", "q3")
        total = sd[1, 2, first].astype(F32)
        for slot in range(2):
            total = total + qb[slot].astype(F32)
        sd[1, 2, first] = total.astype(BF16)
        send("vp", sd.at[1, 2, upper], vp, dy=1)
        send("vm", sd.at[1, 2, lower], vm, dy=3)

    def via_up(name, came, rows, to, at):
        arrived(name)
        sd[1, 1, rows] = (sd[1, 1, rows].astype(F32) + came[...].astype(F32)).astype(BF16)
        send(to, sd.at[1, 1, rows], ap.at[at, upper], dy=1)

    def via_down(name, came, rows, to, at):
        arrived(name)
        sd[1, 3, rows] = (sd[1, 3, rows].astype(F32) + came[...].astype(F32)).astype(BF16)
        send(to, sd.at[1, 3, rows], am.at[at, lower], dy=3)

    task("Vp", "vp", vp, upper, "a10t", 2)(via_up)
    task("Vm", "vm", vm, lower, "a30l", 2)(via_down)
    task("V3p", "vp3", vp3, upper3, "a13t", 3)(via_up)
    task("V3m", "vm3", vm3, lower3, "a33l", 3)(via_down)

    def input_total(j):
        if j in (0, 3):
            arrived(f"a1{j}l", f"a1{j}t", f"a3{j}t", f"a3{j}l")
        else:
            arrived(f"a1{j}", f"a3{j}")
        at, rows = PLACE[j], (first, second)[PLACE[j] % 2]
        total = sd[at // 2, 0, rows].astype(F32) + ap[at].astype(F32) + am[at].astype(F32)
        total = total.astype(BF16)
        rb[at, 0] = total[:, :COLS]
        rb[at, 1] = total[:, COLS:]
        if j == 0:
            own[c] = rb[at, c]
            send("xro", rb.at[at, other], own.at[c], dc=1)
        else:
            step = STEP[j]
            send(f"xr{step}s", rb.at[at, c], xr.at[step - 1, c], dx=step)
            send(f"xr{step}o", rb.at[at, other], xr.at[step - 1, c], dx=step, dc=1)

    for j in range(4):
        task(f"R{j}", j)(input_total)

    @task("RF")
    def input_final():
        arrived("xr1s", "xr1o", "xr3s", "xr3o", "xr2s", "xr2o", "xro")
        for half in range(2):
            total = own[half].astype(F32)
            for slot in range(3):
                total = total + xr[slot, half].astype(F32)
            out[pl.ds(half * HALF, HALF), :] = total.astype(BF16)
        put_x.start()

    def weight_part(d, h):
        part = lax.dot_general(
            xb[ring(z, d) * 2 + h], hid[...], (((0,), (0,)), ((), ())), preferred_element_type=F32
        ).astype(BF16)
        dwp[d, h, 0] = part[:, :COLS]
        dwp[d, h, 1] = part[:, COLS:]
        send(f"e{d}{h}", dwp.at[d, h, other], dwr.at[d, h], dc=1)

    def weight_pair(d, h):
        arrived(f"e{d}{h}")
        total = (dwp[d, h, c].astype(F32) + dwr[d, h].astype(F32)).astype(BF16)
        for p in range(2):
            step = lax.rem(h * 2 + p - x + 4, 4)
            at = lax.rem(lax.rem(3 * step + 3, 5), 4)
            rows = pl.ds(pl.multiple_of(at * 96, 96), 96)
            dws[d, 0, rows] = total[p * ROWS : p * ROWS + 96]
            dws[d, 1, rows] = total[p * ROWS + 96 : p * ROWS + ROWS]
            if d == 2:
                via_copy("zvp", at, rows).start()
                via_copy("zvm", at, rows).start()

    for d in range(4):
        for h in range(2):
            task(f"D{d}{h}", d, h)(weight_part)
            task(f"E{d}{h}", d, h)(weight_pair)

    def sub_rows(q):
        return pl.ds(q * 96, 96)

    via_slots = {}

    def via_copy(name, at, rows):
        up = name == "zvp"
        return pltpu.make_async_remote_copy(
            src_ref=dws.at[2, 0 if up else 1, rows],
            dst_ref=(zvp if up else zvm).at[rows],
            send_sem=ssem.at[via_slots[name] + at],
            recv_sem=rsem.at[via_slots[name] + at],
            device_id=device(dz=1 if up else 3),
            device_id_type=MESH,
        )

    for name in ("zvp", "zvm"):
        via_slots[name] = len(sites)
        for q in range(4):
            sites[f"{name}{q}"] = via_copy(name, q, sub_rows(q))

    def weight_direct(q):
        rows = sub_rows(q)
        send(f"zdp{q}", dws.at[1, 1, rows], zap.at[1, rows], dz=1)
        send(f"zdm{q}", dws.at[3, 0, rows], zam.at[0, rows], dz=3)

    def weight_via(q):
        arrived(f"zvp{q}", f"zvm{q}")
        rows = sub_rows(q)
        dws[1, 0, rows] = (dws[1, 0, rows].astype(F32) + zvp[rows].astype(F32)).astype(BF16)
        send(f"zcp{q}", dws.at[1, 0, rows], zap.at[0, rows], dz=1)
        dws[3, 1, rows] = (dws[3, 1, rows].astype(F32) + zvm[rows].astype(F32)).astype(BF16)
        send(f"zcm{q}", dws.at[3, 1, rows], zam.at[1, rows], dz=3)

    def weight_last(q):
        arrived(f"zdp{q}", f"zdm{q}", f"zcp{q}", f"zcm{q}")
        rows = sub_rows(q)
        for half in range(2):
            total = (
                dws[0, half, rows].astype(F32) + zap[half, rows].astype(F32) + zam[half, rows].astype(F32)
            )
            tot[q, pl.ds(half * 96, 96)] = (total * SCALE).astype(BF16)
        if q < 3:
            send(f"t{q}", tot.at[q], dw_ref.at[:, sub_block(0)], dx=SUB[q])
        else:
            put_w.start()

    for q in range(4):
        task(f"Zd{q}", q)(weight_direct)
        task(f"Zc{q}", q)(weight_via)
        task(f"ZL{q}", q)(weight_last)

    left = []

    @task("sent")
    def early_sends():
        for name in left:
            sites[name].wait_send()

    x_send(1, "s")
    x_send(3, "o")
    w_send(1)
    w_send(3)
    x_send(1, "o")
    x_send(3, "s")
    y_send(0, "yp", "s")
    y_send(0, "ym", "o")
    z_send(0, "zp", 0)
    z_send(0, "zm", 1)
    y_send(0, "yp", "o")
    y_send(0, "ym", "s")
    z_send(0, "zp", 1)
    z_send(0, "zm", 0)
    w_pair("ws0", 0, 0)
    send("xs", x_ref.at[half_of(other)], xb.at[chunk(0, c), place(0)], dc=1)
    for name in ORDER:
        if name == "PbA":
            left.extend(n for n in sites if n[:2] != "zv")
        tasks[name]()
    for name, copy in sites.items():
        if name not in left:
            copy.wait_send()
    arrived("t0", "t1", "t2")
    put_w.wait()
    put_x.wait()


def hand_on(a_ref, b_ref, a_out, b_out, a_buf, b_buf, sems):
    parts = [(b_ref.at[pl.ds(k * 96, 96)], b_buf.at[pl.ds(k * 96, 96)], b_out.at[pl.ds(k * 96, 96)]) for k in range(2)]
    parts.append((a_ref, a_buf, a_out))
    loads = [pltpu.make_async_copy(src, buf, sems.at[0, k]) for k, (src, buf, _) in enumerate(parts)]
    stores = [pltpu.make_async_copy(buf, dst, sems.at[1, k]) for k, (_, buf, dst) in enumerate(parts)]
    for copy in loads:
        copy.start()
    for load, store in zip(loads, stores):
        load.wait()
        store.start()
    for copy in stores:
        copy.wait()


def shards(activations, act_grad, up_weight, width_steps):
    any_space = pl.BlockSpec(memory_space=pl.ANY)

    def buffer(*shape):
        return pltpu.VMEM(shape, BF16)

    results = (
        jax.ShapeDtypeStruct((TOK, COLS), BF16),
        jax.ShapeDtypeStruct((ROWS, HID), BF16),
    )
    input_grad, weight_grad = pl.pallas_call(
        kernel,
        out_shape=results,
        in_specs=[any_space] * 4,
        out_specs=(any_space, any_space),
        scratch_shapes=[
            buffer(8, 4 * HALF, COLS),
            buffer(16 * ROWS, 2 * COLS),
            buffer(4 * HALF, 2 * COLS),
            buffer(TOK, HID),
            pltpu.VMEM((2, 128), jnp.int32),
            pltpu.VMEM((4 * HALF, 2 * COLS), F32),
            buffer(4 * HALF, 2 * COLS),
            buffer(2, 4, 2 * HALF, 2 * COLS),
            buffer(2, HALF, 2 * COLS),
            buffer(64, 2 * COLS),
            buffer(64, 2 * COLS),
            buffer(64, 2 * COLS),
            buffer(64, 2 * COLS),
            buffer(4, HALF, 2 * COLS),
            buffer(4, HALF, 2 * COLS),
            buffer(4, 2, HALF, COLS),
            buffer(3, 2, HALF, COLS),
            buffer(2, HALF, COLS),
            buffer(TOK, COLS),
            buffer(4, 2, 2, 384, COLS),
            buffer(4, 2, 384, COLS),
            buffer(4, 2, 384, COLS),
            buffer(384, COLS),
            buffer(384, COLS),
            buffer(2, 384, COLS),
            buffer(2, 384, COLS),
            buffer(4, ROWS, COLS),
            pltpu.SemaphoreType.DMA((N_SEM,)),
            pltpu.SemaphoreType.DMA((N_SEM,)),
            pltpu.SemaphoreType.DMA((4,)),
        ],
        compiler_params=pltpu.CompilerParams(
            collective_id=0, has_side_effects=True, vmem_limit_bytes=60 * 2**20
        ),
        cost_estimate=pl.CostEstimate(
            flops=3 * 2 * 512 * 3072 * 768, bytes_accessed=4 * 2**20, transcendentals=0
        ),
        name="elastic_up_backward",
    )(activations, act_grad, up_weight, width_steps.reshape(2, 128))
    return pl.pallas_call(
        hand_on,
        out_shape=results,
        in_specs=[any_space] * 2,
        out_specs=(any_space, any_space),
        scratch_shapes=[buffer(TOK, COLS), buffer(ROWS, HID), pltpu.SemaphoreType.DMA((2, 3))],
        compiler_params=pltpu.CompilerParams(vmem_limit_bytes=60 * 2**20),
        name="hand_on",
    )(input_grad, weight_grad)


def solution(mesh):
    placed = (P("dp", "tensor"), P("dp", "tensor"), P("dp", "tensor"), P("dp"))
    return jax.shard_map(
        shards,
        mesh=mesh,
        in_specs=placed,
        out_specs=(P("dp", "tensor"), P("dp", "tensor")),
        check_vma=False,
    )
```

```python
import jax
import jax.numpy as jnp
from jax import lax
from jax.experimental import pallas as pl
from jax.experimental.pallas import tpu as pltpu
from jax.sharding import PartitionSpec as P

MESH = pl.DeviceIdType.MESH
F32 = jnp.float32
BF16 = jnp.bfloat16
TOK = 256
HALF = 128
ROWS = 192
COLS = 384
HID = 1536
SCALE = 1.0 / 64.0
N_SEM = 176

STEP = (0, 1, 3, 2)
FROM = (0, 3, 1, 2)
PLACE = (2, 0, 1, 3)
SLOT = (0, 1, 3, 2)
SUB = (2, 1, 3, 0)

ORDER = (
    "mask", "wa2", "zfp0", "yfp0", "yfm0", "xa2", "zfm0", "xb1", "wb2", "wa1", "w2s", "g13", "xb2", "zdp0",
    "xa1", "wb1", "zfm2", "zfp2", "wa3", "zdm0", "zdp2", "xb3", "zl0", "yfm1", "xy1", "wb3", "xa3", "yfp2",
    "zfp1", "xy3", "zdm2", "zfm1", "zfp3", "zfm3", "zl2", "zdp1", "zdm1", "zdm3", "yfm3", "zdp3", "g2",
    "yfp3", "wr1", "zl1", "Pa0", "zl3", "PaA", "wr2", "PbA", "IA1", "IA3", "Pa3", "Pb0", "Pb3", "D20", "IB2",
    "IA2", "IA0", "D21", "E20", "D10", "IB3", "IB1", "D30", "E21", "D31", "D11", "E10", "R1", "E30", "D00",
    "D01", "E31", "E11", "Zc1", "R2", "Zd0", "Zc0", "Zc2", "E00", "Zd1", "Zd2", "Zd3", "IB0", "sent", "E01",
    "S0", "Zc3", "R3", "ZL0", "Vp", "Vm", "ZL1", "ZL2", "R0", "ZL3", "RF",
)

def kernel(
    x_ref, g_ref, w_ref, wid_ref, dx_ref, dw_ref,
    xb, wb, gb, gin, wid, acc, hid, sd, qb, vp, vm, ap, am, rb, xr, own, out,
    dwp, dwr, dws, zvp, zvm, zap, zam, tot, ssem, rsem, lsem,
):
    dp, tensor = lax.axis_index("dp"), lax.axis_index("tensor")
    z, x = lax.div(dp, 4), lax.rem(dp, 4)
    y, c = lax.div(tensor, 2), lax.rem(tensor, 2)
    other = 1 - c

    def ring(v, step):
        return lax.rem(v + step, 4)

    def device(dz=0, dx=0, dy=0, dc=0):
        return (
            ring(z, dz) * 4 + ring(x, dx),
            ring(y, dy) * 2 + (other if dc else c),
        )

    sites = {}

    def send(name, src, dst, **to):
        slot = len(sites)
        copy = pltpu.make_async_remote_copy(
            src_ref=src,
            dst_ref=dst,
            send_sem=ssem.at[slot],
            recv_sem=rsem.at[slot],
            device_id=device(**to),
            device_id_type=MESH,
        )
        copy.start()
        sites[name] = copy

    taken = set()

    def arrived(*names):
        for name in names:
            if name not in taken:
                taken.add(name)
                sites[name].wait_recv()

    def place(j):
        return pl.ds(PLACE[j] * HALF, HALF)

    def chunk(dy, core):
        return ring(y, dy) * 2 + core

    def half_of(core):
        return pl.ds(pl.multiple_of(core * HALF, HALF), HALF)

    def weight_rows(dz, dx):
        return pl.ds(pl.multiple_of(SLOT[dz] * 768 + ring(x, dx) * ROWS, ROWS), ROWS)

    def weight_half(dz, dx, half):
        start = SLOT[dz] * 768 + ring(x, dx) * ROWS + half * 96
        return pl.ds(pl.multiple_of(start, 96), 96)

    def sub_block(step):
        return pl.ds(pl.multiple_of(ring(x, step) * COLS, COLS), COLS)

    own_cols = pl.ds(pl.multiple_of(c * COLS, COLS), COLS)

    own_w = pltpu.make_async_copy(
        w_ref.at[:, sub_block(0)], wb.at[weight_rows(0, 0), own_cols], lsem.at[2]
    )
    own_x = pltpu.make_async_copy(
        x_ref.at[half_of(c)], xb.at[chunk(0, c), place(0)], lsem.at[1]
    )
    own_g = pltpu.make_async_copy(g_ref, gin, lsem.at[0])
    own_wid = pltpu.make_async_copy(wid_ref, wid, lsem.at[3])
    put_g = pltpu.make_async_copy(
        gin.at[half_of(c), sub_block(0)], gb.at[place(0), own_cols], lsem.at[0]
    )
    put_w = pltpu.make_async_copy(tot.at[3], dw_ref.at[:, sub_block(0)], lsem.at[1])
    put_x = pltpu.make_async_copy(out, dx_ref, lsem.at[2])

    partners = (
        dict(dx=1), dict(dx=3), dict(dx=2), dict(dy=1), dict(dy=3), dict(dz=1), dict(dz=3), dict(dc=1),
        dict(dx=1, dc=1), dict(dx=3, dc=1), dict(dx=2, dc=1), dict(dy=1, dc=1), dict(dy=3, dc=1),
    )
    barrier = pltpu.get_barrier_semaphore()
    for to in partners:
        pl.semaphore_signal(barrier, inc=1, device_id=device(**to), device_id_type=MESH)
    own_wid.start()
    own_g.start()
    own_x.start()
    own_w.start()
    pl.semaphore_wait(barrier, len(partners))

    tasks = {}

    def task(name, *args):
        def enter(step):
            tasks[name] = lambda: step(*args)
            return step

        return enter

    def x_send(step, kind):
        core, dc = (c, 0) if kind == "s" else (other, 1)
        j = FROM[STEP.index(step)]
        dst = xb.at[chunk(0, c), place(STEP.index(j))]
        send(f"x{step}{kind}", x_ref.at[half_of(core)], dst, dx=step, dc=dc)

    def y_send(j, name, kind):
        dy = 1 if name == "yp" else 3
        if j == 0:
            core, dc = (c, 0) if kind == "s" else (other, 1)
            send(f"{name}0{kind}", x_ref.at[half_of(core)], xb.at[chunk(0, c), place(0)], dy=dy, dc=dc)
        else:
            ref = xb.at[chunk(0, c if kind == "s" else other), place(j)]
            send(f"{name}{j}{kind}", ref, ref, dy=dy)

    def x_arrive(j, kind):
        if j < 3:
            arrived(f"x{FROM[j]}{kind}")
        else:
            arrived("xf1" if kind == "s" else "xf3")
        if j == 2 and kind == "s":
            at = chunk(0, c)
            send("xf1", xb.at[at, place(2)], xb.at[at, place(3)], dx=1)
        if j == 1 and kind == "o":
            at = chunk(0, other)
            send("xf3", xb.at[at, place(1)], xb.at[at, place(3)], dx=3)
        for name in ("yp", "ym") if kind == "s" else ("ym", "yp"):
            y_send(j, name, kind)

    @task("xy3")
    def across_back():
        arrived("yfp0")
        at = chunk(2, c)
        send("xy3s", xb.at[at, place(0)], xb.at[at, place(1)], dx=3)

    @task("xy1")
    def across_on():
        arrived("yfm0")
        at = chunk(2, other)
        send("xy1o", xb.at[at, place(0)], xb.at[at, place(2)], dx=1)

    def y_forward_up(j):
        arrived(f"yp{j}s")
        ref = xb.at[chunk(3, c), place(j)]
        send(f"yfp{j}", ref, ref, dy=1)

    def y_forward_down(j):
        arrived(f"ym{j}o")
        ref = xb.at[chunk(1, other), place(j)]
        send(f"yfm{j}", ref, ref, dy=3)

    def w_send(step, half):
        src = w_ref.at[pl.ds(half * 96, 96), sub_block(step)]
        dst = wb.at[weight_half(0, 0, half), own_cols]
        send(f"w{step}{'ab'[half]}", src, dst, dx=step)

    def z_send(j, name, half):
        to = 1 if name == "zp" else 3
        src = wb.at[weight_half(0, STEP[j], half), own_cols]
        if j == 0:
            src = w_ref.at[pl.ds(half * 96, 96), sub_block(0)]
        dst = wb.at[weight_half(4 - to, STEP[j], half), own_cols]
        send(f"{name}{j}{'ab'[half]}", src, dst, dz=to)

    def w_arrive(j, half):
        arrived(f"w{FROM[j]}{'ab'[half]}")
        for name in ("zm", "zp") if half else ("zp", "zm"):
            z_send(j, name, half)
        ref = wb.at[weight_half(0, STEP[j], half), own_cols]
        send(f"ws{'ab'[half]}{j}", ref, ref, dc=1)

    def w_pair(name, dz, j):
        dst = wb.at[weight_rows(dz, STEP[j]), own_cols]
        src = w_ref.at[:, sub_block(0)] if name == "ws0" else dst
        send(name, src, dst, dc=1)

    def z_forward_up(j):
        arrived(f"zp{j}a")
        src = wb.at[weight_half(3, STEP[j], 0), own_cols]
        send(f"zfp{j}", src, wb.at[weight_half(2, STEP[j], 0), own_cols], dz=1)

    def z_forward_down(j):
        arrived(f"zm{j}b")
        src = wb.at[weight_half(1, STEP[j], 1), own_cols]
        send(f"zfm{j}", src, wb.at[weight_half(2, STEP[j], 1), own_cols], dz=3)

    def z_whole_up(j):
        arrived(f"zp{j}b")
        w_pair(f"d1{j}", 3, j)

    def z_whole_down(j):
        arrived(f"zm{j}a")
        w_pair(f"d3{j}", 1, j)

    def z_across(j):
        arrived(f"zfp{j}", f"zfm{j}")
        w_pair(f"d2{j}", 2, j)

    @task("w2s")
    def w_across():
        w_send(2, 0)
        w_send(2, 1)

    @task("wr1")
    def weights_near():
        own_w.wait()
        for j in range(4):
            arrived(f"d1{j}", f"d3{j}")
            arrived(*((f"wsa{j}", f"wsb{j}") if j else ("ws0",)))

    @task("wr2")
    def weights_across():
        for j in range(4):
            arrived(f"d2{j}")

    def g_send(step, kind):
        core, dc = (c, 0) if kind == "s" else (other, 1)
        j = FROM[STEP.index(step)]
        dst = gb.at[place(STEP.index(j)), own_cols]
        send(f"g{step}{kind}", gin.at[half_of(core), sub_block(step)], dst, dx=step, dc=dc)

    @task("mask")
    def mask():
        own_wid.wait()
        own_g.wait()
        for half in range(2):
            rows = pl.ds(half * 128, 128)
            width = jnp.broadcast_to(wid[half : half + 1, :], (128, 128)).T
            keep = jnp.where(width > tensor, 1.0, 0.0).astype(BF16)
            for part in range(HID // 128):
                lanes = pl.ds(part * 128, 128)
                gin[rows, lanes] = gin[rows, lanes] * keep
        put_g.start()
        send("gs", gin.at[half_of(other), sub_block(0)], gb.at[place(0), own_cols], dc=1)

    @task("g13")
    def g_near():
        g_send(1, "s")
        g_send(3, "s")
        g_send(1, "o")
        g_send(3, "o")

    @task("g2")
    def g_across():
        g_send(2, "s")
        g_send(2, "o")

    for j in range(4):
        if j:
            task(f"xa{j}", j, "s")(x_arrive)
            task(f"xb{j}", j, "o")(x_arrive)
            task(f"wa{j}", j, 0)(w_arrive)
            task(f"wb{j}", j, 1)(w_arrive)
        task(f"yfp{j}", j)(y_forward_up)
        task(f"yfm{j}", j)(y_forward_down)
        task(f"zfp{j}", j)(z_forward_up)
        task(f"zfm{j}", j)(z_forward_down)
        task(f"zdp{j}", j)(z_whole_up)
        task(f"zdm{j}", j)(z_whole_down)
        task(f"zl{j}", j)(z_across)

    def features(dz, rows):
        return [xb[ring(z, dz) * 2 + h, rows, :] for h in range(2)]

    def batch(places):
        return pl.ds(PLACE[places[0]] * HALF, HALF * len(places))

    def hidden_near(*places):
        for j in places:
            arrived(f"yp{j}o", f"ym{j}s")
            if j == 1:
                arrived("yp1s", "xy3s")
            else:
                arrived(f"yfp{j}")
            if j == 2:
                arrived("ym2o", "xy1o")
            else:
                arrived(f"yfm{j}")
            if j == 0:
                own_x.wait()
                arrived("xs")
        rows = batch(places)
        part = jnp.concatenate(features(0, rows) + features(1, rows) + features(3, rows), axis=1)
        acc[rows, :] = jnp.dot(part, wb[pl.ds(0, 2304), :], preferred_element_type=F32)

    def hidden_last(*places):
        for j in places:
            if j == 0:
                put_g.wait()
                arrived("gs")
            else:
                arrived(f"g{FROM[j]}s", f"g{FROM[j]}o")
        rows = batch(places)
        part = jnp.concatenate(features(2, rows), axis=1)
        preact = acc[rows, :] + jnp.dot(part, wb[pl.ds(2304, 768), :], preferred_element_type=F32)
        slope = 2.0 * jnp.maximum(preact, 0.0)
        hid[rows, :] = (gb[rows, :].astype(F32) * slope).astype(BF16)

    for name, places in (("A", (1, 2)), ("0", (0,)), ("3", (3,))):
        task("Pa" + name, *places)(hidden_near)
        task("Pb" + name, *places)(hidden_last)

    first, second = pl.ds(0, 128), pl.ds(128, 128)
    upper, lower = pl.ds(0, 64), pl.ds(64, 64)

    def input_part(b, d):
        dz = lax.rem(y + d - z + 4, 4)
        slot = dz + lax.div(dz, 2) - 2 * lax.div(dz, 3)
        rows = pl.ds(pl.multiple_of(slot * 768, 768), 768)
        sd[b, d] = lax.dot_general(
            hid[pl.ds(b * 256, 256), :], wb[rows, :], (((1,), (1,)), ((), ())), preferred_element_type=F32
        ).astype(BF16)
        if d == 2 and b == 0:
            send("q1", sd.at[0, 2, first], qb.at[0], dx=1)
            send("q3", sd.at[0, 2, second], qb.at[1], dx=3)
        elif d == 2:
            send("q2", sd.at[1, 2, second], qb.at[2], dx=2)
        elif d == 1 and b == 0:
            send("a11", sd.at[0, 1, first], ap.at[0], dy=1)
            send("a12", sd.at[0, 1, second], ap.at[1], dy=1)
        elif d == 3 and b == 0:
            send("a31", sd.at[0, 3, first], am.at[0], dy=3)
            send("a32", sd.at[0, 3, second], am.at[1], dy=3)
        elif d == 1:
            send("a13", sd.at[1, 1, second], ap.at[3], dy=1)
            send("a10l", sd.at[1, 1, lower], ap.at[2, lower], dy=1)
        elif d == 3:
            send("a33", sd.at[1, 3, second], am.at[3], dy=3)
            send("a30t", sd.at[1, 3, upper], am.at[2, upper], dy=3)

    for b in range(2):
        for d in range(4):
            task(f"I{'AB'[b]}{d}", b, d)(input_part)

    @task("S0")
    def across_total():
        arrived("q1", "q3", "q2")
        total = sd[1, 2, first].astype(F32)
        for slot in range(3):
            total = total + qb[slot].astype(F32)
        sd[1, 2, first] = total.astype(BF16)
        send("vp", sd.at[1, 2, upper], vp, dy=1)
        send("vm", sd.at[1, 2, lower], vm, dy=3)

    @task("Vp")
    def via_up():
        arrived("vp")
        sd[1, 1, upper] = (sd[1, 1, upper].astype(F32) + vp[...].astype(F32)).astype(BF16)
        send("a10t", sd.at[1, 1, upper], ap.at[2, upper], dy=1)

    @task("Vm")
    def via_down():
        arrived("vm")
        sd[1, 3, lower] = (sd[1, 3, lower].astype(F32) + vm[...].astype(F32)).astype(BF16)
        send("a30l", sd.at[1, 3, lower], am.at[2, lower], dy=3)

    def input_total(j):
        if j == 0:
            arrived("a10l", "a10t", "a30t", "a30l")
        else:
            arrived(f"a1{j}", f"a3{j}")
        at, rows = PLACE[j], (first, second)[PLACE[j] % 2]
        total = sd[at // 2, 0, rows].astype(F32) + ap[at].astype(F32) + am[at].astype(F32)
        total = total.astype(BF16)
        rb[at, 0] = total[:, :COLS]
        rb[at, 1] = total[:, COLS:]
        if j == 0:
            own[c] = rb[at, c]
            send("xro", rb.at[at, other], own.at[c], dc=1)
        else:
            step = STEP[j]
            send(f"xr{step}s", rb.at[at, c], xr.at[step - 1, c], dx=step)
            send(f"xr{step}o", rb.at[at, other], xr.at[step - 1, c], dx=step, dc=1)

    for j in range(4):
        task(f"R{j}", j)(input_total)

    @task("RF")
    def input_final():
        arrived("xr1s", "xr1o", "xr3s", "xr3o", "xr2s", "xr2o", "xro")
        for half in range(2):
            total = own[half].astype(F32)
            for slot in range(3):
                total = total + xr[slot, half].astype(F32)
            out[pl.ds(half * HALF, HALF), :] = total.astype(BF16)
        put_x.start()

    def weight_part(d, h):
        part = lax.dot_general(
            xb[ring(z, d) * 2 + h], hid[...], (((0,), (0,)), ((), ())), preferred_element_type=F32
        ).astype(BF16)
        dwp[d, h, 0] = part[:, :COLS]
        dwp[d, h, 1] = part[:, COLS:]
        send(f"e{d}{h}", dwp.at[d, h, other], dwr.at[d, h], dc=1)

    def weight_pair(d, h):
        arrived(f"e{d}{h}")
        total = (dwp[d, h, c].astype(F32) + dwr[d, h].astype(F32)).astype(BF16)
        for p in range(2):
            step = lax.rem(h * 2 + p - x + 4, 4)
            at = lax.rem(lax.rem(3 * step + 3, 5), 4)
            rows = pl.ds(pl.multiple_of(at * 96, 96), 96)
            dws[d, 0, rows] = total[p * ROWS : p * ROWS + 96]
            dws[d, 1, rows] = total[p * ROWS + 96 : p * ROWS + ROWS]
            if d == 2:
                via_copy("zvp", at, rows).start()
                via_copy("zvm", at, rows).start()

    for d in range(4):
        for h in range(2):
            task(f"D{d}{h}", d, h)(weight_part)
            task(f"E{d}{h}", d, h)(weight_pair)

    def sub_rows(q):
        return pl.ds(q * 96, 96)

    via_slots = {}

    def via_copy(name, at, rows):
        up = name == "zvp"
        return pltpu.make_async_remote_copy(
            src_ref=dws.at[2, 0 if up else 1, rows],
            dst_ref=(zvp if up else zvm).at[rows],
            send_sem=ssem.at[via_slots[name] + at],
            recv_sem=rsem.at[via_slots[name] + at],
            device_id=device(dz=1 if up else 3),
            device_id_type=MESH,
        )

    for name in ("zvp", "zvm"):
        via_slots[name] = len(sites)
        for q in range(4):
            sites[f"{name}{q}"] = via_copy(name, q, sub_rows(q))

    def weight_direct(q):
        rows = sub_rows(q)
        send(f"zdp{q}", dws.at[1, 1, rows], zap.at[1, rows], dz=1)
        send(f"zdm{q}", dws.at[3, 0, rows], zam.at[0, rows], dz=3)

    def weight_via(q):
        arrived(f"zvp{q}", f"zvm{q}")
        rows = sub_rows(q)
        dws[1, 0, rows] = (dws[1, 0, rows].astype(F32) + zvp[rows].astype(F32)).astype(BF16)
        send(f"zcp{q}", dws.at[1, 0, rows], zap.at[0, rows], dz=1)
        dws[3, 1, rows] = (dws[3, 1, rows].astype(F32) + zvm[rows].astype(F32)).astype(BF16)
        send(f"zcm{q}", dws.at[3, 1, rows], zam.at[1, rows], dz=3)

    def weight_last(q):
        arrived(f"zdp{q}", f"zdm{q}", f"zcp{q}", f"zcm{q}")
        rows = sub_rows(q)
        for half in range(2):
            total = (
                dws[0, half, rows].astype(F32) + zap[half, rows].astype(F32) + zam[half, rows].astype(F32)
            )
            tot[q, pl.ds(half * 96, 96)] = (total * SCALE).astype(BF16)
        if q < 3:
            send(f"t{q}", tot.at[q], dw_ref.at[:, sub_block(0)], dx=SUB[q])
        else:
            put_w.start()

    for q in range(4):
        task(f"Zd{q}", q)(weight_direct)
        task(f"Zc{q}", q)(weight_via)
        task(f"ZL{q}", q)(weight_last)

    left = []

    @task("sent")
    def early_sends():
        for name in left:
            sites[name].wait_send()

    w_send(1, 0)
    w_send(3, 1)
    x_send(1, "s")
    x_send(3, "o")
    w_send(1, 1)
    w_send(3, 0)
    x_send(1, "o")
    x_send(3, "s")
    y_send(0, "yp", "s")
    y_send(0, "ym", "o")
    z_send(0, "zp", 0)
    z_send(0, "zm", 1)
    y_send(0, "yp", "o")
    y_send(0, "ym", "s")
    z_send(0, "zp", 1)
    z_send(0, "zm", 0)
    w_pair("ws0", 0, 0)
    send("xs", x_ref.at[half_of(other)], xb.at[chunk(0, c), place(0)], dc=1)
    for name in ORDER:
        if name == "PbA":
            left.extend(n for n in sites if n[:2] != "zv")
        tasks[name]()
    for name, copy in sites.items():
        if name not in left:
            copy.wait_send()
    arrived("t0", "t1", "t2")
    put_w.wait()
    put_x.wait()


def hand_on(a_ref, b_ref, a_out, b_out, a_buf, b_buf, sems):
    parts = [(b_ref.at[pl.ds(k * 96, 96)], b_buf.at[pl.ds(k * 96, 96)], b_out.at[pl.ds(k * 96, 96)]) for k in range(2)]
    parts.append((a_ref, a_buf, a_out))
    loads = [pltpu.make_async_copy(src, buf, sems.at[0, k]) for k, (src, buf, _) in enumerate(parts)]
    stores = [pltpu.make_async_copy(buf, dst, sems.at[1, k]) for k, (_, buf, dst) in enumerate(parts)]
    for copy in loads:
        copy.start()
    for load, store in zip(loads, stores):
        load.wait()
        store.start()
    for copy in stores:
        copy.wait()


def shards(activations, act_grad, up_weight, width_steps):
    any_space = pl.BlockSpec(memory_space=pl.ANY)

    def buffer(*shape):
        return pltpu.VMEM(shape, BF16)

    results = (
        jax.ShapeDtypeStruct((TOK, COLS), BF16),
        jax.ShapeDtypeStruct((ROWS, HID), BF16),
    )
    input_grad, weight_grad = pl.pallas_call(
        kernel,
        out_shape=results,
        in_specs=[any_space] * 4,
        out_specs=(any_space, any_space),
        scratch_shapes=[
            buffer(8, 4 * HALF, COLS),
            buffer(16 * ROWS, 2 * COLS),
            buffer(4 * HALF, 2 * COLS),
            buffer(TOK, HID),
            pltpu.VMEM((2, 128), jnp.int32),
            pltpu.VMEM((4 * HALF, 2 * COLS), F32),
            buffer(4 * HALF, 2 * COLS),
            buffer(2, 4, 2 * HALF, 2 * COLS),
            buffer(3, HALF, 2 * COLS),
            buffer(64, 2 * COLS),
            buffer(64, 2 * COLS),
            buffer(4, HALF, 2 * COLS),
            buffer(4, HALF, 2 * COLS),
            buffer(4, 2, HALF, COLS),
            buffer(3, 2, HALF, COLS),
            buffer(2, HALF, COLS),
            buffer(TOK, COLS),
            buffer(4, 2, 2, 384, COLS),
            buffer(4, 2, 384, COLS),
            buffer(4, 2, 384, COLS),
            buffer(384, COLS),
            buffer(384, COLS),
            buffer(2, 384, COLS),
            buffer(2, 384, COLS),
            buffer(4, ROWS, COLS),
            pltpu.SemaphoreType.DMA((N_SEM,)),
            pltpu.SemaphoreType.DMA((N_SEM,)),
            pltpu.SemaphoreType.DMA((4,)),
        ],
        compiler_params=pltpu.CompilerParams(
            collective_id=0, has_side_effects=True, vmem_limit_bytes=60 * 2**20
        ),
        cost_estimate=pl.CostEstimate(
            flops=3 * 2 * 512 * 3072 * 768, bytes_accessed=4 * 2**20, transcendentals=0
        ),
        name="elastic_up_backward",
    )(activations, act_grad, up_weight, width_steps.reshape(2, 128))
    return pl.pallas_call(
        hand_on,
        out_shape=results,
        in_specs=[any_space] * 2,
        out_specs=(any_space, any_space),
        scratch_shapes=[buffer(TOK, COLS), buffer(ROWS, HID), pltpu.SemaphoreType.DMA((2, 3))],
        compiler_params=pltpu.CompilerParams(vmem_limit_bytes=60 * 2**20),
        name="hand_on",
    )(input_grad, weight_grad)


def solution(mesh):
    placed = (P("dp", "tensor"), P("dp", "tensor"), P("dp", "tensor"), P("dp"))
    return jax.shard_map(
        shards,
        mesh=mesh,
        in_specs=placed,
        out_specs=(P("dp", "tensor"), P("dp", "tensor")),
        check_vma=False,
    )
```

```python
import jax
import jax.numpy as jnp
from jax import lax
from jax.experimental import pallas as pl
from jax.experimental.pallas import tpu as pltpu
from jax.sharding import PartitionSpec as P

MESH = pl.DeviceIdType.MESH
F32 = jnp.float32
BF16 = jnp.bfloat16
TOK = 256
HALF = 128
ROWS = 192
COLS = 384
HID = 1536
SCALE = 1.0 / 64.0
N_SEM = 208

STEP = (0, 1, 3, 2)
FROM = (0, 3, 1, 2)
PLACE = (2, 0, 1, 3)
SLOT = (0, 1, 3, 2)
SUB = (2, 1, 3, 0)

ORDER = (
    "wb1", "zfp0", "yfm0", "zfm0", "yfp0", "wa2", "xa2", "zdm0", "xb1", "w2s", "wb2", "xb2", "zfm1", "wa1",
    "xa3", "zfp2", "zdp0", "mask", "g13", "xa1", "xb3", "xy1", "wa3", "wb3", "yfm1", "yfp2", "zl0", "zdm1",
    "xy3", "zfp1", "zfm2", "yfp3", "zfp3", "g2", "zfm3", "zdm2", "zdp3", "zdp1", "zdp2", "zdm3", "yfm3",
    "zl1", "wr1", "zl2", "Pa0", "zl3", "PaA", "wr2", "PbA", "IA3", "IA1", "Pb3", "Pb0", "D21", "D20", "IB2",
    "sent", "D10", "D30", "E21", "E20", "Zv0", "Zv1", "IA2", "D31", "D11", "E30", "IB3", "IA0", "Zv2", "E10",
    "Ql", "E31", "Qu", "R2s", "IB1", "E11", "Zd1", "R1s", "Zc0", "IB0", "D01", "R1o", "R2o", "Zd0", "Zc2",
    "Zc1", "R3s", "S0", "Zd2", "Zv3", "D00", "E01", "R3o", "E00", "ZL0", "Zd3", "Vm", "Vp", "ZL1", "ZL2",
    "Zc3", "RF", "ZL3",
)

def kernel(
    x_ref, g_ref, w_ref, wid_ref, dx_ref, dw_ref,
    xb, wb, gb, gin, wid, acc, hid, sd, qb, qv, vp, vm, ap, am, ap0, am0, rb, xr, own, out,
    dwp, dwr, dws, zvp, zvm, zap, zam, tot, ssem, rsem, lsem,
):
    dp, tensor = lax.axis_index("dp"), lax.axis_index("tensor")
    z, x = lax.div(dp, 4), lax.rem(dp, 4)
    y, c = lax.div(tensor, 2), lax.rem(tensor, 2)
    other = 1 - c

    def ring(v, step):
        return lax.rem(v + step, 4)

    def device(dz=0, dx=0, dy=0, dc=0):
        return (
            ring(z, dz) * 4 + ring(x, dx),
            ring(y, dy) * 2 + (other if dc else c),
        )

    sites = {}

    def send(name, src, dst, **to):
        slot = len(sites)
        copy = pltpu.make_async_remote_copy(
            src_ref=src,
            dst_ref=dst,
            send_sem=ssem.at[slot],
            recv_sem=rsem.at[slot],
            device_id=device(**to),
            device_id_type=MESH,
        )
        copy.start()
        sites[name] = copy

    taken = set()

    def arrived(*names):
        for name in names:
            if name not in taken:
                taken.add(name)
                sites[name].wait_recv()

    def place(j):
        return pl.ds(PLACE[j] * HALF, HALF)

    def chunk(dy, core):
        return ring(y, dy) * 2 + core

    def half_of(core):
        return pl.ds(pl.multiple_of(core * HALF, HALF), HALF)

    def weight_rows(dz, dx):
        return pl.ds(pl.multiple_of(SLOT[dz] * 768 + ring(x, dx) * ROWS, ROWS), ROWS)

    def weight_half(dz, dx, half):
        start = SLOT[dz] * 768 + ring(x, dx) * ROWS + half * 96
        return pl.ds(pl.multiple_of(start, 96), 96)

    def sub_block(step):
        return pl.ds(pl.multiple_of(ring(x, step) * COLS, COLS), COLS)

    own_cols = pl.ds(pl.multiple_of(c * COLS, COLS), COLS)
    other_cols = pl.ds(pl.multiple_of(other * COLS, COLS), COLS)
    both = (("s", own_cols, 0), ("o", other_cols, 1))

    own_w = pltpu.make_async_copy(
        w_ref.at[:, sub_block(0)], wb.at[weight_rows(0, 0), own_cols], lsem.at[2]
    )
    own_x = pltpu.make_async_copy(
        x_ref.at[half_of(c)], xb.at[chunk(0, c), place(0)], lsem.at[1]
    )
    own_g = pltpu.make_async_copy(g_ref, gin, lsem.at[0])
    own_wid = pltpu.make_async_copy(wid_ref, wid, lsem.at[3])
    put_g = pltpu.make_async_copy(
        gin.at[half_of(c), sub_block(0)], gb.at[place(0), own_cols], lsem.at[0]
    )
    put_w = pltpu.make_async_copy(tot.at[3], dw_ref.at[:, sub_block(0)], lsem.at[1])
    put_x = pltpu.make_async_copy(out, dx_ref, lsem.at[2])

    partners = (
        dict(dx=1), dict(dx=3), dict(dx=2), dict(dy=1), dict(dy=3), dict(dz=1), dict(dz=3), dict(dc=1),
        dict(dx=1, dc=1), dict(dx=3, dc=1), dict(dx=2, dc=1), dict(dy=1, dc=1), dict(dy=3, dc=1),
    )
    barrier = pltpu.get_barrier_semaphore()
    for to in partners:
        pl.semaphore_signal(barrier, inc=1, device_id=device(**to), device_id_type=MESH)
    own_wid.start()
    own_g.start()
    own_x.start()
    own_w.start()
    pl.semaphore_wait(barrier, len(partners))

    tasks = {}

    def task(name, *args):
        def enter(step):
            tasks[name] = lambda: step(*args)
            return step

        return enter

    def x_send(step, kind):
        core, dc = (c, 0) if kind == "s" else (other, 1)
        j = FROM[STEP.index(step)]
        dst = xb.at[chunk(0, c), place(STEP.index(j))]
        send(f"x{step}{kind}", x_ref.at[half_of(core)], dst, dx=step, dc=dc)

    def y_send(j, name, kind):
        dy = 1 if name == "yp" else 3
        if j == 0:
            core, dc = (c, 0) if kind == "s" else (other, 1)
            send(f"{name}0{kind}", x_ref.at[half_of(core)], xb.at[chunk(0, c), place(0)], dy=dy, dc=dc)
        else:
            ref = xb.at[chunk(0, c if kind == "s" else other), place(j)]
            send(f"{name}{j}{kind}", ref, ref, dy=dy)

    def x_arrive(j, kind):
        if j < 3:
            arrived(f"x{FROM[j]}{kind}")
        else:
            arrived("xf1" if kind == "s" else "xf3")
        if j == 2 and kind == "s":
            at = chunk(0, c)
            send("xf1", xb.at[at, place(2)], xb.at[at, place(3)], dx=1)
        if j == 1 and kind == "o":
            at = chunk(0, other)
            send("xf3", xb.at[at, place(1)], xb.at[at, place(3)], dx=3)
        for name in ("yp", "ym") if kind == "s" else ("ym", "yp"):
            y_send(j, name, kind)

    @task("xy3")
    def across_back():
        arrived("yfp0")
        at = chunk(2, c)
        send("xy3s", xb.at[at, place(0)], xb.at[at, place(1)], dx=3)

    @task("xy1")
    def across_on():
        arrived("yfm0")
        at = chunk(2, other)
        send("xy1o", xb.at[at, place(0)], xb.at[at, place(2)], dx=1)

    def y_forward_up(j):
        arrived(f"yp{j}s")
        ref = xb.at[chunk(3, c), place(j)]
        send(f"yfp{j}", ref, ref, dy=1)

    def y_forward_down(j):
        arrived(f"ym{j}o")
        ref = xb.at[chunk(1, other), place(j)]
        send(f"yfm{j}", ref, ref, dy=3)

    def w_send(step, half):
        src = w_ref.at[pl.ds(half * 96, 96), sub_block(step)]
        dst = wb.at[weight_half(0, 0, half), own_cols]
        send(f"w{step}{'ab'[half]}", src, dst, dx=step)

    def z_send(j, name, half):
        to = 1 if name == "zp" else 3
        src = wb.at[weight_half(0, STEP[j], half), own_cols]
        if j == 0:
            src = w_ref.at[pl.ds(half * 96, 96), sub_block(0)]
        dst = wb.at[weight_half(4 - to, STEP[j], half), own_cols]
        send(f"{name}{j}{'ab'[half]}", src, dst, dz=to)

    def w_arrive(j, half):
        arrived(f"w{FROM[j]}{'ab'[half]}")
        for name in ("zm", "zp") if half else ("zp", "zm"):
            z_send(j, name, half)
        ref = wb.at[weight_half(0, STEP[j], half), own_cols]
        send(f"ws{'ab'[half]}{j}", ref, ref, dc=1)

    def w_pair(name, dz, j):
        dst = wb.at[weight_rows(dz, STEP[j]), own_cols]
        src = w_ref.at[:, sub_block(0)] if name == "ws0" else dst
        send(name, src, dst, dc=1)

    def z_forward_up(j):
        arrived(f"zp{j}a")
        src = wb.at[weight_half(3, STEP[j], 0), own_cols]
        send(f"zfp{j}", src, wb.at[weight_half(2, STEP[j], 0), own_cols], dz=1)

    def z_forward_down(j):
        arrived(f"zm{j}b")
        src = wb.at[weight_half(1, STEP[j], 1), own_cols]
        send(f"zfm{j}", src, wb.at[weight_half(2, STEP[j], 1), own_cols], dz=3)

    def z_whole_up(j):
        arrived(f"zp{j}b")
        w_pair(f"d1{j}", 3, j)

    def z_whole_down(j):
        arrived(f"zm{j}a")
        w_pair(f"d3{j}", 1, j)

    def z_across(j):
        arrived(f"zfp{j}", f"zfm{j}")
        w_pair(f"d2{j}", 2, j)

    @task("w2s")
    def w_across():
        w_send(2, 0)
        w_send(2, 1)

    @task("wr1")
    def weights_near():
        own_w.wait()
        for j in range(4):
            arrived(f"d1{j}", f"d3{j}")
            arrived(*((f"wsa{j}", f"wsb{j}") if j else ("ws0",)))

    @task("wr2")
    def weights_across():
        for j in range(4):
            arrived(f"d2{j}")

    def g_send(step, kind):
        core, dc = (c, 0) if kind == "s" else (other, 1)
        j = FROM[STEP.index(step)]
        dst = gb.at[place(STEP.index(j)), own_cols]
        send(f"g{step}{kind}", gin.at[half_of(core), sub_block(step)], dst, dx=step, dc=dc)

    @task("mask")
    def mask():
        own_wid.wait()
        own_g.wait()
        for half in range(2):
            rows = pl.ds(half * 128, 128)
            width = jnp.broadcast_to(wid[half : half + 1, :], (128, 128)).T
            keep = jnp.where(width > tensor, 1.0, 0.0).astype(BF16)
            for part in range(HID // 128):
                lanes = pl.ds(part * 128, 128)
                gin[rows, lanes] = gin[rows, lanes] * keep
        put_g.start()
        send("gs", gin.at[half_of(other), sub_block(0)], gb.at[place(0), own_cols], dc=1)

    @task("g13")
    def g_near():
        g_send(1, "s")
        g_send(3, "s")
        g_send(1, "o")
        g_send(3, "o")

    @task("g2")
    def g_across():
        g_send(2, "s")
        g_send(2, "o")

    for j in range(4):
        if j:
            task(f"xa{j}", j, "s")(x_arrive)
            task(f"xb{j}", j, "o")(x_arrive)
            task(f"wa{j}", j, 0)(w_arrive)
            task(f"wb{j}", j, 1)(w_arrive)
        task(f"yfp{j}", j)(y_forward_up)
        task(f"yfm{j}", j)(y_forward_down)
        task(f"zfp{j}", j)(z_forward_up)
        task(f"zfm{j}", j)(z_forward_down)
        task(f"zdp{j}", j)(z_whole_up)
        task(f"zdm{j}", j)(z_whole_down)
        task(f"zl{j}", j)(z_across)

    def features(dz, rows):
        return [xb[ring(z, dz) * 2 + h, rows, :] for h in range(2)]

    def batch(places):
        return pl.ds(PLACE[places[0]] * HALF, HALF * len(places))

    def tokens_ready(*places):
        for j in places:
            arrived(f"yp{j}o", f"ym{j}s")
            if j == 1:
                arrived("yp1s", "xy3s")
            else:
                arrived(f"yfp{j}")
            if j == 2:
                arrived("ym2o", "xy1o")
            else:
                arrived(f"yfm{j}")
            if j == 0:
                own_x.wait()
                arrived("xs")

    def hidden_near(*places):
        tokens_ready(*places)
        rows = batch(places)
        part = jnp.concatenate(features(0, rows) + features(1, rows) + features(3, rows), axis=1)
        acc[rows, :] = jnp.dot(part, wb[pl.ds(0, 2304), :], preferred_element_type=F32)

    def hidden_last(*places):
        for j in places:
            if j == 0:
                put_g.wait()
                arrived("gs")
            else:
                arrived(f"g{FROM[j]}s", f"g{FROM[j]}o")
        rows = batch(places)
        if places == (3,):
            tokens_ready(3)
            part = jnp.concatenate(sum((features(d, rows) for d in (0, 1, 3, 2)), []), axis=1)
            preact = jnp.dot(part, wb[...], preferred_element_type=F32)
        else:
            part = jnp.concatenate(features(2, rows), axis=1)
            preact = acc[rows, :] + jnp.dot(part, wb[pl.ds(2304, 768), :], preferred_element_type=F32)
        slope = 2.0 * jnp.maximum(preact, 0.0)
        hid[rows, :] = (gb[rows, :].astype(F32) * slope).astype(BF16)

    for name, places in (("A", (1, 2)), ("0", (0,)), ("3", (3,))):
        if name != "3":
            task("Pa" + name, *places)(hidden_near)
        task("Pb" + name, *places)(hidden_last)

    first, second = pl.ds(0, 128), pl.ds(128, 128)
    upper, lower = pl.ds(0, 64), pl.ds(64, 64)
    upper2, lower2 = pl.ds(128, 64), pl.ds(192, 64)

    def input_part(b, d):
        dz = lax.rem(y + d - z + 4, 4)
        slot = dz + lax.div(dz, 2) - 2 * lax.div(dz, 3)
        rows = pl.ds(pl.multiple_of(slot * 768, 768), 768)
        sd[b, d] = lax.dot_general(
            hid[pl.ds(b * 256, 256), :], wb[rows, :], (((1,), (1,)), ((), ())), preferred_element_type=F32
        ).astype(BF16)
        if d == 2 and b == 0:
            send("q1l", sd.at[0, 2, lower], qb.at[0, lower], dx=1)
            send("q3u", sd.at[0, 2, upper2], qb.at[1, upper], dx=3)
        elif d == 2:
            send("q2a", sd.at[1, 2, upper2], qv.at[0], dx=1)
            send("q2b", sd.at[1, 2, lower2], qv.at[1], dx=3)
        elif d == 0 and b == 1:
            own[c] = sd[1, 0, first, own_cols]
            send("xro", sd.at[1, 0, first, other_cols], own.at[c], dc=1)
        elif d != 0:
            got, dy = (ap, 1) if d == 1 else (am, 3)
            for kind, cols, _ in both:
                for j in (1, 2) if b == 0 else (3,):
                    rows = second if PLACE[j] % 2 else first
                    send(f"a{d}{j}{kind}", sd.at[b, d, rows, cols], got.at[PLACE[j], :, cols], dy=dy)
            if b == 1:
                own_send("a10l" if d == 1 else "a30t", d, lower if d == 1 else upper)

    def own_send(name, d, rows):
        got, dy = (ap0, 1) if d == 1 else (am0, 3)
        for kind, cols, dc in both:
            send(name + kind, sd.at[1, d, rows, cols], got.at[c, rows], dy=dy, dc=dc)

    for b in range(2):
        for d in range(4):
            task(f"I{'AB'[b]}{d}", b, d)(input_part)

    @task("Qu")
    def across_up():
        arrived("q2a")
        sd[0, 2, upper] = (sd[0, 2, upper].astype(F32) + qv[0].astype(F32)).astype(BF16)
        send("q1u", sd.at[0, 2, upper], qb.at[0, upper], dx=1)

    @task("Ql")
    def across_down():
        arrived("q2b")
        sd[0, 2, lower2] = (sd[0, 2, lower2].astype(F32) + qv[1].astype(F32)).astype(BF16)
        send("q3l", sd.at[0, 2, lower2], qb.at[1, lower], dx=3)

    @task("S0")
    def across_total():
        arrived("q1l", "q1u", "q3u", "q3l")
        total = sd[1, 2, first].astype(F32) + qb[0].astype(F32) + qb[1].astype(F32)
        sd[1, 2, first] = total.astype(BF16)
        send("vp", sd.at[1, 2, upper], vp, dy=1)
        send("vm", sd.at[1, 2, lower], vm, dy=3)

    @task("Vp")
    def via_up():
        arrived("vp")
        sd[1, 1, upper] = (sd[1, 1, upper].astype(F32) + vp[...].astype(F32)).astype(BF16)
        own_send("a10t", 1, upper)

    @task("Vm")
    def via_down():
        arrived("vm")
        sd[1, 3, lower] = (sd[1, 3, lower].astype(F32) + vm[...].astype(F32)).astype(BF16)
        own_send("a30l", 3, lower)

    def input_total(j, kind, cols, dc):
        arrived(f"a1{j}{kind}", f"a3{j}{kind}")
        at, rows = PLACE[j], (first, second)[PLACE[j] % 2]
        total = (
            sd[at // 2, 0, rows, cols].astype(F32) + ap[at, :, cols].astype(F32) + am[at, :, cols].astype(F32)
        )
        rb[at, dc] = total.astype(BF16)
        send(f"xr{STEP[j]}{kind}", rb.at[at, dc], xr.at[STEP[j] - 1, c], dx=STEP[j], dc=dc)

    for j in range(1, 4):
        for kind, cols, dc in both:
            task(f"R{j}{kind}", j, kind, cols, dc)(input_total)

    @task("RF")
    def input_final():
        arrived("xr1s", "xr1o", "xr3s", "xr3o", "xr2s", "xr2o", "xro")
        for name in ("a10l", "a10t", "a30t", "a30l"):
            arrived(name + "s", name + "o")
        for half in range(2):
            total = own[half].astype(F32) + ap0[half].astype(F32) + am0[half].astype(F32)
            for slot in range(3):
                total = total + xr[slot, half].astype(F32)
            out[pl.ds(half * HALF, HALF), :] = total.astype(BF16)
        put_x.start()

    def weight_part(d, h):
        part = lax.dot_general(
            xb[ring(z, d) * 2 + h], hid[...], (((0,), (0,)), ((), ())), preferred_element_type=F32
        ).astype(BF16)
        dwp[d, h, 0] = part[:, :COLS]
        dwp[d, h, 1] = part[:, COLS:]
        send(f"e{d}{h}", dwp.at[d, h, other], dwr.at[d, h], dc=1)

    def weight_pair(d, h):
        arrived(f"e{d}{h}")
        total = (dwp[d, h, c].astype(F32) + dwr[d, h].astype(F32)).astype(BF16)
        for p in range(2):
            step = lax.rem(h * 2 + p - x + 4, 4)
            at = lax.rem(lax.rem(3 * step + 3, 5), 4)
            rows = pl.ds(pl.multiple_of(at * 96, 96), 96)
            dws[d, 0, rows] = total[p * ROWS : p * ROWS + 96]
            dws[d, 1, rows] = total[p * ROWS + 96 : p * ROWS + ROWS]

    for d in range(4):
        for h in range(2):
            task(f"D{d}{h}", d, h)(weight_part)
            task(f"E{d}{h}", d, h)(weight_pair)

    def sub_rows(q):
        return pl.ds(q * 96, 96)

    def weight_first(q):
        rows = sub_rows(q)
        send(f"zvp{q}", dws.at[2, 0, rows], zvp.at[rows], dz=1)
        send(f"zvm{q}", dws.at[2, 1, rows], zvm.at[rows], dz=3)

    def weight_direct(q):
        rows = sub_rows(q)
        send(f"zdp{q}", dws.at[1, 1, rows], zap.at[1, rows], dz=1)
        send(f"zdm{q}", dws.at[3, 0, rows], zam.at[0, rows], dz=3)

    def weight_via(q):
        arrived(f"zvp{q}", f"zvm{q}")
        rows = sub_rows(q)
        dws[1, 0, rows] = (dws[1, 0, rows].astype(F32) + zvp[rows].astype(F32)).astype(BF16)
        send(f"zcp{q}", dws.at[1, 0, rows], zap.at[0, rows], dz=1)
        dws[3, 1, rows] = (dws[3, 1, rows].astype(F32) + zvm[rows].astype(F32)).astype(BF16)
        send(f"zcm{q}", dws.at[3, 1, rows], zam.at[1, rows], dz=3)

    def weight_last(q):
        arrived(f"zdp{q}", f"zdm{q}", f"zcp{q}", f"zcm{q}")
        rows = sub_rows(q)
        for half in range(2):
            total = (
                dws[0, half, rows].astype(F32) + zap[half, rows].astype(F32) + zam[half, rows].astype(F32)
            )
            tot[q, pl.ds(half * 96, 96)] = (total * SCALE).astype(BF16)
        if q < 3:
            send(f"t{q}", tot.at[q], dw_ref.at[:, sub_block(0)], dx=SUB[q])
        else:
            put_w.start()

    for q in range(4):
        task(f"Zv{q}", q)(weight_first)
        task(f"Zd{q}", q)(weight_direct)
        task(f"Zc{q}", q)(weight_via)
        task(f"ZL{q}", q)(weight_last)

    left = []

    @task("sent")
    def early_sends():
        for name in left:
            sites[name].wait_send()

    w_send(1, 0)
    w_send(3, 1)
    x_send(1, "s")
    x_send(3, "o")
    w_send(1, 1)
    w_send(3, 0)
    x_send(1, "o")
    x_send(3, "s")
    y_send(0, "yp", "s")
    y_send(0, "ym", "o")
    z_send(0, "zp", 0)
    z_send(0, "zm", 1)
    y_send(0, "yp", "o")
    y_send(0, "ym", "s")
    z_send(0, "zp", 1)
    z_send(0, "zm", 0)
    w_pair("ws0", 0, 0)
    send("xs", x_ref.at[half_of(other)], xb.at[chunk(0, c), place(0)], dc=1)
    for name in ORDER:
        if not left and name[0] in "ID":
            left.extend(sites)
        tasks[name]()
    for name, copy in sites.items():
        if name not in left:
            copy.wait_send()
    arrived("t0", "t1", "t2")
    put_w.wait()
    put_x.wait()


def hand_on(a_ref, b_ref, a_out, b_out, a_buf, b_buf, sems):
    parts = [(b_ref.at[pl.ds(k * 96, 96)], b_buf.at[pl.ds(k * 96, 96)], b_out.at[pl.ds(k * 96, 96)]) for k in range(2)]
    parts.append((a_ref, a_buf, a_out))
    loads = [pltpu.make_async_copy(src, buf, sems.at[0, k]) for k, (src, buf, _) in enumerate(parts)]
    stores = [pltpu.make_async_copy(buf, dst, sems.at[1, k]) for k, (_, buf, dst) in enumerate(parts)]
    for copy in loads:
        copy.start()
    for load, store in zip(loads, stores):
        load.wait()
        store.start()
    for copy in stores:
        copy.wait()


def shards(activations, act_grad, up_weight, width_steps):
    any_space = pl.BlockSpec(memory_space=pl.ANY)

    def buffer(*shape):
        return pltpu.VMEM(shape, BF16)

    results = (
        jax.ShapeDtypeStruct((TOK, COLS), BF16),
        jax.ShapeDtypeStruct((ROWS, HID), BF16),
    )
    input_grad, weight_grad = pl.pallas_call(
        kernel,
        out_shape=results,
        in_specs=[any_space] * 4,
        out_specs=(any_space, any_space),
        scratch_shapes=[
            buffer(8, 4 * HALF, COLS),
            buffer(16 * ROWS, 2 * COLS),
            buffer(4 * HALF, 2 * COLS),
            buffer(TOK, HID),
            pltpu.VMEM((2, 128), jnp.int32),
            pltpu.VMEM((4 * HALF, 2 * COLS), F32),
            buffer(4 * HALF, 2 * COLS),
            buffer(2, 4, 2 * HALF, 2 * COLS),
            buffer(2, HALF, 2 * COLS),
            buffer(2, 64, 2 * COLS),
            buffer(64, 2 * COLS),
            buffer(64, 2 * COLS),
            buffer(4, HALF, 2 * COLS),
            buffer(4, HALF, 2 * COLS),
            buffer(2, HALF, COLS),
            buffer(2, HALF, COLS),
            buffer(4, 2, HALF, COLS),
            buffer(3, 2, HALF, COLS),
            buffer(2, HALF, COLS),
            buffer(TOK, COLS),
            buffer(4, 2, 2, 384, COLS),
            buffer(4, 2, 384, COLS),
            buffer(4, 2, 384, COLS),
            buffer(384, COLS),
            buffer(384, COLS),
            buffer(2, 384, COLS),
            buffer(2, 384, COLS),
            buffer(4, ROWS, COLS),
            pltpu.SemaphoreType.DMA((N_SEM,)),
            pltpu.SemaphoreType.DMA((N_SEM,)),
            pltpu.SemaphoreType.DMA((4,)),
        ],
        compiler_params=pltpu.CompilerParams(
            collective_id=0, has_side_effects=True, vmem_limit_bytes=60 * 2**20
        ),
        cost_estimate=pl.CostEstimate(
            flops=3 * 2 * 512 * 3072 * 768, bytes_accessed=4 * 2**20, transcendentals=0
        ),
        name="elastic_up_backward",
    )(activations, act_grad, up_weight, width_steps.reshape(2, 128))
    return pl.pallas_call(
        hand_on,
        out_shape=results,
        in_specs=[any_space] * 2,
        out_specs=(any_space, any_space),
        scratch_shapes=[buffer(TOK, COLS), buffer(ROWS, HID), pltpu.SemaphoreType.DMA((2, 3))],
        compiler_params=pltpu.CompilerParams(vmem_limit_bytes=60 * 2**20),
        name="hand_on",
    )(input_grad, weight_grad)


def solution(mesh):
    placed = (P("dp", "tensor"), P("dp", "tensor"), P("dp", "tensor"), P("dp"))
    return jax.shard_map(
        shards,
        mesh=mesh,
        in_specs=placed,
        out_specs=(P("dp", "tensor"), P("dp", "tensor")),
        check_vma=False,
    )
```

```python
import jax
import jax.numpy as jnp
from jax import lax
from jax.experimental import pallas as pl
from jax.experimental.pallas import tpu as pltpu
from jax.sharding import PartitionSpec as P

MESH = pl.DeviceIdType.MESH
F32 = jnp.float32
BF16 = jnp.bfloat16
TOK = 256
HALF = 128
ROWS = 192
COLS = 384
HID = 1536
SCALE = 1.0 / 64.0
N_SEM = 176

STEP = (0, 1, 3, 2)
FROM = (0, 3, 1, 2)
PLACE = (2, 0, 1, 3)
SLOT = (0, 1, 3, 2)
SUB = (2, 1, 3, 0)

ORDER = (
    "mask", "wa2", "zfp0", "yfp0", "yfm0", "xa2", "zfm0", "xb1", "wb2", "wa1", "w2s", "g13", "xb2", "zdp0",
    "xa1", "wb1", "zfm2", "zfp2", "wa3", "zdm0", "zdp2", "xb3", "zl0", "yfm1", "xy1", "wb3", "xa3", "yfp2",
    "zfp1", "xy3", "zdm2", "zfm1", "zfp3", "zfm3", "zl2", "zdp1", "zdm1", "zdm3", "yfm3", "zdp3", "g2",
    "yfp3", "wr1", "zl1", "Pa0", "zl3", "PaA", "wr2", "PbA", "IA1", "IA3", "Pb0", "Pb3", "D20", "IB2",
    "IA2", "IA0", "D21", "E20", "D10", "IB3", "IB1", "D30", "E21", "D31", "D11", "E10", "R1", "E30", "D00",
    "D01", "E31", "E11", "Zc1", "R2", "Zd0", "Zc0", "Zc2", "E00", "Zd1", "Zd2", "Zd3", "IB0", "sent", "E01",
    "S0", "Zc3", "R3", "ZL0", "Vp", "Vm", "ZL1", "ZL2", "R0", "ZL3", "RF",
)

def kernel(
    x_ref, g_ref, w_ref, wid_ref, dx_ref, dw_ref,
    xb, wb, gb, gin, wid, acc, hid, sd, qb, vp, vm, ap, am, rb, xr, own, out,
    dwp, dwr, dws, zvp, zvm, zap, zam, tot, ssem, rsem, lsem,
):
    dp, tensor = lax.axis_index("dp"), lax.axis_index("tensor")
    z, x = lax.div(dp, 4), lax.rem(dp, 4)
    y, c = lax.div(tensor, 2), lax.rem(tensor, 2)
    other = 1 - c

    def ring(v, step):
        return lax.rem(v + step, 4)

    def device(dz=0, dx=0, dy=0, dc=0):
        return (
            ring(z, dz) * 4 + ring(x, dx),
            ring(y, dy) * 2 + (other if dc else c),
        )

    sites = {}

    def send(name, src, dst, **to):
        slot = len(sites)
        copy = pltpu.make_async_remote_copy(
            src_ref=src,
            dst_ref=dst,
            send_sem=ssem.at[slot],
            recv_sem=rsem.at[slot],
            device_id=device(**to),
            device_id_type=MESH,
        )
        copy.start()
        sites[name] = copy

    taken = set()

    def arrived(*names):
        for name in names:
            if name not in taken:
                taken.add(name)
                sites[name].wait_recv()

    def place(j):
        return pl.ds(PLACE[j] * HALF, HALF)

    def chunk(dy, core):
        return ring(y, dy) * 2 + core

    def half_of(core):
        return pl.ds(pl.multiple_of(core * HALF, HALF), HALF)

    def weight_rows(dz, dx):
        return pl.ds(pl.multiple_of(SLOT[dz] * 768 + ring(x, dx) * ROWS, ROWS), ROWS)

    def weight_half(dz, dx, half):
        start = SLOT[dz] * 768 + ring(x, dx) * ROWS + half * 96
        return pl.ds(pl.multiple_of(start, 96), 96)

    def sub_block(step):
        return pl.ds(pl.multiple_of(ring(x, step) * COLS, COLS), COLS)

    own_cols = pl.ds(pl.multiple_of(c * COLS, COLS), COLS)

    own_w = pltpu.make_async_copy(
        w_ref.at[:, sub_block(0)], wb.at[weight_rows(0, 0), own_cols], lsem.at[2]
    )
    own_x = pltpu.make_async_copy(
        x_ref.at[half_of(c)], xb.at[chunk(0, c), place(0)], lsem.at[1]
    )
    own_g = pltpu.make_async_copy(g_ref, gin, lsem.at[0])
    own_wid = pltpu.make_async_copy(wid_ref, wid, lsem.at[3])
    put_g = pltpu.make_async_copy(
        gin.at[half_of(c), sub_block(0)], gb.at[place(0), own_cols], lsem.at[0]
    )
    put_w = pltpu.make_async_copy(tot.at[3], dw_ref.at[:, sub_block(0)], lsem.at[1])
    put_x = pltpu.make_async_copy(out, dx_ref, lsem.at[2])

    partners = (
        dict(dx=1), dict(dx=3), dict(dx=2), dict(dy=1), dict(dy=3), dict(dz=1), dict(dz=3), dict(dc=1),
        dict(dx=1, dc=1), dict(dx=3, dc=1), dict(dx=2, dc=1), dict(dy=1, dc=1), dict(dy=3, dc=1),
    )
    barrier = pltpu.get_barrier_semaphore()
    for to in partners:
        pl.semaphore_signal(barrier, inc=1, device_id=device(**to), device_id_type=MESH)
    own_wid.start()
    own_g.start()
    own_x.start()
    own_w.start()
    pl.semaphore_wait(barrier, len(partners))

    tasks = {}

    def task(name, *args):
        def enter(step):
            tasks[name] = lambda: step(*args)
            return step

        return enter

    def x_send(step, kind):
        core, dc = (c, 0) if kind == "s" else (other, 1)
        j = FROM[STEP.index(step)]
        dst = xb.at[chunk(0, c), place(STEP.index(j))]
        send(f"x{step}{kind}", x_ref.at[half_of(core)], dst, dx=step, dc=dc)

    def y_send(j, name, kind):
        dy = 1 if name == "yp" else 3
        if j == 0:
            core, dc = (c, 0) if kind == "s" else (other, 1)
            send(f"{name}0{kind}", x_ref.at[half_of(core)], xb.at[chunk(0, c), place(0)], dy=dy, dc=dc)
        else:
            ref = xb.at[chunk(0, c if kind == "s" else other), place(j)]
            send(f"{name}{j}{kind}", ref, ref, dy=dy)

    def x_arrive(j, kind):
        if j < 3:
            arrived(f"x{FROM[j]}{kind}")
        else:
            arrived("xf1" if kind == "s" else "xf3")
        if j == 2 and kind == "s":
            at = chunk(0, c)
            send("xf1", xb.at[at, place(2)], xb.at[at, place(3)], dx=1)
        if j == 1 and kind == "o":
            at = chunk(0, other)
            send("xf3", xb.at[at, place(1)], xb.at[at, place(3)], dx=3)
        for name in ("yp", "ym") if kind == "s" else ("ym", "yp"):
            y_send(j, name, kind)

    @task("xy3")
    def across_back():
        arrived("yfp0")
        at = chunk(2, c)
        send("xy3s", xb.at[at, place(0)], xb.at[at, place(1)], dx=3)

    @task("xy1")
    def across_on():
        arrived("yfm0")
        at = chunk(2, other)
        send("xy1o", xb.at[at, place(0)], xb.at[at, place(2)], dx=1)

    def y_forward_up(j):
        arrived(f"yp{j}s")
        ref = xb.at[chunk(3, c), place(j)]
        send(f"yfp{j}", ref, ref, dy=1)

    def y_forward_down(j):
        arrived(f"ym{j}o")
        ref = xb.at[chunk(1, other), place(j)]
        send(f"yfm{j}", ref, ref, dy=3)

    def w_send(step, half):
        src = w_ref.at[pl.ds(half * 96, 96), sub_block(step)]
        dst = wb.at[weight_half(0, 0, half), own_cols]
        send(f"w{step}{'ab'[half]}", src, dst, dx=step)

    def z_send(j, name, half):
        to = 1 if name == "zp" else 3
        src = wb.at[weight_half(0, STEP[j], half), own_cols]
        if j == 0:
            src = w_ref.at[pl.ds(half * 96, 96), sub_block(0)]
        dst = wb.at[weight_half(4 - to, STEP[j], half), own_cols]
        send(f"{name}{j}{'ab'[half]}", src, dst, dz=to)

    def w_arrive(j, half):
        arrived(f"w{FROM[j]}{'ab'[half]}")
        for name in ("zm", "zp") if half else ("zp", "zm"):
            z_send(j, name, half)
        ref = wb.at[weight_half(0, STEP[j], half), own_cols]
        send(f"ws{'ab'[half]}{j}", ref, ref, dc=1)

    def w_pair(name, dz, j):
        dst = wb.at[weight_rows(dz, STEP[j]), own_cols]
        src = w_ref.at[:, sub_block(0)] if name == "ws0" else dst
        send(name, src, dst, dc=1)

    def z_forward_up(j):
        arrived(f"zp{j}a")
        src = wb.at[weight_half(3, STEP[j], 0), own_cols]
        send(f"zfp{j}", src, wb.at[weight_half(2, STEP[j], 0), own_cols], dz=1)

    def z_forward_down(j):
        arrived(f"zm{j}b")
        src = wb.at[weight_half(1, STEP[j], 1), own_cols]
        send(f"zfm{j}", src, wb.at[weight_half(2, STEP[j], 1), own_cols], dz=3)

    def z_whole_up(j):
        arrived(f"zp{j}b")
        w_pair(f"d1{j}", 3, j)

    def z_whole_down(j):
        arrived(f"zm{j}a")
        w_pair(f"d3{j}", 1, j)

    def z_across(j):
        arrived(f"zfp{j}", f"zfm{j}")
        w_pair(f"d2{j}", 2, j)

    @task("w2s")
    def w_across():
        w_send(2, 0)
        w_send(2, 1)

    @task("wr1")
    def weights_near():
        own_w.wait()
        for j in range(4):
            arrived(f"d1{j}", f"d3{j}")
            arrived(*((f"wsa{j}", f"wsb{j}") if j else ("ws0",)))

    @task("wr2")
    def weights_across():
        for j in range(4):
            arrived(f"d2{j}")

    def g_send(step, kind):
        core, dc = (c, 0) if kind == "s" else (other, 1)
        j = FROM[STEP.index(step)]
        dst = gb.at[place(STEP.index(j)), own_cols]
        send(f"g{step}{kind}", gin.at[half_of(core), sub_block(step)], dst, dx=step, dc=dc)

    @task("mask")
    def mask():
        own_wid.wait()
        own_g.wait()
        for half in range(2):
            rows = pl.ds(half * 128, 128)
            width = jnp.broadcast_to(wid[half : half + 1, :], (128, 128)).T
            keep = jnp.where(width > tensor, 1.0, 0.0).astype(BF16)
            for part in range(HID // 128):
                lanes = pl.ds(part * 128, 128)
                gin[rows, lanes] = gin[rows, lanes] * keep
        put_g.start()
        send("gs", gin.at[half_of(other), sub_block(0)], gb.at[place(0), own_cols], dc=1)

    @task("g13")
    def g_near():
        g_send(1, "s")
        g_send(3, "s")
        g_send(1, "o")
        g_send(3, "o")

    @task("g2")
    def g_across():
        g_send(2, "s")
        g_send(2, "o")

    for j in range(4):
        if j:
            task(f"xa{j}", j, "s")(x_arrive)
            task(f"xb{j}", j, "o")(x_arrive)
            task(f"wa{j}", j, 0)(w_arrive)
            task(f"wb{j}", j, 1)(w_arrive)
        task(f"yfp{j}", j)(y_forward_up)
        task(f"yfm{j}", j)(y_forward_down)
        task(f"zfp{j}", j)(z_forward_up)
        task(f"zfm{j}", j)(z_forward_down)
        task(f"zdp{j}", j)(z_whole_up)
        task(f"zdm{j}", j)(z_whole_down)
        task(f"zl{j}", j)(z_across)

    def features(dz, rows):
        return [xb[ring(z, dz) * 2 + h, rows, :] for h in range(2)]

    def batch(places):
        return pl.ds(PLACE[places[0]] * HALF, HALF * len(places))

    def tokens_ready(*places):
        for j in places:
            arrived(f"yp{j}o", f"ym{j}s")
            if j == 1:
                arrived("yp1s", "xy3s")
            else:
                arrived(f"yfp{j}")
            if j == 2:
                arrived("ym2o", "xy1o")
            else:
                arrived(f"yfm{j}")
            if j == 0:
                own_x.wait()
                arrived("xs")

    def hidden_near(*places):
        tokens_ready(*places)
        rows = batch(places)
        part = jnp.concatenate(features(0, rows) + features(1, rows) + features(3, rows), axis=1)
        acc[rows, :] = jnp.dot(part, wb[pl.ds(0, 2304), :], preferred_element_type=F32)

    def hidden_last(*places):
        for j in places:
            if j == 0:
                put_g.wait()
                arrived("gs")
            else:
                arrived(f"g{FROM[j]}s", f"g{FROM[j]}o")
        rows = batch(places)
        if places == (3,):
            tokens_ready(3)
            part = jnp.concatenate(sum((features(d, rows) for d in (0, 1, 3, 2)), []), axis=1)
            preact = jnp.dot(part, wb[...], preferred_element_type=F32)
        else:
            part = jnp.concatenate(features(2, rows), axis=1)
            preact = acc[rows, :] + jnp.dot(part, wb[pl.ds(2304, 768), :], preferred_element_type=F32)
        slope = 2.0 * jnp.maximum(preact, 0.0)
        hid[rows, :] = (gb[rows, :].astype(F32) * slope).astype(BF16)

    for name, places in (("A", (1, 2)), ("0", (0,)), ("3", (3,))):
        if name != "3":
            task("Pa" + name, *places)(hidden_near)
        task("Pb" + name, *places)(hidden_last)

    first, second = pl.ds(0, 128), pl.ds(128, 128)
    upper, lower = pl.ds(0, 64), pl.ds(64, 64)

    def input_part(b, d):
        dz = lax.rem(y + d - z + 4, 4)
        slot = dz + lax.div(dz, 2) - 2 * lax.div(dz, 3)
        rows = pl.ds(pl.multiple_of(slot * 768, 768), 768)
        sd[b, d] = lax.dot_general(
            hid[pl.ds(b * 256, 256), :], wb[rows, :], (((1,), (1,)), ((), ())), preferred_element_type=F32
        ).astype(BF16)
        if d == 2 and b == 0:
            send("q1", sd.at[0, 2, first], qb.at[0], dx=1)
            send("q3", sd.at[0, 2, second], qb.at[1], dx=3)
        elif d == 2:
            send("q2", sd.at[1, 2, second], qb.at[2], dx=2)
        elif d == 1 and b == 0:
            send("a11", sd.at[0, 1, first], ap.at[0], dy=1)
            send("a12", sd.at[0, 1, second], ap.at[1], dy=1)
        elif d == 3 and b == 0:
            send("a31", sd.at[0, 3, first], am.at[0], dy=3)
            send("a32", sd.at[0, 3, second], am.at[1], dy=3)
        elif d == 1:
            send("a13", sd.at[1, 1, second], ap.at[3], dy=1)
            send("a10l", sd.at[1, 1, lower], ap.at[2, lower], dy=1)
        elif d == 3:
            send("a33", sd.at[1, 3, second], am.at[3], dy=3)
            send("a30t", sd.at[1, 3, upper], am.at[2, upper], dy=3)

    for b in range(2):
        for d in range(4):
            task(f"I{'AB'[b]}{d}", b, d)(input_part)

    @task("S0")
    def across_total():
        arrived("q1", "q3", "q2")
        total = sd[1, 2, first].astype(F32)
        for slot in range(3):
            total = total + qb[slot].astype(F32)
        sd[1, 2, first] = total.astype(BF16)
        send("vp", sd.at[1, 2, upper], vp, dy=1)
        send("vm", sd.at[1, 2, lower], vm, dy=3)

    @task("Vp")
    def via_up():
        arrived("vp")
        sd[1, 1, upper] = (sd[1, 1, upper].astype(F32) + vp[...].astype(F32)).astype(BF16)
        send("a10t", sd.at[1, 1, upper], ap.at[2, upper], dy=1)

    @task("Vm")
    def via_down():
        arrived("vm")
        sd[1, 3, lower] = (sd[1, 3, lower].astype(F32) + vm[...].astype(F32)).astype(BF16)
        send("a30l", sd.at[1, 3, lower], am.at[2, lower], dy=3)

    def input_total(j):
        if j == 0:
            arrived("a10l", "a10t", "a30t", "a30l")
        else:
            arrived(f"a1{j}", f"a3{j}")
        at, rows = PLACE[j], (first, second)[PLACE[j] % 2]
        total = sd[at // 2, 0, rows].astype(F32) + ap[at].astype(F32) + am[at].astype(F32)
        total = total.astype(BF16)
        rb[at, 0] = total[:, :COLS]
        rb[at, 1] = total[:, COLS:]
        if j == 0:
            own[c] = rb[at, c]
            send("xro", rb.at[at, other], own.at[c], dc=1)
        else:
            step = STEP[j]
            send(f"xr{step}s", rb.at[at, c], xr.at[step - 1, c], dx=step)
            send(f"xr{step}o", rb.at[at, other], xr.at[step - 1, c], dx=step, dc=1)

    for j in range(4):
        task(f"R{j}", j)(input_total)

    @task("RF")
    def input_final():
        arrived("xr1s", "xr1o", "xr3s", "xr3o", "xr2s", "xr2o", "xro")
        for half in range(2):
            total = own[half].astype(F32)
            for slot in range(3):
                total = total + xr[slot, half].astype(F32)
            out[pl.ds(half * HALF, HALF), :] = total.astype(BF16)
        put_x.start()

    def weight_part(d, h):
        part = lax.dot_general(
            xb[ring(z, d) * 2 + h], hid[...], (((0,), (0,)), ((), ())), preferred_element_type=F32
        ).astype(BF16)
        dwp[d, h, 0] = part[:, :COLS]
        dwp[d, h, 1] = part[:, COLS:]
        send(f"e{d}{h}", dwp.at[d, h, other], dwr.at[d, h], dc=1)

    def weight_pair(d, h):
        arrived(f"e{d}{h}")
        total = (dwp[d, h, c].astype(F32) + dwr[d, h].astype(F32)).astype(BF16)
        for p in range(2):
            step = lax.rem(h * 2 + p - x + 4, 4)
            at = lax.rem(lax.rem(3 * step + 3, 5), 4)
            rows = pl.ds(pl.multiple_of(at * 96, 96), 96)
            dws[d, 0, rows] = total[p * ROWS : p * ROWS + 96]
            dws[d, 1, rows] = total[p * ROWS + 96 : p * ROWS + ROWS]
            if d == 2:
                via_copy("zvp", at, rows).start()
                via_copy("zvm", at, rows).start()

    for d in range(4):
        for h in range(2):
            task(f"D{d}{h}", d, h)(weight_part)
            task(f"E{d}{h}", d, h)(weight_pair)

    def sub_rows(q):
        return pl.ds(q * 96, 96)

    via_slots = {}

    def via_copy(name, at, rows):
        up = name == "zvp"
        return pltpu.make_async_remote_copy(
            src_ref=dws.at[2, 0 if up else 1, rows],
            dst_ref=(zvp if up else zvm).at[rows],
            send_sem=ssem.at[via_slots[name] + at],
            recv_sem=rsem.at[via_slots[name] + at],
            device_id=device(dz=1 if up else 3),
            device_id_type=MESH,
        )

    for name in ("zvp", "zvm"):
        via_slots[name] = len(sites)
        for q in range(4):
            sites[f"{name}{q}"] = via_copy(name, q, sub_rows(q))

    def weight_direct(q):
        rows = sub_rows(q)
        send(f"zdp{q}", dws.at[1, 1, rows], zap.at[1, rows], dz=1)
        send(f"zdm{q}", dws.at[3, 0, rows], zam.at[0, rows], dz=3)

    def weight_via(q):
        arrived(f"zvp{q}", f"zvm{q}")
        rows = sub_rows(q)
        dws[1, 0, rows] = (dws[1, 0, rows].astype(F32) + zvp[rows].astype(F32)).astype(BF16)
        send(f"zcp{q}", dws.at[1, 0, rows], zap.at[0, rows], dz=1)
        dws[3, 1, rows] = (dws[3, 1, rows].astype(F32) + zvm[rows].astype(F32)).astype(BF16)
        send(f"zcm{q}", dws.at[3, 1, rows], zam.at[1, rows], dz=3)

    def weight_last(q):
        arrived(f"zdp{q}", f"zdm{q}", f"zcp{q}", f"zcm{q}")
        rows = sub_rows(q)
        for half in range(2):
            total = (
                dws[0, half, rows].astype(F32) + zap[half, rows].astype(F32) + zam[half, rows].astype(F32)
            )
            tot[q, pl.ds(half * 96, 96)] = (total * SCALE).astype(BF16)
        if q < 3:
            send(f"t{q}", tot.at[q], dw_ref.at[:, sub_block(0)], dx=SUB[q])
        else:
            put_w.start()

    for q in range(4):
        task(f"Zd{q}", q)(weight_direct)
        task(f"Zc{q}", q)(weight_via)
        task(f"ZL{q}", q)(weight_last)

    left = []

    @task("sent")
    def early_sends():
        for name in left:
            sites[name].wait_send()

    w_send(1, 0)
    w_send(3, 1)
    x_send(1, "s")
    x_send(3, "o")
    w_send(1, 1)
    w_send(3, 0)
    x_send(1, "o")
    x_send(3, "s")
    y_send(0, "yp", "s")
    y_send(0, "ym", "o")
    z_send(0, "zp", 0)
    z_send(0, "zm", 1)
    y_send(0, "yp", "o")
    y_send(0, "ym", "s")
    z_send(0, "zp", 1)
    z_send(0, "zm", 0)
    w_pair("ws0", 0, 0)
    send("xs", x_ref.at[half_of(other)], xb.at[chunk(0, c), place(0)], dc=1)
    for name in ORDER:
        if name == "PbA":
            left.extend(n for n in sites if n[:2] != "zv")
        tasks[name]()
    for name, copy in sites.items():
        if name not in left:
            copy.wait_send()
    arrived("t0", "t1", "t2")
    put_w.wait()
    put_x.wait()


def hand_on(a_ref, b_ref, a_out, b_out, a_buf, b_buf, sems):
    parts = [(b_ref.at[pl.ds(k * 96, 96)], b_buf.at[pl.ds(k * 96, 96)], b_out.at[pl.ds(k * 96, 96)]) for k in range(2)]
    parts.append((a_ref, a_buf, a_out))
    loads = [pltpu.make_async_copy(src, buf, sems.at[0, k]) for k, (src, buf, _) in enumerate(parts)]
    stores = [pltpu.make_async_copy(buf, dst, sems.at[1, k]) for k, (_, buf, dst) in enumerate(parts)]
    for copy in loads:
        copy.start()
    for load, store in zip(loads, stores):
        load.wait()
        store.start()
    for copy in stores:
        copy.wait()


def shards(activations, act_grad, up_weight, width_steps):
    any_space = pl.BlockSpec(memory_space=pl.ANY)

    def buffer(*shape):
        return pltpu.VMEM(shape, BF16)

    results = (
        jax.ShapeDtypeStruct((TOK, COLS), BF16),
        jax.ShapeDtypeStruct((ROWS, HID), BF16),
    )
    input_grad, weight_grad = pl.pallas_call(
        kernel,
        out_shape=results,
        in_specs=[any_space] * 4,
        out_specs=(any_space, any_space),
        scratch_shapes=[
            buffer(8, 4 * HALF, COLS),
            buffer(16 * ROWS, 2 * COLS),
            buffer(4 * HALF, 2 * COLS),
            buffer(TOK, HID),
            pltpu.VMEM((2, 128), jnp.int32),
            pltpu.VMEM((4 * HALF, 2 * COLS), F32),
            buffer(4 * HALF, 2 * COLS),
            buffer(2, 4, 2 * HALF, 2 * COLS),
            buffer(3, HALF, 2 * COLS),
            buffer(64, 2 * COLS),
            buffer(64, 2 * COLS),
            buffer(4, HALF, 2 * COLS),
            buffer(4, HALF, 2 * COLS),
            buffer(4, 2, HALF, COLS),
            buffer(3, 2, HALF, COLS),
            buffer(2, HALF, COLS),
            buffer(TOK, COLS),
            buffer(4, 2, 2, 384, COLS),
            buffer(4, 2, 384, COLS),
            buffer(4, 2, 384, COLS),
            buffer(384, COLS),
            buffer(384, COLS),
            buffer(2, 384, COLS),
            buffer(2, 384, COLS),
            buffer(4, ROWS, COLS),
            pltpu.SemaphoreType.DMA((N_SEM,)),
            pltpu.SemaphoreType.DMA((N_SEM,)),
            pltpu.SemaphoreType.DMA((4,)),
        ],
        compiler_params=pltpu.CompilerParams(
            collective_id=0, has_side_effects=True, vmem_limit_bytes=60 * 2**20
        ),
        cost_estimate=pl.CostEstimate(
            flops=3 * 2 * 512 * 3072 * 768, bytes_accessed=4 * 2**20, transcendentals=0
        ),
        name="elastic_up_backward",
    )(activations, act_grad, up_weight, width_steps.reshape(2, 128))
    return pl.pallas_call(
        hand_on,
        out_shape=results,
        in_specs=[any_space] * 2,
        out_specs=(any_space, any_space),
        scratch_shapes=[buffer(TOK, COLS), buffer(ROWS, HID), pltpu.SemaphoreType.DMA((2, 3))],
        compiler_params=pltpu.CompilerParams(vmem_limit_bytes=60 * 2**20),
        name="hand_on",
    )(input_grad, weight_grad)


def solution(mesh):
    placed = (P("dp", "tensor"), P("dp", "tensor"), P("dp", "tensor"), P("dp"))
    return jax.shard_map(
        shards,
        mesh=mesh,
        in_specs=placed,
        out_specs=(P("dp", "tensor"), P("dp", "tensor")),
        check_vma=False,
    )
```

```python
import jax
import jax.numpy as jnp
from jax import lax
from jax.experimental import pallas as pl
from jax.experimental.pallas import tpu as pltpu
from jax.sharding import PartitionSpec as P

MESH = pl.DeviceIdType.MESH
F32 = jnp.float32
BF16 = jnp.bfloat16
TOK = 256
HALF = 128
ROWS = 192
COLS = 384
HID = 1536
SCALE = 1.0 / 64.0
N_SEM = 176

STEP = (0, 1, 3, 2)
FROM = (0, 3, 1, 2)
PLACE = (2, 0, 1, 3)
SLOT = (0, 1, 3, 2)
SUB = (2, 1, 3, 0)

ORDER = (
    "mask", "wa2", "zfp0", "yfp0", "yfm0", "xa2", "zfm0", "xb1", "wb2", "wa1", "w2s", "g13", "xb2", "zdp0",
    "xa1", "wb1", "zfm2", "zfp2", "wa3", "zdm0", "zdp2", "xb3", "zl0", "yfm1", "xy1", "wb3", "xa3", "yfp2",
    "zfp1", "xy3", "zdm2", "zfm1", "zfp3", "zfm3", "zl2", "zdp1", "zdm1", "zdm3", "yfm3", "zdp3", "g2",
    "yfp3", "wr1", "zl1", "Pa0", "zl3", "PaA", "wr2", "PbA", "IA1", "IA3", "IA2", "Pb0", "Pb3", "D20", "IB2",
    "IA0", "D21", "E20", "D10", "IB3", "IB1", "D30", "E21", "D31", "D11", "E10", "R1", "E30", "D00", "D01",
    "E31", "E11", "Zc1", "R2", "Zd0", "Zc0", "Zc2", "E00", "sent", "Zd1", "Zd2", "Zd3", "IB0", "E01", "S0",
    "Zc3", "R3", "ZL0", "Vp", "Vm", "ZL1", "ZL2", "R0", "ZL3", "RF",
)

def kernel(
    x_ref, g_ref, w_ref, wid_ref, dx_ref, dw_ref,
    xb, wb, gb, gin, wid, acc, hid, sd, qb, vp, vm, ap, am, rb, xr, own, out,
    dwp, dwr, dws, zvp, zvm, zap, zam, tot, ssem, rsem, lsem,
):
    dp, tensor = lax.axis_index("dp"), lax.axis_index("tensor")
    z, x = lax.div(dp, 4), lax.rem(dp, 4)
    y, c = lax.div(tensor, 2), lax.rem(tensor, 2)
    other = 1 - c

    def ring(v, step):
        return lax.rem(v + step, 4)

    def device(dz=0, dx=0, dy=0, dc=0):
        return (
            ring(z, dz) * 4 + ring(x, dx),
            ring(y, dy) * 2 + (other if dc else c),
        )

    sites = {}

    def send(name, src, dst, **to):
        slot = len(sites)
        copy = pltpu.make_async_remote_copy(
            src_ref=src,
            dst_ref=dst,
            send_sem=ssem.at[slot],
            recv_sem=rsem.at[slot],
            device_id=device(**to),
            device_id_type=MESH,
        )
        copy.start()
        sites[name] = copy

    taken = set()

    def arrived(*names):
        for name in names:
            if name not in taken:
                taken.add(name)
                sites[name].wait_recv()

    def place(j):
        return pl.ds(PLACE[j] * HALF, HALF)

    def chunk(dy, core):
        return ring(y, dy) * 2 + core

    def half_of(core):
        return pl.ds(pl.multiple_of(core * HALF, HALF), HALF)

    def weight_rows(dz, dx):
        return pl.ds(pl.multiple_of(SLOT[dz] * 768 + ring(x, dx) * ROWS, ROWS), ROWS)

    def weight_half(dz, dx, half):
        start = SLOT[dz] * 768 + ring(x, dx) * ROWS + half * 96
        return pl.ds(pl.multiple_of(start, 96), 96)

    def sub_block(step):
        return pl.ds(pl.multiple_of(ring(x, step) * COLS, COLS), COLS)

    own_cols = pl.ds(pl.multiple_of(c * COLS, COLS), COLS)

    own_w = pltpu.make_async_copy(
        w_ref.at[:, sub_block(0)], wb.at[weight_rows(0, 0), own_cols], lsem.at[2]
    )
    own_x = pltpu.make_async_copy(
        x_ref.at[half_of(c)], xb.at[chunk(0, c), place(0)], lsem.at[1]
    )
    own_g = pltpu.make_async_copy(g_ref, gin, lsem.at[0])
    own_wid = pltpu.make_async_copy(wid_ref, wid, lsem.at[3])
    put_g = pltpu.make_async_copy(
        gin.at[half_of(c), sub_block(0)], gb.at[place(0), own_cols], lsem.at[0]
    )
    put_w = pltpu.make_async_copy(tot.at[3], dw_ref.at[:, sub_block(0)], lsem.at[1])
    put_x = pltpu.make_async_copy(out, dx_ref, lsem.at[2])

    partners = (
        dict(dx=1), dict(dx=3), dict(dx=2), dict(dy=1), dict(dy=3), dict(dz=1), dict(dz=3), dict(dc=1),
        dict(dx=1, dc=1), dict(dx=3, dc=1), dict(dx=2, dc=1), dict(dy=1, dc=1), dict(dy=3, dc=1),
    )
    barrier = pltpu.get_barrier_semaphore()
    for to in partners:
        pl.semaphore_signal(barrier, inc=1, device_id=device(**to), device_id_type=MESH)
    own_wid.start()
    own_g.start()
    own_x.start()
    own_w.start()
    pl.semaphore_wait(barrier, len(partners))

    tasks = {}

    def task(name, *args):
        def enter(step):
            tasks[name] = lambda: step(*args)
            return step

        return enter

    def x_send(step, kind):
        core, dc = (c, 0) if kind == "s" else (other, 1)
        j = FROM[STEP.index(step)]
        dst = xb.at[chunk(0, c), place(STEP.index(j))]
        send(f"x{step}{kind}", x_ref.at[half_of(core)], dst, dx=step, dc=dc)

    def y_send(j, name, kind):
        dy = 1 if name == "yp" else 3
        if j == 0:
            core, dc = (c, 0) if kind == "s" else (other, 1)
            send(f"{name}0{kind}", x_ref.at[half_of(core)], xb.at[chunk(0, c), place(0)], dy=dy, dc=dc)
        else:
            ref = xb.at[chunk(0, c if kind == "s" else other), place(j)]
            send(f"{name}{j}{kind}", ref, ref, dy=dy)

    def x_arrive(j, kind):
        if j < 3:
            arrived(f"x{FROM[j]}{kind}")
        else:
            arrived("xf1" if kind == "s" else "xf3")
        if j == 2 and kind == "s":
            at = chunk(0, c)
            send("xf1", xb.at[at, place(2)], xb.at[at, place(3)], dx=1)
        if j == 1 and kind == "o":
            at = chunk(0, other)
            send("xf3", xb.at[at, place(1)], xb.at[at, place(3)], dx=3)
        for name in ("yp", "ym") if kind == "s" else ("ym", "yp"):
            y_send(j, name, kind)

    @task("xy3")
    def across_back():
        arrived("yfp0")
        at = chunk(2, c)
        send("xy3s", xb.at[at, place(0)], xb.at[at, place(1)], dx=3)

    @task("xy1")
    def across_on():
        arrived("yfm0")
        at = chunk(2, other)
        send("xy1o", xb.at[at, place(0)], xb.at[at, place(2)], dx=1)

    def y_forward_up(j):
        arrived(f"yp{j}s")
        ref = xb.at[chunk(3, c), place(j)]
        send(f"yfp{j}", ref, ref, dy=1)

    def y_forward_down(j):
        arrived(f"ym{j}o")
        ref = xb.at[chunk(1, other), place(j)]
        send(f"yfm{j}", ref, ref, dy=3)

    def w_send(step, half):
        src = w_ref.at[pl.ds(half * 96, 96), sub_block(step)]
        dst = wb.at[weight_half(0, 0, half), own_cols]
        send(f"w{step}{'ab'[half]}", src, dst, dx=step)

    def z_send(j, name, half):
        to = 1 if name == "zp" else 3
        src = wb.at[weight_half(0, STEP[j], half), own_cols]
        if j == 0:
            src = w_ref.at[pl.ds(half * 96, 96), sub_block(0)]
        dst = wb.at[weight_half(4 - to, STEP[j], half), own_cols]
        send(f"{name}{j}{'ab'[half]}", src, dst, dz=to)

    def w_arrive(j, half):
        arrived(f"w{FROM[j]}{'ab'[half]}")
        for name in ("zm", "zp") if half else ("zp", "zm"):
            z_send(j, name, half)
        ref = wb.at[weight_half(0, STEP[j], half), own_cols]
        send(f"ws{'ab'[half]}{j}", ref, ref, dc=1)

    def w_pair(name, dz, j):
        dst = wb.at[weight_rows(dz, STEP[j]), own_cols]
        src = w_ref.at[:, sub_block(0)] if name == "ws0" else dst
        send(name, src, dst, dc=1)

    def z_forward_up(j):
        arrived(f"zp{j}a")
        src = wb.at[weight_half(3, STEP[j], 0), own_cols]
        send(f"zfp{j}", src, wb.at[weight_half(2, STEP[j], 0), own_cols], dz=1)

    def z_forward_down(j):
        arrived(f"zm{j}b")
        src = wb.at[weight_half(1, STEP[j], 1), own_cols]
        send(f"zfm{j}", src, wb.at[weight_half(2, STEP[j], 1), own_cols], dz=3)

    def z_whole_up(j):
        arrived(f"zp{j}b")
        w_pair(f"d1{j}", 3, j)

    def z_whole_down(j):
        arrived(f"zm{j}a")
        w_pair(f"d3{j}", 1, j)

    def z_across(j):
        arrived(f"zfp{j}", f"zfm{j}")
        w_pair(f"d2{j}", 2, j)

    @task("w2s")
    def w_across():
        w_send(2, 0)
        w_send(2, 1)

    @task("wr1")
    def weights_near():
        own_w.wait()
        for j in range(4):
            arrived(f"d1{j}", f"d3{j}")
            arrived(*((f"wsa{j}", f"wsb{j}") if j else ("ws0",)))

    @task("wr2")
    def weights_across():
        for j in range(4):
            arrived(f"d2{j}")

    def g_send(step, kind):
        core, dc = (c, 0) if kind == "s" else (other, 1)
        j = FROM[STEP.index(step)]
        dst = gb.at[place(STEP.index(j)), own_cols]
        send(f"g{step}{kind}", gin.at[half_of(core), sub_block(step)], dst, dx=step, dc=dc)

    @task("mask")
    def mask():
        own_wid.wait()
        own_g.wait()
        for half in range(2):
            rows = pl.ds(half * 128, 128)
            width = jnp.broadcast_to(wid[half : half + 1, :], (128, 128)).T
            keep = jnp.where(width > tensor, 1.0, 0.0).astype(BF16)
            for part in range(HID // 128):
                lanes = pl.ds(part * 128, 128)
                gin[rows, lanes] = gin[rows, lanes] * keep
        put_g.start()
        send("gs", gin.at[half_of(other), sub_block(0)], gb.at[place(0), own_cols], dc=1)

    @task("g13")
    def g_near():
        g_send(1, "s")
        g_send(3, "s")
        g_send(1, "o")
        g_send(3, "o")

    @task("g2")
    def g_across():
        g_send(2, "s")
        g_send(2, "o")

    for j in range(4):
        if j:
            task(f"xa{j}", j, "s")(x_arrive)
            task(f"xb{j}", j, "o")(x_arrive)
            task(f"wa{j}", j, 0)(w_arrive)
            task(f"wb{j}", j, 1)(w_arrive)
        task(f"yfp{j}", j)(y_forward_up)
        task(f"yfm{j}", j)(y_forward_down)
        task(f"zfp{j}", j)(z_forward_up)
        task(f"zfm{j}", j)(z_forward_down)
        task(f"zdp{j}", j)(z_whole_up)
        task(f"zdm{j}", j)(z_whole_down)
        task(f"zl{j}", j)(z_across)

    def features(dz, rows):
        return [xb[ring(z, dz) * 2 + h, rows, :] for h in range(2)]

    def batch(places):
        return pl.ds(PLACE[places[0]] * HALF, HALF * len(places))

    def tokens_ready(*places):
        for j in places:
            arrived(f"yp{j}o", f"ym{j}s")
            if j == 1:
                arrived("yp1s", "xy3s")
            else:
                arrived(f"yfp{j}")
            if j == 2:
                arrived("ym2o", "xy1o")
            else:
                arrived(f"yfm{j}")
            if j == 0:
                own_x.wait()
                arrived("xs")

    def hidden_near(*places):
        tokens_ready(*places)
        rows = batch(places)
        part = jnp.concatenate(features(0, rows) + features(1, rows) + features(3, rows), axis=1)
        acc[rows, :] = jnp.dot(part, wb[pl.ds(0, 2304), :], preferred_element_type=F32)

    def hidden_last(*places):
        for j in places:
            if j == 0:
                put_g.wait()
                arrived("gs")
            else:
                arrived(f"g{FROM[j]}s", f"g{FROM[j]}o")
        rows = batch(places)
        if places == (3,):
            tokens_ready(3)
            part = jnp.concatenate(sum((features(d, rows) for d in (0, 1, 3, 2)), []), axis=1)
            preact = jnp.dot(part, wb[...], preferred_element_type=F32)
        else:
            part = jnp.concatenate(features(2, rows), axis=1)
            preact = acc[rows, :] + jnp.dot(part, wb[pl.ds(2304, 768), :], preferred_element_type=F32)
        slope = 2.0 * jnp.maximum(preact, 0.0)
        hid[rows, :] = (gb[rows, :].astype(F32) * slope).astype(BF16)

    for name, places in (("A", (1, 2)), ("0", (0,)), ("3", (3,))):
        if name != "3":
            task("Pa" + name, *places)(hidden_near)
        task("Pb" + name, *places)(hidden_last)

    first, second = pl.ds(0, 128), pl.ds(128, 128)
    upper, lower = pl.ds(0, 64), pl.ds(64, 64)

    def input_part(b, d):
        dz = lax.rem(y + d - z + 4, 4)
        slot = dz + lax.div(dz, 2) - 2 * lax.div(dz, 3)
        rows = pl.ds(pl.multiple_of(slot * 768, 768), 768)
        sd[b, d] = lax.dot_general(
            hid[pl.ds(b * 256, 256), :], wb[rows, :], (((1,), (1,)), ((), ())), preferred_element_type=F32
        ).astype(BF16)
        if d == 2 and b == 0:
            send("q1", sd.at[0, 2, first], qb.at[0], dx=1)
            send("q3", sd.at[0, 2, second], qb.at[1], dx=3)
        elif d == 2:
            send("q2", sd.at[1, 2, second], qb.at[2], dx=2)
        elif d == 1 and b == 0:
            send("a11", sd.at[0, 1, first], ap.at[0], dy=1)
            send("a12", sd.at[0, 1, second], ap.at[1], dy=1)
        elif d == 3 and b == 0:
            send("a31", sd.at[0, 3, first], am.at[0], dy=3)
            send("a32", sd.at[0, 3, second], am.at[1], dy=3)
        elif d == 1:
            send("a13", sd.at[1, 1, second], ap.at[3], dy=1)
            send("a10l", sd.at[1, 1, lower], ap.at[2, lower], dy=1)
        elif d == 3:
            send("a33", sd.at[1, 3, second], am.at[3], dy=3)
            send("a30t", sd.at[1, 3, upper], am.at[2, upper], dy=3)

    for b in range(2):
        for d in range(4):
            task(f"I{'AB'[b]}{d}", b, d)(input_part)

    @task("S0")
    def across_total():
        arrived("q1", "q3", "q2")
        total = sd[1, 2, first].astype(F32)
        for slot in range(3):
            total = total + qb[slot].astype(F32)
        sd[1, 2, first] = total.astype(BF16)
        send("vp", sd.at[1, 2, upper], vp, dy=1)
        send("vm", sd.at[1, 2, lower], vm, dy=3)

    @task("Vp")
    def via_up():
        arrived("vp")
        sd[1, 1, upper] = (sd[1, 1, upper].astype(F32) + vp[...].astype(F32)).astype(BF16)
        send("a10t", sd.at[1, 1, upper], ap.at[2, upper], dy=1)

    @task("Vm")
    def via_down():
        arrived("vm")
        sd[1, 3, lower] = (sd[1, 3, lower].astype(F32) + vm[...].astype(F32)).astype(BF16)
        send("a30l", sd.at[1, 3, lower], am.at[2, lower], dy=3)

    def input_total(j):
        if j == 0:
            arrived("a10l", "a10t", "a30t", "a30l")
        else:
            arrived(f"a1{j}", f"a3{j}")
        at, rows = PLACE[j], (first, second)[PLACE[j] % 2]
        total = sd[at // 2, 0, rows].astype(F32) + ap[at].astype(F32) + am[at].astype(F32)
        total = total.astype(BF16)
        rb[at, 0] = total[:, :COLS]
        rb[at, 1] = total[:, COLS:]
        if j == 0:
            own[c] = rb[at, c]
            send("xro", rb.at[at, other], own.at[c], dc=1)
        else:
            step = STEP[j]
            send(f"xr{step}s", rb.at[at, c], xr.at[step - 1, c], dx=step)
            send(f"xr{step}o", rb.at[at, other], xr.at[step - 1, c], dx=step, dc=1)

    for j in range(4):
        task(f"R{j}", j)(input_total)

    @task("RF")
    def input_final():
        arrived("xr1s", "xr1o", "xr3s", "xr3o", "xr2s", "xr2o", "xro")
        for half in range(2):
            total = own[half].astype(F32)
            for slot in range(3):
                total = total + xr[slot, half].astype(F32)
            out[pl.ds(half * HALF, HALF), :] = total.astype(BF16)
        put_x.start()

    def weight_part(d, h):
        part = lax.dot_general(
            xb[ring(z, d) * 2 + h], hid[...], (((0,), (0,)), ((), ())), preferred_element_type=F32
        ).astype(BF16)
        dwp[d, h, 0] = part[:, :COLS]
        dwp[d, h, 1] = part[:, COLS:]
        send(f"e{d}{h}", dwp.at[d, h, other], dwr.at[d, h], dc=1)

    def weight_pair(d, h):
        arrived(f"e{d}{h}")
        total = (dwp[d, h, c].astype(F32) + dwr[d, h].astype(F32)).astype(BF16)
        for p in range(2):
            step = lax.rem(h * 2 + p - x + 4, 4)
            at = lax.rem(lax.rem(3 * step + 3, 5), 4)
            rows = pl.ds(pl.multiple_of(at * 96, 96), 96)
            dws[d, 0, rows] = total[p * ROWS : p * ROWS + 96]
            dws[d, 1, rows] = total[p * ROWS + 96 : p * ROWS + ROWS]
            if d == 2:
                via_copy("zvp", at, rows).start()
                via_copy("zvm", at, rows).start()

    for d in range(4):
        for h in range(2):
            task(f"D{d}{h}", d, h)(weight_part)
            task(f"E{d}{h}", d, h)(weight_pair)

    def sub_rows(q):
        return pl.ds(q * 96, 96)

    via_slots = {}

    def via_copy(name, at, rows):
        up = name == "zvp"
        return pltpu.make_async_remote_copy(
            src_ref=dws.at[2, 0 if up else 1, rows],
            dst_ref=(zvp if up else zvm).at[rows],
            send_sem=ssem.at[via_slots[name] + at],
            recv_sem=rsem.at[via_slots[name] + at],
            device_id=device(dz=1 if up else 3),
            device_id_type=MESH,
        )

    for name in ("zvp", "zvm"):
        via_slots[name] = len(sites)
        for q in range(4):
            sites[f"{name}{q}"] = via_copy(name, q, sub_rows(q))

    def weight_direct(q):
        rows = sub_rows(q)
        send(f"zdp{q}", dws.at[1, 1, rows], zap.at[1, rows], dz=1)
        send(f"zdm{q}", dws.at[3, 0, rows], zam.at[0, rows], dz=3)

    def weight_via(q):
        arrived(f"zvp{q}", f"zvm{q}")
        rows = sub_rows(q)
        dws[1, 0, rows] = (dws[1, 0, rows].astype(F32) + zvp[rows].astype(F32)).astype(BF16)
        send(f"zcp{q}", dws.at[1, 0, rows], zap.at[0, rows], dz=1)
        dws[3, 1, rows] = (dws[3, 1, rows].astype(F32) + zvm[rows].astype(F32)).astype(BF16)
        send(f"zcm{q}", dws.at[3, 1, rows], zam.at[1, rows], dz=3)

    def weight_last(q):
        arrived(f"zdp{q}", f"zdm{q}", f"zcp{q}", f"zcm{q}")
        rows = sub_rows(q)
        for half in range(2):
            total = (
                dws[0, half, rows].astype(F32) + zap[half, rows].astype(F32) + zam[half, rows].astype(F32)
            )
            tot[q, pl.ds(half * 96, 96)] = (total * SCALE).astype(BF16)
        if q < 3:
            send(f"t{q}", tot.at[q], dw_ref.at[:, sub_block(0)], dx=SUB[q])
        else:
            put_w.start()

    for q in range(4):
        task(f"Zd{q}", q)(weight_direct)
        task(f"Zc{q}", q)(weight_via)
        task(f"ZL{q}", q)(weight_last)

    left = []

    @task("sent")
    def early_sends():
        for name in left:
            sites[name].wait_send()

    w_send(1, 0)
    w_send(3, 1)
    x_send(1, "s")
    x_send(3, "o")
    w_send(1, 1)
    w_send(3, 0)
    x_send(1, "o")
    x_send(3, "s")
    y_send(0, "yp", "s")
    y_send(0, "ym", "o")
    z_send(0, "zp", 0)
    z_send(0, "zm", 1)
    y_send(0, "yp", "o")
    y_send(0, "ym", "s")
    z_send(0, "zp", 1)
    z_send(0, "zm", 0)
    w_pair("ws0", 0, 0)
    send("xs", x_ref.at[half_of(other)], xb.at[chunk(0, c), place(0)], dc=1)
    for name in ORDER:
        if name == "PbA":
            left.extend(n for n in sites if n[:2] != "zv")
        tasks[name]()
    for name, copy in sites.items():
        if name not in left:
            copy.wait_send()
    arrived("t0", "t1", "t2")
    put_w.wait()
    put_x.wait()


def hand_on(a_ref, b_ref, a_out, b_out, a_buf, b_buf, sems):
    parts = [(b_ref.at[pl.ds(k * 96, 96)], b_buf.at[pl.ds(k * 96, 96)], b_out.at[pl.ds(k * 96, 96)]) for k in range(2)]
    parts.append((a_ref, a_buf, a_out))
    loads = [pltpu.make_async_copy(src, buf, sems.at[0, k]) for k, (src, buf, _) in enumerate(parts)]
    stores = [pltpu.make_async_copy(buf, dst, sems.at[1, k]) for k, (_, buf, dst) in enumerate(parts)]
    for copy in loads:
        copy.start()
    for load, store in zip(loads, stores):
        load.wait()
        store.start()
    for copy in stores:
        copy.wait()


def shards(activations, act_grad, up_weight, width_steps):
    any_space = pl.BlockSpec(memory_space=pl.ANY)

    def buffer(*shape):
        return pltpu.VMEM(shape, BF16)

    results = (
        jax.ShapeDtypeStruct((TOK, COLS), BF16),
        jax.ShapeDtypeStruct((ROWS, HID), BF16),
    )
    input_grad, weight_grad = pl.pallas_call(
        kernel,
        out_shape=results,
        in_specs=[any_space] * 4,
        out_specs=(any_space, any_space),
        scratch_shapes=[
            buffer(8, 4 * HALF, COLS),
            buffer(16 * ROWS, 2 * COLS),
            buffer(4 * HALF, 2 * COLS),
            buffer(TOK, HID),
            pltpu.VMEM((2, 128), jnp.int32),
            pltpu.VMEM((4 * HALF, 2 * COLS), F32),
            buffer(4 * HALF, 2 * COLS),
            buffer(2, 4, 2 * HALF, 2 * COLS),
            buffer(3, HALF, 2 * COLS),
            buffer(64, 2 * COLS),
            buffer(64, 2 * COLS),
            buffer(4, HALF, 2 * COLS),
            buffer(4, HALF, 2 * COLS),
            buffer(4, 2, HALF, COLS),
            buffer(3, 2, HALF, COLS),
            buffer(2, HALF, COLS),
            buffer(TOK, COLS),
            buffer(4, 2, 2, 384, COLS),
            buffer(4, 2, 384, COLS),
            buffer(4, 2, 384, COLS),
            buffer(384, COLS),
            buffer(384, COLS),
            buffer(2, 384, COLS),
            buffer(2, 384, COLS),
            buffer(4, ROWS, COLS),
            pltpu.SemaphoreType.DMA((N_SEM,)),
            pltpu.SemaphoreType.DMA((N_SEM,)),
            pltpu.SemaphoreType.DMA((4,)),
        ],
        compiler_params=pltpu.CompilerParams(
            collective_id=0, has_side_effects=True, vmem_limit_bytes=60 * 2**20
        ),
        cost_estimate=pl.CostEstimate(
            flops=3 * 2 * 512 * 3072 * 768, bytes_accessed=4 * 2**20, transcendentals=0
        ),
        name="elastic_up_backward",
    )(activations, act_grad, up_weight, width_steps.reshape(2, 128))
    return pl.pallas_call(
        hand_on,
        out_shape=results,
        in_specs=[any_space] * 2,
        out_specs=(any_space, any_space),
        scratch_shapes=[buffer(TOK, COLS), buffer(ROWS, HID), pltpu.SemaphoreType.DMA((2, 3))],
        compiler_params=pltpu.CompilerParams(vmem_limit_bytes=60 * 2**20),
        name="hand_on",
    )(input_grad, weight_grad)


def solution(mesh):
    placed = (P("dp", "tensor"), P("dp", "tensor"), P("dp", "tensor"), P("dp"))
    return jax.shard_map(
        shards,
        mesh=mesh,
        in_specs=placed,
        out_specs=(P("dp", "tensor"), P("dp", "tensor")),
        check_vma=False,
    )
```

```python
import jax
import jax.numpy as jnp
from jax import lax
from jax.experimental import pallas as pl
from jax.experimental.pallas import tpu as pltpu
from jax.sharding import PartitionSpec as P

MESH = pl.DeviceIdType.MESH
F32 = jnp.float32
BF16 = jnp.bfloat16
TOK = 256
HALF = 128
ROWS = 192
COLS = 384
HID = 1536
SCALE = 1.0 / 64.0
N_SEM = 176

STEP = (0, 1, 3, 2)
FROM = (0, 3, 1, 2)
PLACE = (2, 0, 1, 3)
SLOT = (0, 1, 3, 2)
SUB = (2, 1, 3, 0)

ORDER = (
    "mask", "wa2", "zfp0", "yfp0", "yfm0", "xa2", "zfm0", "xb1", "wb2", "wa1", "w2s", "g13", "xb2", "zdp0",
    "xa1", "wb1", "zfm2", "zfp2", "wa3", "zdm0", "zdp2", "xb3", "zl0", "yfm1", "xy1", "wb3", "xa3", "yfp2",
    "zfp1", "xy3", "zdm2", "zfm1", "zfp3", "zfm3", "zl2", "zdp1", "zdm1", "zdm3", "yfm3", "zdp3", "g2",
    "yfp3", "wr1", "zl1", "Pa0", "zl3", "PaA", "wr2", "PbA", "IA1", "IA3", "Pb0", "Pb3", "D20", "IB2",
    "IA2", "IA0", "D21", "E20", "D10", "IB3", "IB1", "D30", "E21", "D31", "D11", "E10", "R1", "E30", "D00",
    "D01", "E31", "E11", "Zc1", "R2", "Zd0", "Zc0", "Zc2", "E00", "Zd1", "Zd2", "Zd3", "IB0", "E01",
    "S0", "Zc3", "R3", "sent", "ZL0", "Vp", "Vm", "ZL1", "ZL2", "R0", "ZL3", "RF",
)

def kernel(
    x_ref, g_ref, w_ref, wid_ref, dx_ref, dw_ref,
    xb, wb, gb, gin, wid, acc, hid, sd, qb, vp, vm, ap, am, rb, xr, own, out,
    dwp, dwr, dws, zvp, zvm, zap, zam, tot, ssem, rsem, lsem,
):
    dp, tensor = lax.axis_index("dp"), lax.axis_index("tensor")
    z, x = lax.div(dp, 4), lax.rem(dp, 4)
    y, c = lax.div(tensor, 2), lax.rem(tensor, 2)
    other = 1 - c

    def ring(v, step):
        return lax.rem(v + step, 4)

    def device(dz=0, dx=0, dy=0, dc=0):
        return (
            ring(z, dz) * 4 + ring(x, dx),
            ring(y, dy) * 2 + (other if dc else c),
        )

    sites = {}

    def send(name, src, dst, **to):
        slot = len(sites)
        copy = pltpu.make_async_remote_copy(
            src_ref=src,
            dst_ref=dst,
            send_sem=ssem.at[slot],
            recv_sem=rsem.at[slot],
            device_id=device(**to),
            device_id_type=MESH,
        )
        copy.start()
        sites[name] = copy

    taken = set()

    def arrived(*names):
        for name in names:
            if name not in taken:
                taken.add(name)
                sites[name].wait_recv()

    def place(j):
        return pl.ds(PLACE[j] * HALF, HALF)

    def chunk(dy, core):
        return ring(y, dy) * 2 + core

    def half_of(core):
        return pl.ds(pl.multiple_of(core * HALF, HALF), HALF)

    def weight_rows(dz, dx):
        return pl.ds(pl.multiple_of(SLOT[dz] * 768 + ring(x, dx) * ROWS, ROWS), ROWS)

    def weight_half(dz, dx, half):
        start = SLOT[dz] * 768 + ring(x, dx) * ROWS + half * 96
        return pl.ds(pl.multiple_of(start, 96), 96)

    def sub_block(step):
        return pl.ds(pl.multiple_of(ring(x, step) * COLS, COLS), COLS)

    own_cols = pl.ds(pl.multiple_of(c * COLS, COLS), COLS)

    own_w = pltpu.make_async_copy(
        w_ref.at[:, sub_block(0)], wb.at[weight_rows(0, 0), own_cols], lsem.at[2]
    )
    own_x = pltpu.make_async_copy(
        x_ref.at[half_of(c)], xb.at[chunk(0, c), place(0)], lsem.at[1]
    )
    own_g = pltpu.make_async_copy(g_ref, gin, lsem.at[0])
    own_wid = pltpu.make_async_copy(wid_ref, wid, lsem.at[3])
    put_g = pltpu.make_async_copy(
        gin.at[half_of(c), sub_block(0)], gb.at[place(0), own_cols], lsem.at[0]
    )
    put_w = pltpu.make_async_copy(tot.at[3], dw_ref.at[:, sub_block(0)], lsem.at[1])
    put_x = pltpu.make_async_copy(out, dx_ref, lsem.at[2])

    partners = (
        dict(dx=1), dict(dx=3), dict(dx=2), dict(dy=1), dict(dy=3), dict(dz=1), dict(dz=3), dict(dc=1),
        dict(dx=1, dc=1), dict(dx=3, dc=1), dict(dx=2, dc=1), dict(dy=1, dc=1), dict(dy=3, dc=1),
    )
    barrier = pltpu.get_barrier_semaphore()
    for to in partners:
        pl.semaphore_signal(barrier, inc=1, device_id=device(**to), device_id_type=MESH)
    own_wid.start()
    own_g.start()
    own_x.start()
    own_w.start()
    pl.semaphore_wait(barrier, len(partners))

    tasks = {}

    def task(name, *args):
        def enter(step):
            tasks[name] = lambda: step(*args)
            return step

        return enter

    def x_send(step, kind):
        core, dc = (c, 0) if kind == "s" else (other, 1)
        j = FROM[STEP.index(step)]
        dst = xb.at[chunk(0, c), place(STEP.index(j))]
        send(f"x{step}{kind}", x_ref.at[half_of(core)], dst, dx=step, dc=dc)

    def y_send(j, name, kind):
        dy = 1 if name == "yp" else 3
        if j == 0:
            core, dc = (c, 0) if kind == "s" else (other, 1)
            send(f"{name}0{kind}", x_ref.at[half_of(core)], xb.at[chunk(0, c), place(0)], dy=dy, dc=dc)
        else:
            ref = xb.at[chunk(0, c if kind == "s" else other), place(j)]
            send(f"{name}{j}{kind}", ref, ref, dy=dy)

    def x_arrive(j, kind):
        if j < 3:
            arrived(f"x{FROM[j]}{kind}")
        else:
            arrived("xf1" if kind == "s" else "xf3")
        if j == 2 and kind == "s":
            at = chunk(0, c)
            send("xf1", xb.at[at, place(2)], xb.at[at, place(3)], dx=1)
        if j == 1 and kind == "o":
            at = chunk(0, other)
            send("xf3", xb.at[at, place(1)], xb.at[at, place(3)], dx=3)
        for name in ("yp", "ym") if kind == "s" else ("ym", "yp"):
            y_send(j, name, kind)

    @task("xy3")
    def across_back():
        arrived("yfp0")
        at = chunk(2, c)
        send("xy3s", xb.at[at, place(0)], xb.at[at, place(1)], dx=3)

    @task("xy1")
    def across_on():
        arrived("yfm0")
        at = chunk(2, other)
        send("xy1o", xb.at[at, place(0)], xb.at[at, place(2)], dx=1)

    def y_forward_up(j):
        arrived(f"yp{j}s")
        ref = xb.at[chunk(3, c), place(j)]
        send(f"yfp{j}", ref, ref, dy=1)

    def y_forward_down(j):
        arrived(f"ym{j}o")
        ref = xb.at[chunk(1, other), place(j)]
        send(f"yfm{j}", ref, ref, dy=3)

    def w_send(step, half):
        src = w_ref.at[pl.ds(half * 96, 96), sub_block(step)]
        dst = wb.at[weight_half(0, 0, half), own_cols]
        send(f"w{step}{'ab'[half]}", src, dst, dx=step)

    def z_send(j, name, half):
        to = 1 if name == "zp" else 3
        src = wb.at[weight_half(0, STEP[j], half), own_cols]
        if j == 0:
            src = w_ref.at[pl.ds(half * 96, 96), sub_block(0)]
        dst = wb.at[weight_half(4 - to, STEP[j], half), own_cols]
        send(f"{name}{j}{'ab'[half]}", src, dst, dz=to)

    def w_arrive(j, half):
        arrived(f"w{FROM[j]}{'ab'[half]}")
        for name in ("zm", "zp") if half else ("zp", "zm"):
            z_send(j, name, half)
        ref = wb.at[weight_half(0, STEP[j], half), own_cols]
        send(f"ws{'ab'[half]}{j}", ref, ref, dc=1)

    def w_pair(name, dz, j):
        dst = wb.at[weight_rows(dz, STEP[j]), own_cols]
        src = w_ref.at[:, sub_block(0)] if name == "ws0" else dst
        send(name, src, dst, dc=1)

    def z_forward_up(j):
        arrived(f"zp{j}a")
        src = wb.at[weight_half(3, STEP[j], 0), own_cols]
        send(f"zfp{j}", src, wb.at[weight_half(2, STEP[j], 0), own_cols], dz=1)

    def z_forward_down(j):
        arrived(f"zm{j}b")
        src = wb.at[weight_half(1, STEP[j], 1), own_cols]
        send(f"zfm{j}", src, wb.at[weight_half(2, STEP[j], 1), own_cols], dz=3)

    def z_whole_up(j):
        arrived(f"zp{j}b")
        w_pair(f"d1{j}", 3, j)

    def z_whole_down(j):
        arrived(f"zm{j}a")
        w_pair(f"d3{j}", 1, j)

    def z_across(j):
        arrived(f"zfp{j}", f"zfm{j}")
        w_pair(f"d2{j}", 2, j)

    @task("w2s")
    def w_across():
        w_send(2, 0)
        w_send(2, 1)

    @task("wr1")
    def weights_near():
        own_w.wait()
        for j in range(4):
            arrived(f"d1{j}", f"d3{j}")
            arrived(*((f"wsa{j}", f"wsb{j}") if j else ("ws0",)))

    @task("wr2")
    def weights_across():
        for j in range(4):
            arrived(f"d2{j}")

    def g_send(step, kind):
        core, dc = (c, 0) if kind == "s" else (other, 1)
        j = FROM[STEP.index(step)]
        dst = gb.at[place(STEP.index(j)), own_cols]
        send(f"g{step}{kind}", gin.at[half_of(core), sub_block(step)], dst, dx=step, dc=dc)

    @task("mask")
    def mask():
        own_wid.wait()
        own_g.wait()
        for half in range(2):
            rows = pl.ds(half * 128, 128)
            width = jnp.broadcast_to(wid[half : half + 1, :], (128, 128)).T
            keep = jnp.where(width > tensor, 1.0, 0.0).astype(BF16)
            for part in range(HID // 128):
                lanes = pl.ds(part * 128, 128)
                gin[rows, lanes] = gin[rows, lanes] * keep
        put_g.start()
        send("gs", gin.at[half_of(other), sub_block(0)], gb.at[place(0), own_cols], dc=1)

    @task("g13")
    def g_near():
        g_send(1, "s")
        g_send(3, "s")
        g_send(1, "o")
        g_send(3, "o")

    @task("g2")
    def g_across():
        g_send(2, "s")
        g_send(2, "o")

    for j in range(4):
        if j:
            task(f"xa{j}", j, "s")(x_arrive)
            task(f"xb{j}", j, "o")(x_arrive)
            task(f"wa{j}", j, 0)(w_arrive)
            task(f"wb{j}", j, 1)(w_arrive)
        task(f"yfp{j}", j)(y_forward_up)
        task(f"yfm{j}", j)(y_forward_down)
        task(f"zfp{j}", j)(z_forward_up)
        task(f"zfm{j}", j)(z_forward_down)
        task(f"zdp{j}", j)(z_whole_up)
        task(f"zdm{j}", j)(z_whole_down)
        task(f"zl{j}", j)(z_across)

    def features(dz, rows):
        return [xb[ring(z, dz) * 2 + h, rows, :] for h in range(2)]

    def batch(places):
        return pl.ds(PLACE[places[0]] * HALF, HALF * len(places))

    def tokens_ready(*places):
        for j in places:
            arrived(f"yp{j}o", f"ym{j}s")
            if j == 1:
                arrived("yp1s", "xy3s")
            else:
                arrived(f"yfp{j}")
            if j == 2:
                arrived("ym2o", "xy1o")
            else:
                arrived(f"yfm{j}")
            if j == 0:
                own_x.wait()
                arrived("xs")

    def hidden_near(*places):
        tokens_ready(*places)
        rows = batch(places)
        part = jnp.concatenate(features(0, rows) + features(1, rows) + features(3, rows), axis=1)
        acc[rows, :] = jnp.dot(part, wb[pl.ds(0, 2304), :], preferred_element_type=F32)

    def hidden_last(*places):
        for j in places:
            if j == 0:
                put_g.wait()
                arrived("gs")
            else:
                arrived(f"g{FROM[j]}s", f"g{FROM[j]}o")
        rows = batch(places)
        if places == (3,):
            tokens_ready(3)
            part = jnp.concatenate(sum((features(d, rows) for d in (0, 1, 3, 2)), []), axis=1)
            preact = jnp.dot(part, wb[...], preferred_element_type=F32)
        else:
            part = jnp.concatenate(features(2, rows), axis=1)
            preact = acc[rows, :] + jnp.dot(part, wb[pl.ds(2304, 768), :], preferred_element_type=F32)
        slope = 2.0 * jnp.maximum(preact, 0.0)
        hid[rows, :] = (gb[rows, :].astype(F32) * slope).astype(BF16)

    for name, places in (("A", (1, 2)), ("0", (0,)), ("3", (3,))):
        if name != "3":
            task("Pa" + name, *places)(hidden_near)
        task("Pb" + name, *places)(hidden_last)

    first, second = pl.ds(0, 128), pl.ds(128, 128)
    upper, lower = pl.ds(0, 64), pl.ds(64, 64)

    def input_part(b, d):
        dz = lax.rem(y + d - z + 4, 4)
        slot = dz + lax.div(dz, 2) - 2 * lax.div(dz, 3)
        rows = pl.ds(pl.multiple_of(slot * 768, 768), 768)
        sd[b, d] = lax.dot_general(
            hid[pl.ds(b * 256, 256), :], wb[rows, :], (((1,), (1,)), ((), ())), preferred_element_type=F32
        ).astype(BF16)
        if d == 2 and b == 0:
            send("q1", sd.at[0, 2, first], qb.at[0], dx=1)
            send("q3", sd.at[0, 2, second], qb.at[1], dx=3)
        elif d == 2:
            send("q2", sd.at[1, 2, second], qb.at[2], dx=2)
        elif d == 1 and b == 0:
            send("a11", sd.at[0, 1, first], ap.at[0], dy=1)
            send("a12", sd.at[0, 1, second], ap.at[1], dy=1)
        elif d == 3 and b == 0:
            send("a31", sd.at[0, 3, first], am.at[0], dy=3)
            send("a32", sd.at[0, 3, second], am.at[1], dy=3)
        elif d == 1:
            send("a13", sd.at[1, 1, second], ap.at[3], dy=1)
            send("a10l", sd.at[1, 1, lower], ap.at[2, lower], dy=1)
        elif d == 3:
            send("a33", sd.at[1, 3, second], am.at[3], dy=3)
            send("a30t", sd.at[1, 3, upper], am.at[2, upper], dy=3)

    for b in range(2):
        for d in range(4):
            task(f"I{'AB'[b]}{d}", b, d)(input_part)

    @task("S0")
    def across_total():
        arrived("q1", "q3", "q2")
        total = sd[1, 2, first].astype(F32)
        for slot in range(3):
            total = total + qb[slot].astype(F32)
        sd[1, 2, first] = total.astype(BF16)
        send("vp", sd.at[1, 2, upper], vp, dy=1)
        send("vm", sd.at[1, 2, lower], vm, dy=3)

    @task("Vp")
    def via_up():
        arrived("vp")
        sd[1, 1, upper] = (sd[1, 1, upper].astype(F32) + vp[...].astype(F32)).astype(BF16)
        send("a10t", sd.at[1, 1, upper], ap.at[2, upper], dy=1)

    @task("Vm")
    def via_down():
        arrived("vm")
        sd[1, 3, lower] = (sd[1, 3, lower].astype(F32) + vm[...].astype(F32)).astype(BF16)
        send("a30l", sd.at[1, 3, lower], am.at[2, lower], dy=3)

    def input_total(j):
        if j == 0:
            arrived("a10l", "a10t", "a30t", "a30l")
        else:
            arrived(f"a1{j}", f"a3{j}")
        at, rows = PLACE[j], (first, second)[PLACE[j] % 2]
        total = sd[at // 2, 0, rows].astype(F32) + ap[at].astype(F32) + am[at].astype(F32)
        total = total.astype(BF16)
        rb[at, 0] = total[:, :COLS]
        rb[at, 1] = total[:, COLS:]
        if j == 0:
            own[c] = rb[at, c]
            send("xro", rb.at[at, other], own.at[c], dc=1)
        else:
            step = STEP[j]
            send(f"xr{step}s", rb.at[at, c], xr.at[step - 1, c], dx=step)
            send(f"xr{step}o", rb.at[at, other], xr.at[step - 1, c], dx=step, dc=1)

    for j in range(4):
        task(f"R{j}", j)(input_total)

    @task("RF")
    def input_final():
        arrived("xr1s", "xr1o", "xr3s", "xr3o", "xr2s", "xr2o", "xro")
        for half in range(2):
            total = own[half].astype(F32)
            for slot in range(3):
                total = total + xr[slot, half].astype(F32)
            out[pl.ds(half * HALF, HALF), :] = total.astype(BF16)
        put_x.start()

    def weight_part(d, h):
        part = lax.dot_general(
            xb[ring(z, d) * 2 + h], hid[...], (((0,), (0,)), ((), ())), preferred_element_type=F32
        ).astype(BF16)
        dwp[d, h, 0] = part[:, :COLS]
        dwp[d, h, 1] = part[:, COLS:]
        send(f"e{d}{h}", dwp.at[d, h, other], dwr.at[d, h], dc=1)

    def weight_pair(d, h):
        arrived(f"e{d}{h}")
        total = (dwp[d, h, c].astype(F32) + dwr[d, h].astype(F32)).astype(BF16)
        for p in range(2):
            step = lax.rem(h * 2 + p - x + 4, 4)
            at = lax.rem(lax.rem(3 * step + 3, 5), 4)
            rows = pl.ds(pl.multiple_of(at * 96, 96), 96)
            dws[d, 0, rows] = total[p * ROWS : p * ROWS + 96]
            dws[d, 1, rows] = total[p * ROWS + 96 : p * ROWS + ROWS]
            if d == 2:
                via_copy("zvp", at, rows).start()
                via_copy("zvm", at, rows).start()

    for d in range(4):
        for h in range(2):
            task(f"D{d}{h}", d, h)(weight_part)
            task(f"E{d}{h}", d, h)(weight_pair)

    def sub_rows(q):
        return pl.ds(q * 96, 96)

    via_slots = {}

    def via_copy(name, at, rows):
        up = name == "zvp"
        return pltpu.make_async_remote_copy(
            src_ref=dws.at[2, 0 if up else 1, rows],
            dst_ref=(zvp if up else zvm).at[rows],
            send_sem=ssem.at[via_slots[name] + at],
            recv_sem=rsem.at[via_slots[name] + at],
            device_id=device(dz=1 if up else 3),
            device_id_type=MESH,
        )

    for name in ("zvp", "zvm"):
        via_slots[name] = len(sites)
        for q in range(4):
            sites[f"{name}{q}"] = via_copy(name, q, sub_rows(q))

    def weight_direct(q):
        rows = sub_rows(q)
        send(f"zdp{q}", dws.at[1, 1, rows], zap.at[1, rows], dz=1)
        send(f"zdm{q}", dws.at[3, 0, rows], zam.at[0, rows], dz=3)

    def weight_via(q):
        arrived(f"zvp{q}", f"zvm{q}")
        rows = sub_rows(q)
        dws[1, 0, rows] = (dws[1, 0, rows].astype(F32) + zvp[rows].astype(F32)).astype(BF16)
        send(f"zcp{q}", dws.at[1, 0, rows], zap.at[0, rows], dz=1)
        dws[3, 1, rows] = (dws[3, 1, rows].astype(F32) + zvm[rows].astype(F32)).astype(BF16)
        send(f"zcm{q}", dws.at[3, 1, rows], zam.at[1, rows], dz=3)

    def weight_last(q):
        arrived(f"zdp{q}", f"zdm{q}", f"zcp{q}", f"zcm{q}")
        rows = sub_rows(q)
        for half in range(2):
            total = (
                dws[0, half, rows].astype(F32) + zap[half, rows].astype(F32) + zam[half, rows].astype(F32)
            )
            tot[q, pl.ds(half * 96, 96)] = (total * SCALE).astype(BF16)
        if q < 3:
            send(f"t{q}", tot.at[q], dw_ref.at[:, sub_block(0)], dx=SUB[q])
        else:
            put_w.start()

    for q in range(4):
        task(f"Zd{q}", q)(weight_direct)
        task(f"Zc{q}", q)(weight_via)
        task(f"ZL{q}", q)(weight_last)

    left = []

    @task("sent")
    def early_sends():
        for name in left:
            sites[name].wait_send()

    w_send(1, 0)
    w_send(3, 1)
    x_send(1, "s")
    x_send(3, "o")
    w_send(1, 1)
    w_send(3, 0)
    x_send(1, "o")
    x_send(3, "s")
    y_send(0, "yp", "s")
    y_send(0, "ym", "o")
    z_send(0, "zp", 0)
    z_send(0, "zm", 1)
    y_send(0, "yp", "o")
    y_send(0, "ym", "s")
    z_send(0, "zp", 1)
    z_send(0, "zm", 0)
    w_pair("ws0", 0, 0)
    send("xs", x_ref.at[half_of(other)], xb.at[chunk(0, c), place(0)], dc=1)
    for name in ORDER:
        if name == "PbA":
            left.extend(n for n in sites if n[:2] != "zv")
        tasks[name]()
    for name, copy in sites.items():
        if name not in left:
            copy.wait_send()
    arrived("t0", "t1", "t2")
    put_w.wait()
    put_x.wait()


def hand_on(a_ref, b_ref, a_out, b_out, a_buf, b_buf, sems):
    parts = [(b_ref.at[pl.ds(k * 96, 96)], b_buf.at[pl.ds(k * 96, 96)], b_out.at[pl.ds(k * 96, 96)]) for k in range(2)]
    parts.append((a_ref, a_buf, a_out))
    loads = [pltpu.make_async_copy(src, buf, sems.at[0, k]) for k, (src, buf, _) in enumerate(parts)]
    stores = [pltpu.make_async_copy(buf, dst, sems.at[1, k]) for k, (_, buf, dst) in enumerate(parts)]
    for copy in loads:
        copy.start()
    for load, store in zip(loads, stores):
        load.wait()
        store.start()
    for copy in stores:
        copy.wait()


def shards(activations, act_grad, up_weight, width_steps):
    any_space = pl.BlockSpec(memory_space=pl.ANY)

    def buffer(*shape):
        return pltpu.VMEM(shape, BF16)

    results = (
        jax.ShapeDtypeStruct((TOK, COLS), BF16),
        jax.ShapeDtypeStruct((ROWS, HID), BF16),
    )
    input_grad, weight_grad = pl.pallas_call(
        kernel,
        out_shape=results,
        in_specs=[any_space] * 4,
        out_specs=(any_space, any_space),
        scratch_shapes=[
            buffer(8, 4 * HALF, COLS),
            buffer(16 * ROWS, 2 * COLS),
            buffer(4 * HALF, 2 * COLS),
            buffer(TOK, HID),
            pltpu.VMEM((2, 128), jnp.int32),
            pltpu.VMEM((4 * HALF, 2 * COLS), F32),
            buffer(4 * HALF, 2 * COLS),
            buffer(2, 4, 2 * HALF, 2 * COLS),
            buffer(3, HALF, 2 * COLS),
            buffer(64, 2 * COLS),
            buffer(64, 2 * COLS),
            buffer(4, HALF, 2 * COLS),
            buffer(4, HALF, 2 * COLS),
            buffer(4, 2, HALF, COLS),
            buffer(3, 2, HALF, COLS),
            buffer(2, HALF, COLS),
            buffer(TOK, COLS),
            buffer(4, 2, 2, 384, COLS),
            buffer(4, 2, 384, COLS),
            buffer(4, 2, 384, COLS),
            buffer(384, COLS),
            buffer(384, COLS),
            buffer(2, 384, COLS),
            buffer(2, 384, COLS),
            buffer(4, ROWS, COLS),
            pltpu.SemaphoreType.DMA((N_SEM,)),
            pltpu.SemaphoreType.DMA((N_SEM,)),
            pltpu.SemaphoreType.DMA((4,)),
        ],
        compiler_params=pltpu.CompilerParams(
            collective_id=0, has_side_effects=True, vmem_limit_bytes=60 * 2**20
        ),
        cost_estimate=pl.CostEstimate(
            flops=3 * 2 * 512 * 3072 * 768, bytes_accessed=4 * 2**20, transcendentals=0
        ),
        name="elastic_up_backward",
    )(activations, act_grad, up_weight, width_steps.reshape(2, 128))
    return pl.pallas_call(
        hand_on,
        out_shape=results,
        in_specs=[any_space] * 2,
        out_specs=(any_space, any_space),
        scratch_shapes=[buffer(TOK, COLS), buffer(ROWS, HID), pltpu.SemaphoreType.DMA((2, 3))],
        compiler_params=pltpu.CompilerParams(vmem_limit_bytes=60 * 2**20),
        name="hand_on",
    )(input_grad, weight_grad)


def solution(mesh):
    placed = (P("dp", "tensor"), P("dp", "tensor"), P("dp", "tensor"), P("dp"))
    return jax.shard_map(
        shards,
        mesh=mesh,
        in_specs=placed,
        out_specs=(P("dp", "tensor"), P("dp", "tensor")),
        check_vma=False,
    )
```
